128 devices in a mesh: dp: 32 (over y, x, core), tensor: 4 (over z).
Axes of the slice: x: 4, y: 4, z: 4, core: 2. Of those that a mesh axis runs over, the one named last changes fastest.
Arguments:
- acts: bfloat16 [2, 16384, 5120], P(None, 'dp', 'tensor'), may hold values from -6 to 6
- cotangent: bfloat16 [2, 16384, 5120], P(None, 'dp'), may hold values from -6 to 6
- q_start: float32 [2, 5120, 32], replicated, may hold values from -0.078125 to 0.078125
Outputs:
- p_factor: float32 [2, 5120, 32], P(None, 'tensor')
- q_factor: float32 [2, 5120, 32], replicated
The draws below stay inside these ranges and needn't reach their ends.
All inputs are finite; a program needn't handle non-finite values.
Results may differ from the reference program's by a relative error of at most 0.0003.
Values sent between devices are 32-bit elements; how exact they have to be, the bound alone decides.
A program may use at most 192 MiB of HBM per device.

```python
import jax
import jax.numpy as jnp
from jax import lax

D = 5120
R = 32
LAYERS = 2
TOKENS = 16384
N_DP = 32


def level_of(rng, shape, shards, smallest, top_value):
    loudness = 1.0
    for position, parts in shards:
        heights = jax.random.uniform(jax.random.fold_in(jax.random.fold_in(rng, 6), position), (parts,), jnp.float32, smallest / len(shards), top_value / len(shards))
        loudness = loudness * jnp.repeat(jnp.exp(heights), shape[position] // parts).reshape((-1,) + (1,) * (len(shape) - 1 - position))
    return loudness


def bell_draw(stream_key, shape, spread, bound, shards=(), held_as=jnp.bfloat16):
    factor_of = level_of(stream_key, shape, shards, -0.22, 0.18) if shards else 1.0
    entries = jax.random.normal(stream_key, shape, jnp.float32) * spread * factor_of
    return jnp.minimum(jnp.maximum(entries, -bound), bound).astype(held_as)


def setup_inputs(seed: int = 0) -> dict:
    key_list = jax.random.split(jax.random.key(seed), 4)
    return {
        "acts": bell_draw(key_list[0], (LAYERS, TOKENS, D), 1.0, 6.0, ((1, 32), (2, 4))),
        "cotangent": bell_draw(key_list[1], (LAYERS, TOKENS, D), 1.0, 6.0, ((1, 32),)),
        "q_start": bell_draw(key_list[2], (LAYERS, D, R), D ** -0.5, 0.078125, (), jnp.float32),
    }


def reference(acts, cotangent, q_start):
    p_list = []
    q_list = []
    for layer in range(LAYERS):
        grad = jnp.dot(acts[layer].T.astype(jnp.float32), cotangent[layer].astype(jnp.float32), preferred_element_type=jnp.float32) / N_DP
        p_sum = jnp.dot(grad, q_start[layer], precision=lax.Precision.HIGHEST)
        gram = jnp.dot(p_sum.T, p_sum, precision=lax.Precision.HIGHEST)
        lower = jnp.linalg.cholesky(gram)
        p_hat = jax.scipy.linalg.solve_triangular(lower, p_sum.T, lower=True).T
        q_new = jnp.dot(grad.T, p_hat, precision=lax.Precision.HIGHEST)
        p_list.append(p_hat * jnp.sqrt(jnp.float32(D)))
        q_list.append(q_new)
    return (jnp.stack(p_list), jnp.stack(q_list))
```

```python
import functools

import jax
import jax.numpy as jnp
from jax import lax
from jax.experimental import pallas as pl
from jax.experimental.pallas import tpu as pltpu
from jax.sharding import PartitionSpec as P

MESH = pl.DeviceIdType.MESH
F32 = jnp.float32
BF16 = jnp.bfloat16
NN = (((1,), (0,)), ((), ()))
NT = (((1,), (1,)), ((), ()))
TILE = 128
FLY = 4


def dot(a, b, dims):
    return lax.dot_general(a, b, dims, preferred_element_type=F32)


def split3(x):
    hi = x.astype(BF16)
    rest = x - hi.astype(F32)
    mid = rest.astype(BF16)
    low = (rest - mid.astype(F32)).astype(BF16)
    return jnp.concatenate([hi, mid, low], axis=0)


def sum3(x):
    return x[0:32] + x[32:64] + x[64:96]


def to_pieces(ref, value):
    for j in range(16):
        g, h = j // 2, j % 2
        ref[j] = value[4 * g : 4 * g + 4, 640 * h : 640 * h + 640]


def from_pieces(ref):
    halves = []
    for h in range(2):
        halves.append(jnp.concatenate([ref[2 * g + h] for g in range(8)], axis=0))
    return jnp.concatenate(halves, axis=1)


def invert_factor(grams):
    rows = lax.broadcasted_iota(jnp.int32, (32, 128), 0)
    lanes = lax.broadcasted_iota(jnp.int32, (32, 128), 1)
    eye = jnp.where(rows == lanes % 32, 1.0, 0.0).astype(F32)
    work = jnp.where((lanes // 32) % 2 == 1, eye, grams)
    first = lanes < 64
    for k in range(32):
        row = work[k : k + 1, :]
        pivot = jnp.where(first[0:1], row[:, k : k + 1], row[:, 64 + k : 65 + k])
        scale = lax.rsqrt(pivot)
        scale = scale * (1.5 - 0.5 * pivot * scale * scale)
        column = jnp.where(first, work[:, k : k + 1], work[:, 64 + k : 65 + k])
        row = row * scale
        work = jnp.where(rows > k, work - (column * scale) * row, jnp.where(rows == k, row, work))
    return work


def exchange_kernel(
    a_hbm, c_hbm, q_hbm,
    zag, pag, inv_ref,
    a, c, q, q3t, wt, yt, px, pxr, ps, prr, zx, zxr, zs, zrr, gram,
    load_sem, core_sem, corer_sem, send_sem, prs_sem, pag_sem, pfw_sem, g_sem, zrs_sem, zag_sem, zfw_sem,
):
    dp = lax.axis_index("dp")
    z = lax.axis_index("tensor")
    core = lax.rem(dp, 2)
    plane = dp // 2
    y, x = plane // 4, lax.rem(plane, 4)
    mine, other = core, 1 - core
    sibling = {"dp": plane * 2 + other, "tensor": z}

    def peer(i):
        dz, dy, dx = i // 16, lax.rem(i // 4, 4), lax.rem(i, 4)
        to_plane = lax.rem(y + dy, 4) * 4 + lax.rem(x + dx, 4)
        to_z = lax.rem(z + dz, 4)
        return to_plane, to_z, {"dp": to_plane * 2 + core, "tensor": to_z}

    def source(i):
        dz, dy, dx = i // 16, lax.rem(i // 4, 4), lax.rem(i, 4)
        return lax.rem(y + 4 - dy, 4) * 4 + lax.rem(x + 4 - dx, 4), lax.rem(z + 4 - dz, 4)

    def remote(src, dst, send, recv, device):
        return pltpu.make_async_remote_copy(
            src_ref=src, dst_ref=dst, send_sem=send, recv_sem=recv, device_id=device, device_id_type=MESH
        )

    items = []
    for layer in (other, mine):
        items.append((q_hbm.at[layer], q.at[layer]))
    for layer in (other, mine):
        items.append((a_hbm.at[layer], a.at[layer]))
        for t in range(512 // TILE):
            items.append((c_hbm.at[layer, pl.ds(t * TILE, TILE)], c.at[layer, pl.ds(t * TILE, TILE)]))
    loads = [pltpu.make_async_copy(s, d, load_sem.at[i]) for i, (s, d) in enumerate(items)]
    for load in loads[:FLY]:
        load.start()

    barrier = pltpu.get_barrier_semaphore()

    def greet(i, carry):
        pl.semaphore_signal(barrier, inc=1, device_id=peer(i)[2], device_id_type=MESH)
        return carry

    pl.semaphore_signal(barrier, inc=1, device_id=sibling, device_id_type=MESH)
    lax.fori_loop(1, 64, greet, 0)

    def arrive(i):
        loads[i].wait()
        if i + FLY < len(loads):
            loads[i + FLY].start()

    for i, layer in enumerate((other, mine)):
        arrive(i)
        q3t[layer] = split3(q[layer]).T
    core_copies = []
    for n, layer in enumerate((other, mine)):
        base = 2 + n * (1 + 512 // TILE)
        arrive(base)
        for t in range(512 // TILE):
            arrive(base + 1 + t)
            w = dot(c[layer, t * TILE : (t + 1) * TILE, :], q3t[layer], NN)
            wt[:, t * TILE : (t + 1) * TILE] = sum3(w.T) * (1.0 / 32.0)
        part = sum3(dot(split3(wt[...]), a[layer], NN))
        if n == 0:
            to_pieces(px, part)
            pl.semaphore_wait(barrier, 64)
            core_copies.append(remote(px, pxr, core_sem.at[0], corer_sem.at[0], sibling))
            core_copies[0].start()
        else:
            to_pieces(ps, part)
    core_copies[0].wait_recv()
    ps[...] += pxr[...]

    sends = []
    for i in range(1, 16):
        to_plane, _, device = peer(i)
        cp = remote(ps.at[to_plane], prr.at[plane], send_sem.at[i], prs_sem.at[plane], device)
        cp.start()
        sends.append(cp)
    prr[plane] = ps[plane]
    for i in range(1, 16):
        from_plane, _ = source(i)
        remote(ps.at[0], prr.at[from_plane], send_sem.at[i], prs_sem.at[from_plane], sibling).wait_recv()
    pag[mine, plane] = jnp.sum(prr[...], axis=0)
    for cp in sends:
        cp.wait_send()

    sends = []
    for i in range(1, 16):
        _, _, device = peer(i)
        cp = remote(pag.at[mine, plane], pag.at[mine, plane], send_sem.at[i], pag_sem.at[plane], device)
        cp.start()
        sends.append(cp)
    cp = remote(pag.at[mine, plane], pag.at[mine, plane], send_sem.at[0], pfw_sem.at[plane], sibling)
    cp.start()
    sends.append(cp)
    forwards = []
    for i in range(1, 16):
        from_plane, _ = source(i)
        slot = pag.at[mine, from_plane]
        remote(slot, slot, send_sem.at[i], pag_sem.at[from_plane], sibling).wait_recv()
        cp = remote(slot, slot, send_sem.at[15 + i], pfw_sem.at[from_plane], sibling)
        cp.start()
        forwards.append(cp)

    def back(layer):
        p3 = split3(from_pieces(pag.at[layer]))
        yt[layer] = sum3(dot(p3, a[layer], NT)) * (1.0 / 32.0)
        g9 = dot(p3, p3, NT)
        g3 = sum3(g9)
        return g3[:, 0:32] + g3[:, 32:64] + g3[:, 64:96]

    g_mine = back(mine)
    for i in range(16):
        from_plane, _ = source(i)
        slot = pag.at[other, from_plane]
        remote(slot, slot, send_sem.at[i], pfw_sem.at[from_plane], sibling).wait_recv()
    g_other = back(other)
    for cp in sends + forwards:
        cp.wait_send()

    def z_part(layer, ref):
        y3 = split3(yt[layer])
        for b in range(4):
            to_pieces(ref.at[b], sum3(dot(y3, c[layer, :, b * 1280 : (b + 1) * 1280], NN)))

    z_part(other, zx)
    z_copy = remote(zx, zxr, core_sem.at[1], corer_sem.at[1], sibling)
    z_copy.start()
    zero = jnp.zeros((32, 32), F32)
    g_first = jnp.where(core == 0, g_mine, g_other)
    g_second = jnp.where(core == 0, g_other, g_mine)
    gram[z] = jnp.concatenate([g_first, zero, g_second, zero], axis=1)
    g_copies = []
    for dz in range(1, 4):
        device = {"dp": dp, "tensor": lax.rem(z + dz, 4)}
        cp = remote(gram.at[z], gram.at[z], send_sem.at[dz], g_sem.at[z], device)
        cp.start()
        g_copies.append(cp)
    z_part(mine, zs)
    z_copy.wait_recv()
    zs[...] += zxr[...]

    def scatter(i, carry):
        to_plane, to_z, device = peer(i)
        me = z * 16 + plane
        remote(zs.at[to_z, to_plane], zrr.at[me], send_sem.at[32 + i], zrs_sem.at[me], device).start()
        return carry

    lax.fori_loop(1, 64, scatter, 0)
    me = z * 16 + plane
    zrr[me] = zs[z, plane]
    for dz in range(1, 4):
        from_z = lax.rem(z + 4 - dz, 4)
        remote(gram.at[from_z], gram.at[from_z], send_sem.at[0], g_sem.at[from_z], sibling).wait_recv()
    inv_ref[...] = invert_factor(gram[0] + gram[1] + gram[2] + gram[3])

    def scattered(i, carry):
        from_plane, from_z = source(i)
        slot = from_z * 16 + from_plane
        remote(zrr.at[slot], zrr.at[slot], send_sem.at[0], zrs_sem.at[slot], sibling).wait_recv()
        return carry

    lax.fori_loop(1, 64, scattered, 0)
    zag[mine, me] = jnp.sum(zrr[...], axis=0)

    def scatter_done(i, carry):
        remote(zs.at[0, 0], zrr.at[0], send_sem.at[32 + i], zrs_sem.at[0], sibling).wait_send()
        return carry

    lax.fori_loop(1, 64, scatter_done, 0)

    own = zag.at[mine, me]

    def gather(i, carry):
        remote(own, own, send_sem.at[32 + i], zag_sem.at[me], peer(i)[2]).start()
        return carry

    lax.fori_loop(1, 64, gather, 0)
    remote(own, own, send_sem.at[32], zfw_sem.at[me], sibling).start()

    def forward(i, carry):
        from_plane, from_z = source(i)
        place = from_z * 16 + from_plane
        slot = zag.at[mine, place]
        remote(slot, slot, send_sem.at[0], zag_sem.at[place], sibling).wait_recv()
        remote(slot, slot, send_sem.at[96 + i], zfw_sem.at[place], sibling).start()
        return carry

    lax.fori_loop(1, 64, forward, 0)

    def forwarded(i, carry):
        from_plane, from_z = source(i)
        place = from_z * 16 + from_plane
        slot = zag.at[other, place]
        remote(slot, slot, send_sem.at[0], zfw_sem.at[place], sibling).wait_recv()
        return carry

    lax.fori_loop(0, 64, forwarded, 0)

    def sent(i, carry):
        remote(own, own, send_sem.at[32 + i], zag_sem.at[me], sibling).wait_send()
        return carry

    lax.fori_loop(0, 64, sent, 0)

    def forward_sent(i, carry):
        remote(own, own, send_sem.at[96 + i], zag_sem.at[me], sibling).wait_send()
        return carry

    lax.fori_loop(1, 64, forward_sent, 0)
    core_copies[0].wait_send()
    z_copy.wait_send()
    for cp in g_copies:
        cp.wait_send()


def finish_kernel(zag, pag, inv_ref, p_out, q_out, *, root):
    for layer in range(2):
        inverse = inv_ref[:, 64 * layer + 32 : 64 * layer + 64]
        pieces = split3(inverse)
        left = jnp.concatenate([pieces, pieces, pieces], axis=1)
        p_out[layer] = sum3(dot(left, split3(from_pieces(pag.at[layer])), NN)) * root
        for b in range(4):
            block = from_pieces(zag.at[layer, 16 * b : 16 * b + 16])
            q_out[layer, :, b * 1280 : (b + 1) * 1280] = sum3(dot(left, split3(block), NN))


def local(acts, cotangent, q_start):
    width = cotangent.shape[2]
    q_t = jnp.swapaxes(q_start, 1, 2)
    hbm = pl.BlockSpec(memory_space=pl.ANY)
    vmem = pl.BlockSpec(memory_space=pltpu.VMEM)
    dma = pltpu.SemaphoreType.DMA
    zag, pag, inverse = pl.pallas_call(
        exchange_kernel,
        out_shape=(
            jax.ShapeDtypeStruct((2, 64, 4, 640), F32),
            jax.ShapeDtypeStruct((2, 16, 4, 640), F32),
            jax.ShapeDtypeStruct((32, 128), F32),
        ),
        in_specs=[hbm] * 3,
        out_specs=(vmem, vmem, vmem),
        scratch_shapes=[
            pltpu.VMEM((2, 512, 1280), BF16),
            pltpu.VMEM((2, 512, 5120), BF16),
            pltpu.VMEM((2, 32, 5120), F32),
            pltpu.VMEM((2, 5120, 96), BF16),
            pltpu.VMEM((32, 512), F32),
            pltpu.VMEM((2, 32, 512), F32),
            pltpu.VMEM((16, 4, 640), F32),
            pltpu.VMEM((16, 4, 640), F32),
            pltpu.VMEM((16, 4, 640), F32),
            pltpu.VMEM((16, 4, 640), F32),
            pltpu.VMEM((4, 16, 4, 640), F32),
            pltpu.VMEM((4, 16, 4, 640), F32),
            pltpu.VMEM((4, 16, 4, 640), F32),
            pltpu.VMEM((64, 4, 640), F32),
            pltpu.VMEM((4, 32, 128), F32),
            dma((16,)), dma((2,)), dma((2,)), dma((160,)), dma((16,)), dma((16,)), dma((16,)),
            dma((4,)), dma((64,)), dma((64,)), dma((64,)),
        ],
        name="exchange",
        compiler_params=pltpu.CompilerParams(
            collective_id=0, has_side_effects=True, vmem_limit_bytes=50 * 2**20
        ),
    )(acts, cotangent, q_t)
    p_t, q_new = pl.pallas_call(
        functools.partial(finish_kernel, root=float(width) ** 0.5),
        out_shape=(
            jax.ShapeDtypeStruct((2, 32, 1280), F32),
            jax.ShapeDtypeStruct((2, 32, 5120), F32),
        ),
        in_specs=[vmem] * 3,
        out_specs=(vmem, vmem),
        name="finish",
        compiler_params=pltpu.CompilerParams(vmem_limit_bytes=32 * 2**20),
    )(zag, pag, inverse)
    return jnp.swapaxes(p_t, 1, 2), jnp.swapaxes(q_new, 1, 2)


def solution(mesh):
    placed = (P(None, "dp", "tensor"), P(None, "dp", None), P())
    return jax.shard_map(
        local, mesh=mesh, in_specs=placed, out_specs=(P(None, "tensor", None), P()), check_vma=False
    )
```

```python
import functools

import jax
import jax.numpy as jnp
from jax import lax
from jax.experimental import pallas as pl
from jax.experimental.pallas import tpu as pltpu
from jax.sharding import PartitionSpec as P

MESH = pl.DeviceIdType.MESH
F32 = jnp.float32
BF16 = jnp.bfloat16
NN = (((1,), (0,)), ((), ()))
NT = (((1,), (1,)), ((), ()))
TILE = 128


def hops(offset):
    return sum(min(d, 4 - d) for d in offset)


OFFSETS = [(dz, dy, dx) for dz in range(4) for dy in range(4) for dx in range(4)]
CUBE = sorted([o for o in OFFSETS if hops(o) > 0], key=hops, reverse=True)
PLANE = [o for o in CUBE if o[0] == 0]
AXIS = [o for o in CUBE if o[1] == 0 and o[2] == 0]
FLY = 4


def dot(a, b, dims):
    return lax.dot_general(a, b, dims, preferred_element_type=F32)


def split3(x):
    hi = x.astype(BF16)
    rest = x - hi.astype(F32)
    mid = rest.astype(BF16)
    low = (rest - mid.astype(F32)).astype(BF16)
    return jnp.concatenate([hi, mid, low], axis=0)


def sum3(x):
    return x[0:32] + x[32:64] + x[64:96]


def to_pieces(ref, value):
    for j in range(16):
        g, h = j // 2, j % 2
        ref[j] = value[4 * g : 4 * g + 4, 640 * h : 640 * h + 640]


def from_pieces(ref):
    halves = []
    for h in range(2):
        halves.append(jnp.concatenate([ref[2 * g + h] for g in range(8)], axis=0))
    return jnp.concatenate(halves, axis=1)


def invert_factor(grams):
    rows = lax.broadcasted_iota(jnp.int32, (32, 128), 0)
    lanes = lax.broadcasted_iota(jnp.int32, (32, 128), 1)
    eye = jnp.where(rows == lanes % 32, 1.0, 0.0).astype(F32)
    work = jnp.where((lanes // 32) % 2 == 1, eye, grams)
    first = lanes < 64
    for k in range(32):
        row = work[k : k + 1, :]
        pivot = jnp.where(first[0:1], row[:, k : k + 1], row[:, 64 + k : 65 + k])
        scale = lax.rsqrt(pivot)
        scale = scale * (1.5 - 0.5 * pivot * scale * scale)
        column = jnp.where(first, work[:, k : k + 1], work[:, 64 + k : 65 + k])
        row = row * scale
        work = jnp.where(rows > k, work - (column * scale) * row, jnp.where(rows == k, row, work))
    return work


def exchange_kernel(
    a_hbm, c_hbm, q_hbm,
    zag, pag, inv_ref,
    a, c, q, q3t, wt, yt, px, pxr, ps, prr, zx, zxr, zs, zrr, gram,
    load_sem, core_sem, corer_sem, send_sem, prs_sem, pag_sem, pfw_sem, g_sem, zrs_sem, zag_sem, zfw_sem,
):
    dp = lax.axis_index("dp")
    z = lax.axis_index("tensor")
    core = lax.rem(dp, 2)
    plane = dp // 2
    y, x = plane // 4, lax.rem(plane, 4)
    mine, other = core, 1 - core
    sibling = {"dp": plane * 2 + other, "tensor": z}

    ys = [lax.rem(y + d, 4) for d in range(4)]
    xs = [lax.rem(x + d, 4) for d in range(4)]
    zs_at = [lax.rem(z + d, 4) for d in range(4)]

    def place(dz, dy, dx):
        return ys[dy] * 4 + xs[dx], zs_at[dz]

    def device(dz, dy, dx):
        to_plane, to_z = place(dz, dy, dx)
        return {"dp": to_plane * 2 + core, "tensor": to_z}

    def back_from(dz, dy, dx):
        return place((4 - dz) % 4, (4 - dy) % 4, (4 - dx) % 4)

    def remote(src, dst, send, recv, device):
        return pltpu.make_async_remote_copy(
            src_ref=src, dst_ref=dst, send_sem=send, recv_sem=recv, device_id=device, device_id_type=MESH
        )

    pending = []

    def drain():
        for done in pending:
            done()

    items = []
    for layer in (other, mine):
        items.append((q_hbm.at[layer], q.at[layer]))
    for layer in (other, mine):
        items.append((a_hbm.at[layer], a.at[layer]))
        for t in range(512 // TILE):
            items.append((c_hbm.at[layer, pl.ds(t * TILE, TILE)], c.at[layer, pl.ds(t * TILE, TILE)]))
    loads = [pltpu.make_async_copy(s, d, load_sem.at[i]) for i, (s, d) in enumerate(items)]
    for load in loads[:FLY]:
        load.start()

    barrier = pltpu.get_barrier_semaphore()

    pl.semaphore_signal(barrier, inc=1, device_id=sibling, device_id_type=MESH)
    for offset in PLANE + AXIS:
        pl.semaphore_signal(barrier, inc=1, device_id=device(*offset), device_id_type=MESH)

    def arrive(i):
        loads[i].wait()
        if i + FLY < len(loads):
            loads[i + FLY].start()

    for i, layer in enumerate((other, mine)):
        arrive(i)
        q3t[layer] = split3(q[layer]).T
    for n, layer in enumerate((other, mine)):
        base = 2 + n * (1 + 512 // TILE)
        arrive(base)
        for t in range(512 // TILE):
            arrive(base + 1 + t)
            w = dot(c[layer, t * TILE : (t + 1) * TILE, :], q3t[layer], NN)
            wt[:, t * TILE : (t + 1) * TILE] = sum3(w.T) * (1.0 / 32.0)
        part = sum3(dot(split3(wt[...]), a[layer], NN))
        if n == 0:
            to_pieces(px, part)
            pl.semaphore_wait(barrier, 1 + len(PLANE) + len(AXIS))
            p_copy = remote(px, pxr, core_sem.at[0], corer_sem.at[0], sibling)
            p_copy.start()
            pending.append(p_copy.wait_send)
        else:
            to_pieces(ps, part)
    p_copy.wait_recv()
    ps[...] += pxr[...]

    for offset in PLANE:
        to_plane, _ = place(*offset)
        remote(ps.at[to_plane], prr.at[plane], send_sem.at[0], prs_sem.at[0], device(*offset)).start()
    pending.append(remote(ps.at[pl.ds(0, 15)], prr.at[pl.ds(0, 15)], send_sem.at[0], prs_sem.at[0], sibling).wait_send)
    prr[plane] = ps[plane]
    remote(ps.at[pl.ds(0, 15)], prr.at[pl.ds(0, 15)], send_sem.at[0], prs_sem.at[0], sibling).wait_recv()
    pag[mine, plane] = jnp.sum(prr[...], axis=0)

    own = pag.at[mine, plane]
    many = pag.at[mine, pl.ds(0, 15)]
    for offset in PLANE:
        remote(own, own, send_sem.at[1], pag_sem.at[plane], device(*offset)).start()
    pending.append(remote(many, many, send_sem.at[1], pag_sem.at[0], sibling).wait_send)
    remote(own, own, send_sem.at[2], pfw_sem.at[0], sibling).start()
    for offset in reversed(PLANE):
        from_plane, _ = back_from(*offset)
        slot = pag.at[mine, from_plane]
        remote(slot, slot, send_sem.at[0], pag_sem.at[from_plane], sibling).wait_recv()
        remote(slot, slot, send_sem.at[2], pfw_sem.at[0], sibling).start()
    pending.append(remote(pag.at[mine], pag.at[mine], send_sem.at[2], pfw_sem.at[0], sibling).wait_send)

    def back(layer):
        p3 = split3(from_pieces(pag.at[layer]))
        yt[layer] = sum3(dot(p3, a[layer], NT)) * (1.0 / 32.0)
        g9 = dot(p3, p3, NT)
        g3 = sum3(g9)
        return g3[:, 0:32] + g3[:, 32:64] + g3[:, 64:96]

    g_mine = back(mine)
    remote(pag.at[other], pag.at[other], send_sem.at[2], pfw_sem.at[0], sibling).wait_recv()
    g_other = back(other)

    def z_part(y3, layer, b, ref):
        to_pieces(ref.at[b], sum3(dot(y3, c[layer, :, b * 1280 : (b + 1) * 1280], NN)))

    y3 = split3(yt[other])
    z_copies = []
    for b in range(4):
        z_part(y3, other, b, zx)
        cp = remote(zx.at[b], zxr.at[b], core_sem.at[1 + b], corer_sem.at[1 + b], sibling)
        cp.start()
        z_copies.append(cp)
        pending.append(cp.wait_send)
    zero = jnp.zeros((32, 32), F32)
    g_first = jnp.where(core == 0, g_mine, g_other)
    g_second = jnp.where(core == 0, g_other, g_mine)
    gram[z] = jnp.concatenate([g_first, zero, g_second, zero], axis=1)
    for offset in AXIS:
        remote(gram.at[z], gram.at[z], send_sem.at[3], g_sem.at[z], device(*offset)).start()
    pending.append(remote(gram.at[pl.ds(0, 3)], gram.at[pl.ds(0, 3)], send_sem.at[3], g_sem.at[0], sibling).wait_send)
    y3 = split3(yt[mine])
    for b in range(4):
        z_part(y3, mine, b, zs)
    for offset in AXIS:
        _, from_z = back_from(*offset)
        remote(gram.at[from_z], gram.at[from_z], send_sem.at[3], g_sem.at[from_z], sibling).wait_recv()
    for b in range(4):
        z_copies[b].wait_recv()
        zs[b] += zxr[b]

    me = z * 16 + plane
    for offset in CUBE:
        to_plane, to_z = place(*offset)
        remote(zs.at[to_z, to_plane], zrr.at[me], send_sem.at[4], zrs_sem.at[0], device(*offset)).start()
    most = zrr.at[pl.ds(0, 63)]
    pending.append(remote(most, most, send_sem.at[4], zrs_sem.at[0], sibling).wait_send)
    zrr[me] = zs[z, plane]
    inv_ref[...] = invert_factor(gram[0] + gram[1] + gram[2] + gram[3])
    remote(most, most, send_sem.at[4], zrs_sem.at[0], sibling).wait_recv()
    zag[mine, me] = jnp.sum(zrr[...], axis=0)

    own = zag.at[mine, me]
    for offset in CUBE:
        remote(own, own, send_sem.at[5], zag_sem.at[z], device(*offset)).start()
    for dz in (0, 1, 3, 2):
        _, from_z = back_from(dz, 0, 0)
        count = 15 if dz == 0 else 16
        block = zag.at[mine, pl.ds(from_z * 16, count)]
        remote(block, block, send_sem.at[6], zag_sem.at[from_z], sibling).wait_recv()
        block = zag.at[mine, pl.ds(from_z * 16, 16)]
        remote(block, block, send_sem.at[6], zfw_sem.at[0], sibling).start()
    remote(zag.at[other], zag.at[other], send_sem.at[6], zfw_sem.at[0], sibling).wait_recv()
    remote(zag.at[mine], zag.at[mine], send_sem.at[6], zfw_sem.at[0], sibling).wait_send()
    most = zag.at[mine, pl.ds(0, 63)]
    remote(most, most, send_sem.at[5], zag_sem.at[0], sibling).wait_send()
    drain()


def finish_kernel(zag, pag, inv_ref, p_out, q_out, *, root):
    for layer in range(2):
        inverse = inv_ref[:, 64 * layer + 32 : 64 * layer + 64]
        pieces = split3(inverse)
        left = jnp.concatenate([pieces, pieces, pieces], axis=1)
        p_out[layer] = sum3(dot(left, split3(from_pieces(pag.at[layer])), NN)) * root
        for b in range(4):
            block = from_pieces(zag.at[layer, 16 * b : 16 * b + 16])
            q_out[layer, :, b * 1280 : (b + 1) * 1280] = sum3(dot(left, split3(block), NN))


def local(acts, cotangent, q_start):
    width = cotangent.shape[2]
    q_t = jnp.swapaxes(q_start, 1, 2)
    hbm = pl.BlockSpec(memory_space=pltpu.HBM)
    vmem = pl.BlockSpec(memory_space=pltpu.VMEM)
    dma = pltpu.SemaphoreType.DMA
    zag, pag, inverse = pl.pallas_call(
        exchange_kernel,
        out_shape=(
            jax.ShapeDtypeStruct((2, 64, 4, 640), F32),
            jax.ShapeDtypeStruct((2, 16, 4, 640), F32),
            jax.ShapeDtypeStruct((32, 128), F32),
        ),
        in_specs=[hbm] * 3,
        out_specs=(vmem, vmem, vmem),
        scratch_shapes=[
            pltpu.VMEM((2, 512, 1280), BF16),
            pltpu.VMEM((2, 512, 5120), BF16),
            pltpu.VMEM((2, 32, 5120), F32),
            pltpu.VMEM((2, 5120, 96), BF16),
            pltpu.VMEM((32, 512), F32),
            pltpu.VMEM((2, 32, 512), F32),
            pltpu.VMEM((16, 4, 640), F32),
            pltpu.VMEM((16, 4, 640), F32),
            pltpu.VMEM((16, 4, 640), F32),
            pltpu.VMEM((16, 4, 640), F32),
            pltpu.VMEM((4, 16, 4, 640), F32),
            pltpu.VMEM((4, 16, 4, 640), F32),
            pltpu.VMEM((4, 16, 4, 640), F32),
            pltpu.VMEM((64, 4, 640), F32),
            pltpu.VMEM((4, 32, 128), F32),
            dma((16,)), dma((5,)), dma((5,)), dma((7,)), dma((1,)), dma((16,)), dma((1,)),
            dma((4,)), dma((1,)), dma((4,)), dma((1,)),
        ],
        name="exchange",
        compiler_params=pltpu.CompilerParams(
            collective_id=0, has_side_effects=True, vmem_limit_bytes=50 * 2**20
        ),
    )(acts, cotangent, q_t)
    p_t, q_new = pl.pallas_call(
        functools.partial(finish_kernel, root=float(width) ** 0.5),
        out_shape=(
            jax.ShapeDtypeStruct((2, 32, 1280), F32),
            jax.ShapeDtypeStruct((2, 32, 5120), F32),
        ),
        in_specs=[vmem] * 3,
        out_specs=(vmem, vmem),
        name="finish",
        compiler_params=pltpu.CompilerParams(vmem_limit_bytes=32 * 2**20),
    )(zag, pag, inverse)
    return jnp.swapaxes(p_t, 1, 2), jnp.swapaxes(q_new, 1, 2)


def solution(mesh):
    placed = (P(None, "dp", "tensor"), P(None, "dp", None), P())
    return jax.shard_map(
        local, mesh=mesh, in_specs=placed, out_specs=(P(None, "tensor", None), P()), check_vma=False
    )
```

```python
import functools

import jax
import jax.numpy as jnp
from jax import lax
from jax.experimental import pallas as pl
from jax.experimental.pallas import tpu as pltpu
from jax.sharding import PartitionSpec as P

MESH = pl.DeviceIdType.MESH
F32 = jnp.float32
BF16 = jnp.bfloat16
NN = (((1,), (0,)), ((), ()))
NT = (((1,), (1,)), ((), ()))
TILE = 256


def hops(offset):
    return sum(min(d, 4 - d) for d in offset)


OFFSETS = [(dz, dy, dx) for dz in range(4) for dy in range(4) for dx in range(4)]
CUBE = sorted([o for o in OFFSETS if hops(o) > 0], key=hops, reverse=True)
PLANE = [o for o in CUBE if o[0] == 0]
AXIS = [o for o in CUBE if o[1] == 0 and o[2] == 0]
FLY = 5


def dot(a, b, dims):
    return lax.dot_general(a, b, dims, preferred_element_type=F32)


def split3(x):
    hi = x.astype(BF16)
    rest = x - hi.astype(F32)
    mid = rest.astype(BF16)
    low = (rest - mid.astype(F32)).astype(BF16)
    return jnp.concatenate([hi, mid, low], axis=0)


def sum3(x):
    return x[0:32] + x[32:64] + x[64:96]


def to_pieces(ref, value):
    for j in range(16):
        g, h = j // 2, j % 2
        ref[j] = value[4 * g : 4 * g + 4, 640 * h : 640 * h + 640]


def from_pieces(ref):
    halves = []
    for h in range(2):
        halves.append(jnp.concatenate([ref[2 * g + h] for g in range(8)], axis=0))
    return jnp.concatenate(halves, axis=1)


def invert_factor(grams):
    rows = lax.broadcasted_iota(jnp.int32, (32, 128), 0)
    lanes = lax.broadcasted_iota(jnp.int32, (32, 128), 1)
    eye = jnp.where(rows == lanes % 32, 1.0, 0.0).astype(F32)
    work = jnp.where((lanes // 32) % 2 == 1, eye, grams)
    first = lanes < 64
    for k in range(32):
        row = work[k : k + 1, :]
        pivot = jnp.where(first[0:1], row[:, k : k + 1], row[:, 64 + k : 65 + k])
        scale = lax.rsqrt(pivot)
        scale = scale * (1.5 - 0.5 * pivot * scale * scale)
        column = jnp.where(first, work[:, k : k + 1], work[:, 64 + k : 65 + k])
        row = row * scale
        work = jnp.where(rows > k, work - (column * scale) * row, jnp.where(rows == k, row, work))
    return work


def exchange_kernel(
    a_hbm, c_hbm, q_hbm,
    zag, pag, inv_ref,
    a, c, q, q3t, wt, yt, px, pxr, ps, prr, zx, zxr, zs, zrr, gram,
    load_sem, core_sem, corer_sem, send_sem, prs_sem, pag_sem, pfw_sem, g_sem, zrs_sem, zag_sem, zfw_sem, near_sem,
):
    dp = lax.axis_index("dp")
    z = lax.axis_index("tensor")
    core = lax.rem(dp, 2)
    plane = dp // 2
    y, x = plane // 4, lax.rem(plane, 4)
    mine, other = core, 1 - core
    sibling = {"dp": plane * 2 + other, "tensor": z}

    ys = [lax.rem(y + d, 4) for d in range(4)]
    xs = [lax.rem(x + d, 4) for d in range(4)]
    zs_at = [lax.rem(z + d, 4) for d in range(4)]

    def place(dz, dy, dx):
        return ys[dy] * 4 + xs[dx], zs_at[dz]

    def device(dz, dy, dx):
        to_plane, to_z = place(dz, dy, dx)
        return {"dp": to_plane * 2 + core, "tensor": to_z}

    def back_from(dz, dy, dx):
        return place((4 - dz) % 4, (4 - dy) % 4, (4 - dx) % 4)

    def remote(src, dst, send, recv, device):
        return pltpu.make_async_remote_copy(
            src_ref=src, dst_ref=dst, send_sem=send, recv_sem=recv, device_id=device, device_id_type=MESH
        )

    pending = []

    def drain():
        for done in pending:
            done()

    items = []
    for layer in (other, mine):
        items.append((q_hbm.at[layer], q.at[layer]))
    for layer in (other, mine):
        items.append((a_hbm.at[layer], a.at[layer]))
        for t in range(512 // TILE):
            items.append((c_hbm.at[layer, pl.ds(t * TILE, TILE)], c.at[layer, pl.ds(t * TILE, TILE)]))
    loads = [pltpu.make_async_copy(s, d, load_sem.at[i]) for i, (s, d) in enumerate(items)]
    for load in loads[:FLY]:
        load.start()

    barrier = pltpu.get_barrier_semaphore()

    pl.semaphore_signal(barrier, inc=1, device_id=sibling, device_id_type=MESH)
    for offset in PLANE + AXIS:
        pl.semaphore_signal(barrier, inc=1, device_id=device(*offset), device_id_type=MESH)

    def arrive(i):
        loads[i].wait()
        if i + FLY < len(loads):
            loads[i + FLY].start()

    for i, layer in enumerate((other, mine)):
        arrive(i)
        q3t[layer] = split3(q[layer]).T
    for n, layer in enumerate((other, mine)):
        base = 2 + n * (1 + 512 // TILE)
        arrive(base)
        for t in range(512 // TILE):
            arrive(base + 1 + t)
            w = dot(c[layer, t * TILE : (t + 1) * TILE, :], q3t[layer], NN)
            wt[:, t * TILE : (t + 1) * TILE] = sum3(w.T) * (1.0 / 32.0)
        part = sum3(dot(split3(wt[...]), a[layer], NN))
        if n == 0:
            to_pieces(px, part)
            pl.semaphore_wait(barrier, 1 + len(PLANE) + len(AXIS))
            p_copy = remote(px, pxr, core_sem.at[0], corer_sem.at[0], sibling)
            p_copy.start()
            pending.append(p_copy.wait_send)
        else:
            to_pieces(ps, part)
    p_copy.wait_recv()
    ps[...] += pxr[...]

    for offset in PLANE:
        to_plane, _ = place(*offset)
        remote(ps.at[to_plane], prr.at[plane], send_sem.at[0], prs_sem.at[0], device(*offset)).start()
    pending.append(remote(ps.at[pl.ds(0, 15)], prr.at[pl.ds(0, 15)], send_sem.at[0], prs_sem.at[0], sibling).wait_send)
    prr[plane] = ps[plane]
    remote(ps.at[pl.ds(0, 15)], prr.at[pl.ds(0, 15)], send_sem.at[0], prs_sem.at[0], sibling).wait_recv()
    for offset in AXIS:
        pl.semaphore_signal(near_sem, inc=1, device_id=device(*offset), device_id_type=MESH)
    pag[mine, plane] = jnp.sum(prr[...], axis=0)

    own = pag.at[mine, plane]
    many = pag.at[mine, pl.ds(0, 15)]
    for offset in PLANE:
        remote(own, own, send_sem.at[1], pag_sem.at[plane], device(*offset)).start()
    pending.append(remote(many, many, send_sem.at[1], pag_sem.at[0], sibling).wait_send)
    remote(own, own, send_sem.at[2], pfw_sem.at[0], sibling).start()
    for offset in reversed(PLANE):
        from_plane, _ = back_from(*offset)
        slot = pag.at[mine, from_plane]
        remote(slot, slot, send_sem.at[0], pag_sem.at[from_plane], sibling).wait_recv()
        remote(slot, slot, send_sem.at[2], pfw_sem.at[0], sibling).start()
    pending.append(remote(pag.at[mine], pag.at[mine], send_sem.at[2], pfw_sem.at[0], sibling).wait_send)

    def back(layer):
        p3 = split3(from_pieces(pag.at[layer]))
        yt[layer] = sum3(dot(p3, a[layer], NT)) * (1.0 / 32.0)
        g9 = dot(p3, p3, NT)
        g3 = sum3(g9)
        return g3[:, 0:32] + g3[:, 32:64] + g3[:, 64:96]

    g_mine = back(mine)
    remote(pag.at[other], pag.at[other], send_sem.at[2], pfw_sem.at[0], sibling).wait_recv()
    g_other = back(other)

    def z_part(y3, layer, b, ref):
        to_pieces(ref.at[b], sum3(dot(y3, c[layer, :, b * 1280 : (b + 1) * 1280], NN)))

    y3 = split3(yt[other])
    z_copies = []
    for b in range(4):
        z_part(y3, other, b, zx)
        cp = remote(zx.at[b], zxr.at[b], core_sem.at[1 + b], corer_sem.at[1 + b], sibling)
        cp.start()
        z_copies.append(cp)
        pending.append(cp.wait_send)
    zero = jnp.zeros((32, 32), F32)
    g_first = jnp.where(core == 0, g_mine, g_other)
    g_second = jnp.where(core == 0, g_other, g_mine)
    gram[z] = jnp.concatenate([g_first, zero, g_second, zero], axis=1)
    for offset in AXIS:
        remote(gram.at[z], gram.at[z], send_sem.at[3], g_sem.at[z], device(*offset)).start()
    pending.append(remote(gram.at[pl.ds(0, 3)], gram.at[pl.ds(0, 3)], send_sem.at[3], g_sem.at[0], sibling).wait_send)
    y3 = split3(yt[mine])
    for b in range(4):
        z_part(y3, mine, b, zs)
    for b in range(4):
        z_copies[b].wait_recv()
        zs[b] += zxr[b]

    me = z * 16 + plane
    pl.semaphore_wait(near_sem, len(AXIS))
    for offset in CUBE:
        to_plane, to_z = place(*offset)
        remote(zs.at[to_z, to_plane], zrr.at[me], send_sem.at[4], zrs_sem.at[0], device(*offset)).start()
    most = zrr.at[pl.ds(0, 63)]
    pending.append(remote(most, most, send_sem.at[4], zrs_sem.at[0], sibling).wait_send)
    zrr[me] = zs[z, plane]
    for offset in AXIS:
        _, from_z = back_from(*offset)
        remote(gram.at[from_z], gram.at[from_z], send_sem.at[3], g_sem.at[from_z], sibling).wait_recv()
    inv_ref[...] = invert_factor(gram[0] + gram[1] + gram[2] + gram[3])
    remote(most, most, send_sem.at[4], zrs_sem.at[0], sibling).wait_recv()
    zag[mine, me] = jnp.sum(zrr[...], axis=0)

    own = zag.at[mine, me]
    for offset in CUBE:
        remote(own, own, send_sem.at[5], zag_sem.at[z], device(*offset)).start()
    for dz in (0, 1, 3, 2):
        _, from_z = back_from(dz, 0, 0)
        count = 15 if dz == 0 else 16
        block = zag.at[mine, pl.ds(from_z * 16, count)]
        remote(block, block, send_sem.at[6], zag_sem.at[from_z], sibling).wait_recv()
        block = zag.at[mine, pl.ds(from_z * 16, 16)]
        remote(block, block, send_sem.at[6], zfw_sem.at[0], sibling).start()
    remote(zag.at[other], zag.at[other], send_sem.at[6], zfw_sem.at[0], sibling).wait_recv()
    remote(zag.at[mine], zag.at[mine], send_sem.at[6], zfw_sem.at[0], sibling).wait_send()
    most = zag.at[mine, pl.ds(0, 63)]
    remote(most, most, send_sem.at[5], zag_sem.at[0], sibling).wait_send()
    drain()


def finish_kernel(zag, pag, inv_ref, p_out, q_out, *, root):
    for layer in range(2):
        inverse = inv_ref[:, 64 * layer + 32 : 64 * layer + 64]
        pieces = split3(inverse)
        left = jnp.concatenate([pieces, pieces, pieces], axis=1)
        p_out[layer] = sum3(dot(left, split3(from_pieces(pag.at[layer])), NN)) * root
        for b in range(4):
            block = from_pieces(zag.at[layer, 16 * b : 16 * b + 16])
            q_out[layer, :, b * 1280 : (b + 1) * 1280] = sum3(dot(left, split3(block), NN))


def local(acts, cotangent, q_start):
    width = cotangent.shape[2]
    q_t = jnp.swapaxes(q_start, 1, 2)
    hbm = pl.BlockSpec(memory_space=pltpu.HBM)
    vmem = pl.BlockSpec(memory_space=pltpu.VMEM)
    dma = pltpu.SemaphoreType.DMA
    zag, pag, inverse = pl.pallas_call(
        exchange_kernel,
        out_shape=(
            jax.ShapeDtypeStruct((2, 64, 4, 640), F32),
            jax.ShapeDtypeStruct((2, 16, 4, 640), F32),
            jax.ShapeDtypeStruct((32, 128), F32),
        ),
        in_specs=[hbm] * 3,
        out_specs=(vmem, vmem, vmem),
        scratch_shapes=[
            pltpu.VMEM((2, 512, 1280), BF16),
            pltpu.VMEM((2, 512, 5120), BF16),
            pltpu.VMEM((2, 32, 5120), F32),
            pltpu.VMEM((2, 5120, 96), BF16),
            pltpu.VMEM((32, 512), F32),
            pltpu.VMEM((2, 32, 512), F32),
            pltpu.VMEM((16, 4, 640), F32),
            pltpu.VMEM((16, 4, 640), F32),
            pltpu.VMEM((16, 4, 640), F32),
            pltpu.VMEM((16, 4, 640), F32),
            pltpu.VMEM((4, 16, 4, 640), F32),
            pltpu.VMEM((4, 16, 4, 640), F32),
            pltpu.VMEM((4, 16, 4, 640), F32),
            pltpu.VMEM((64, 4, 640), F32),
            pltpu.VMEM((4, 32, 128), F32),
            dma((16,)), dma((5,)), dma((5,)), dma((7,)), dma((1,)), dma((16,)), dma((1,)),
            dma((4,)), dma((1,)), dma((4,)), dma((1,)), pltpu.SemaphoreType.REGULAR,
        ],
        name="exchange",
        compiler_params=pltpu.CompilerParams(
            collective_id=0, has_side_effects=True, vmem_limit_bytes=52 * 2**20
        ),
    )(acts, cotangent, q_t)
    p_t, q_new = pl.pallas_call(
        functools.partial(finish_kernel, root=float(width) ** 0.5),
        out_shape=(
            jax.ShapeDtypeStruct((2, 32, 1280), F32),
            jax.ShapeDtypeStruct((2, 32, 5120), F32),
        ),
        in_specs=[vmem] * 3,
        out_specs=(vmem, vmem),
        name="finish",
        compiler_params=pltpu.CompilerParams(vmem_limit_bytes=32 * 2**20),
    )(zag, pag, inverse)
    return jnp.swapaxes(p_t, 1, 2), jnp.swapaxes(q_new, 1, 2)


def solution(mesh):
    placed = (P(None, "dp", "tensor"), P(None, "dp", None), P())
    return jax.shard_map(
        local, mesh=mesh, in_specs=placed, out_specs=(P(None, "tensor", None), P()), check_vma=False
    )
```

```python
import functools

import jax
import jax.numpy as jnp
from jax import lax
from jax.experimental import pallas as pl
from jax.experimental.pallas import tpu as pltpu
from jax.sharding import PartitionSpec as P

MESH = pl.DeviceIdType.MESH
F32 = jnp.float32
BF16 = jnp.bfloat16
NN = (((1,), (0,)), ((), ()))
NT = (((1,), (1,)), ((), ()))
TILE = 256
WIDTHS = (1792, 1792, 1536)
STARTS = (0, 1792, 3584)


def hops(offset):
    return sum(min(d, 4 - d) for d in offset)


OFFSETS = [(dz, dy, dx) for dz in range(4) for dy in range(4) for dx in range(4)]
CUBE = sorted([o for o in OFFSETS if hops(o) > 0], key=hops, reverse=True)
PLANE = [o for o in CUBE if o[0] == 0]
AXIS = [o for o in CUBE if o[1] == 0 and o[2] == 0]
FLY = 5


def dot(a, b, dims):
    return lax.dot_general(a, b, dims, preferred_element_type=F32)


def split3(x):
    hi = x.astype(BF16)
    rest = x - hi.astype(F32)
    mid = rest.astype(BF16)
    low = (rest - mid.astype(F32)).astype(BF16)
    return jnp.concatenate([hi, mid, low], axis=0)


def sum3(x):
    return x[0:32] + x[32:64] + x[64:96]


def to_pieces(ref, value):
    half = value.shape[1] // 2
    for j in range(16):
        g, h = j // 2, j % 2
        ref[j] = value[4 * g : 4 * g + 4, half * h : half * h + half]


def from_pieces(ref):
    halves = []
    for h in range(2):
        halves.append(jnp.concatenate([ref[2 * g + h] for g in range(8)], axis=0))
    return jnp.concatenate(halves, axis=1)


def invert_factor(grams):
    rows = lax.broadcasted_iota(jnp.int32, (32, 128), 0)
    lanes = lax.broadcasted_iota(jnp.int32, (32, 128), 1)
    eye = jnp.where(rows == lanes % 32, 1.0, 0.0).astype(F32)
    work = jnp.where((lanes // 32) % 2 == 1, eye, grams)
    first = lanes < 64
    for k in range(32):
        row = work[k : k + 1, :]
        pivot = jnp.where(first[0:1], row[:, k : k + 1], row[:, 64 + k : 65 + k])
        scale = lax.rsqrt(pivot)
        scale = scale * (1.5 - 0.5 * pivot * scale * scale)
        column = jnp.where(first, work[:, k : k + 1], work[:, 64 + k : 65 + k])
        row = row * scale
        work = jnp.where(rows > k, work - (column * scale) * row, jnp.where(rows == k, row, work))
    return work


def exchange_kernel(
    a_hbm, c_hbm, q_hbm,
    zag0, zag1, zag2, pag, inv_ref,
    a, c, q, q3t, wt, yt, px, pxr, ps, prr, gram,
    zx0, zx1, zx2, zxr0, zxr1, zxr2, zs0, zs1, zs2, zrr0, zrr1, zrr2, zl0, zl1, zl2,
    load_sem, core_sem, corer_sem, send_sem, prs_sem, pag_sem, pfw_sem, g_sem,
    zsend_sem, zrs_sem, zline_sem, zag_sem, zfw_sem, near_sem,
):
    dp = lax.axis_index("dp")
    z = lax.axis_index("tensor")
    core = lax.rem(dp, 2)
    plane = dp // 2
    y, x = plane // 4, lax.rem(plane, 4)
    mine, other = core, 1 - core
    sibling = {"dp": plane * 2 + other, "tensor": z}

    ys = [lax.rem(y + d, 4) for d in range(4)]
    xs = [lax.rem(x + d, 4) for d in range(4)]
    zs_at = [lax.rem(z + d, 4) for d in range(4)]

    def place(dz, dy, dx):
        return ys[dy] * 4 + xs[dx], zs_at[dz]

    def device(dz, dy, dx):
        to_plane, to_z = place(dz, dy, dx)
        return {"dp": to_plane * 2 + core, "tensor": to_z}

    def back_from(dz, dy, dx):
        return place((4 - dz) % 4, (4 - dy) % 4, (4 - dx) % 4)

    zag, zx, zxr = (zag0, zag1, zag2), (zx0, zx1, zx2), (zxr0, zxr1, zxr2)
    zs, zrr, zl = (zs0, zs1, zs2), (zrr0, zrr1, zrr2), (zl0, zl1, zl2)

    def spin(k, du, dv, dw):
        return ((dw, du, dv), (dv, dw, du), (du, dv, dw))[k]

    def seat(k, offset):
        dz, dy, dx = offset
        u, v = ((ys[dy], xs[dx]), (xs[dx], zs_at[dz]), (zs_at[dz], ys[dy]))[k]
        return u * 4 + v

    def line_at(k):
        return (z, y, x)[k]

    def remote(src, dst, send, recv, device):
        return pltpu.make_async_remote_copy(
            src_ref=src, dst_ref=dst, send_sem=send, recv_sem=recv, device_id=device, device_id_type=MESH
        )

    pending = []

    def drain():
        for done in pending:
            done()

    items = []
    for layer in (other, mine):
        items.append((q_hbm.at[layer], q.at[layer]))
    for layer in (other, mine):
        items.append((a_hbm.at[layer], a.at[layer]))
        for t in range(512 // TILE):
            items.append((c_hbm.at[layer, pl.ds(t * TILE, TILE)], c.at[layer, pl.ds(t * TILE, TILE)]))
    loads = [pltpu.make_async_copy(s, d, load_sem.at[i]) for i, (s, d) in enumerate(items)]
    for load in loads[:FLY]:
        load.start()

    barrier = pltpu.get_barrier_semaphore()

    pl.semaphore_signal(barrier, inc=1, device_id=sibling, device_id_type=MESH)
    for offset in PLANE + AXIS:
        pl.semaphore_signal(barrier, inc=1, device_id=device(*offset), device_id_type=MESH)

    def arrive(i):
        loads[i].wait()
        if i + FLY < len(loads):
            loads[i + FLY].start()

    for i, layer in enumerate((other, mine)):
        arrive(i)
        q3t[layer] = split3(q[layer]).T
    for n, layer in enumerate((other, mine)):
        base = 2 + n * (1 + 512 // TILE)
        arrive(base)
        for t in range(512 // TILE):
            arrive(base + 1 + t)
            w = dot(c[layer, t * TILE : (t + 1) * TILE, :], q3t[layer], NN)
            wt[:, t * TILE : (t + 1) * TILE] = sum3(w.T) * (1.0 / 32.0)
        part = sum3(dot(split3(wt[...]), a[layer], NN))
        if n == 0:
            to_pieces(px, part)
            pl.semaphore_wait(barrier, 1 + len(PLANE) + len(AXIS))
            p_copy = remote(px, pxr, core_sem.at[0], corer_sem.at[0], sibling)
            p_copy.start()
            pending.append(p_copy.wait_send)
        else:
            to_pieces(ps, part)
    p_copy.wait_recv()
    ps[...] += pxr[...]

    for offset in PLANE:
        to_plane, _ = place(*offset)
        remote(ps.at[to_plane], prr.at[plane], send_sem.at[0], prs_sem.at[0], device(*offset)).start()
    pending.append(remote(ps.at[pl.ds(0, 15)], prr.at[pl.ds(0, 15)], send_sem.at[0], prs_sem.at[0], sibling).wait_send)
    prr[plane] = ps[plane]
    remote(ps.at[pl.ds(0, 15)], prr.at[pl.ds(0, 15)], send_sem.at[0], prs_sem.at[0], sibling).wait_recv()
    for offset in AXIS:
        pl.semaphore_signal(near_sem, inc=1, device_id=device(*offset), device_id_type=MESH)
    pag[mine, plane] = jnp.sum(prr[...], axis=0)

    own = pag.at[mine, plane]
    many = pag.at[mine, pl.ds(0, 15)]
    for offset in PLANE:
        remote(own, own, send_sem.at[1], pag_sem.at[plane], device(*offset)).start()
    pending.append(remote(many, many, send_sem.at[1], pag_sem.at[0], sibling).wait_send)
    remote(own, own, send_sem.at[2], pfw_sem.at[0], sibling).start()
    for offset in reversed(PLANE):
        from_plane, _ = back_from(*offset)
        slot = pag.at[mine, from_plane]
        remote(slot, slot, send_sem.at[0], pag_sem.at[from_plane], sibling).wait_recv()
        remote(slot, slot, send_sem.at[2], pfw_sem.at[0], sibling).start()
    pending.append(remote(pag.at[mine], pag.at[mine], send_sem.at[2], pfw_sem.at[0], sibling).wait_send)

    def back(layer):
        p3 = split3(from_pieces(pag.at[layer]))
        yt[layer] = sum3(dot(p3, a[layer], NT)) * (1.0 / 32.0)
        g9 = dot(p3, p3, NT)
        g3 = sum3(g9)
        return g3[:, 0:32] + g3[:, 32:64] + g3[:, 64:96]

    g_mine = back(mine)
    remote(pag.at[other], pag.at[other], send_sem.at[2], pfw_sem.at[0], sibling).wait_recv()
    g_other = back(other)

    def z_part(y3, layer, k, ref):
        to_pieces(ref, sum3(dot(y3, c[layer, :, STARTS[k] : STARTS[k] + WIDTHS[k]], NN)))

    y3 = split3(yt[other])
    z_copies = []
    for k in range(3):
        z_part(y3, other, k, zx[k])
        cp = remote(zx[k], zxr[k], core_sem.at[1 + k], corer_sem.at[1 + k], sibling)
        cp.start()
        z_copies.append(cp)
        pending.append(cp.wait_send)
    zero = jnp.zeros((32, 32), F32)
    g_first = jnp.where(core == 0, g_mine, g_other)
    g_second = jnp.where(core == 0, g_other, g_mine)
    gram[z] = jnp.concatenate([g_first, zero, g_second, zero], axis=1)
    for offset in AXIS:
        remote(gram.at[z], gram.at[z], send_sem.at[3], g_sem.at[z], device(*offset)).start()
    pending.append(remote(gram.at[pl.ds(0, 3)], gram.at[pl.ds(0, 3)], send_sem.at[3], g_sem.at[0], sibling).wait_send)
    y3 = split3(yt[mine])

    def all_of(ref, count, send, recv):
        view = ref.at[pl.ds(0, count)]
        return remote(view, view, send, recv, sibling)

    for k in range(3):
        z_part(y3, mine, k, zs[k])
        z_copies[k].wait_recv()
        zs[k][...] += zxr[k][...]
        if k == 0:
            pl.semaphore_wait(near_sem, len(AXIS))
        me = seat(k, (0, 0, 0))
        for _, du, dv in PLANE:
            offset = spin(k, du, dv, 0)
            remote(
                zs[k].at[seat(k, offset)], zrr[k].at[me], zsend_sem.at[k, 0], zrs_sem.at[k], device(*offset)
            ).start()
        pending.append(all_of(zs[k], 15, zsend_sem.at[k, 0], zrs_sem.at[k]).wait_send)
        zrr[k][me] = zs[k][me]

    for offset in AXIS:
        _, from_z = back_from(*offset)
        remote(gram.at[from_z], gram.at[from_z], send_sem.at[3], g_sem.at[from_z], sibling).wait_recv()
    inv_ref[...] = invert_factor(gram[0] + gram[1] + gram[2] + gram[3])

    for k in range(3):
        all_of(zrr[k], 15, zsend_sem.at[k, 0], zrs_sem.at[k]).wait_recv()
        w = line_at(k)
        zl[k][w] = jnp.sum(zrr[k][...], axis=0)
        for dw, _, _ in AXIS:
            remote(
                zl[k].at[w], zl[k].at[w], zsend_sem.at[k, 1], zline_sem.at[k], device(*spin(k, 0, 0, dw))
            ).start()
        pending.append(all_of(zl[k], 3, zsend_sem.at[k, 1], zline_sem.at[k]).wait_send)
    for k in range(3):
        all_of(zl[k], 3, zsend_sem.at[k, 1], zline_sem.at[k]).wait_recv()
        me = seat(k, (0, 0, 0))
        zag[k][mine, me] = zl[k][0] + zl[k][1] + zl[k][2] + zl[k][3]
        own = zag[k].at[mine, me]
        for _, du, dv in PLANE:
            remote(own, own, zsend_sem.at[k, 2], zag_sem.at[k], device(*spin(k, du, dv, 0))).start()
        pending.append(all_of(zag[k].at[mine], 15, zsend_sem.at[k, 2], zag_sem.at[k]).wait_send)
    for k in range(3):
        all_of(zag[k].at[mine], 15, zsend_sem.at[k, 2], zag_sem.at[k]).wait_recv()
        cp = remote(zag[k].at[mine], zag[k].at[mine], zsend_sem.at[k, 3], zfw_sem.at[k], sibling)
        cp.start()
        pending.append(cp.wait_send)
    for k in range(3):
        remote(zag[k].at[other], zag[k].at[other], zsend_sem.at[k, 3], zfw_sem.at[k], sibling).wait_recv()
    drain()


def finish_kernel(zag0, zag1, zag2, pag, inv_ref, p_out, q_out, *, root):
    for layer in range(2):
        inverse = inv_ref[:, 64 * layer + 32 : 64 * layer + 64]
        pieces = split3(inverse)
        left = jnp.concatenate([pieces, pieces, pieces], axis=1)
        p_out[layer] = sum3(dot(left, split3(from_pieces(pag.at[layer])), NN)) * root
        for zag, start, width in zip((zag0, zag1, zag2), STARTS, WIDTHS):
            block = from_pieces(zag.at[layer])
            q_out[layer, :, start : start + width] = sum3(dot(left, split3(block), NN))


def local(acts, cotangent, q_start):
    width = cotangent.shape[2]
    q_t = jnp.swapaxes(q_start, 1, 2)
    hbm = pl.BlockSpec(memory_space=pltpu.HBM)
    vmem = pl.BlockSpec(memory_space=pltpu.VMEM)
    dma = pltpu.SemaphoreType.DMA
    *gathered, inverse = pl.pallas_call(
        exchange_kernel,
        out_shape=(
            *[jax.ShapeDtypeStruct((2, 16, 4, width // 2), F32) for width in WIDTHS],
            jax.ShapeDtypeStruct((2, 16, 4, 640), F32),
            jax.ShapeDtypeStruct((32, 128), F32),
        ),
        in_specs=[hbm] * 3,
        out_specs=(vmem,) * 5,
        scratch_shapes=[
            pltpu.VMEM((2, 512, 1280), BF16),
            pltpu.VMEM((2, 512, 5120), BF16),
            pltpu.VMEM((2, 32, 5120), F32),
            pltpu.VMEM((2, 5120, 96), BF16),
            pltpu.VMEM((32, 512), F32),
            pltpu.VMEM((2, 32, 512), F32),
            pltpu.VMEM((16, 4, 640), F32),
            pltpu.VMEM((16, 4, 640), F32),
            pltpu.VMEM((16, 4, 640), F32),
            pltpu.VMEM((16, 4, 640), F32),
            pltpu.VMEM((4, 32, 128), F32),
            *[pltpu.VMEM((16, 4, width // 2), F32) for _ in range(4) for width in WIDTHS],
            *[pltpu.VMEM((4, 4, width // 2), F32) for width in WIDTHS],
            dma((16,)), dma((5,)), dma((5,)), dma((7,)), dma((1,)), dma((16,)), dma((1,)),
            dma((4,)), dma((3, 4)), dma((3,)), dma((3,)), dma((3,)), dma((3,)), pltpu.SemaphoreType.REGULAR,
        ],
        name="exchange",
        compiler_params=pltpu.CompilerParams(
            collective_id=0, has_side_effects=True, vmem_limit_bytes=52 * 2**20
        ),
    )(acts, cotangent, q_t)
    p_t, q_new = pl.pallas_call(
        functools.partial(finish_kernel, root=float(width) ** 0.5),
        out_shape=(
            jax.ShapeDtypeStruct((2, 32, 1280), F32),
            jax.ShapeDtypeStruct((2, 32, 5120), F32),
        ),
        in_specs=[vmem] * 5,
        out_specs=(vmem, vmem),
        name="finish",
        compiler_params=pltpu.CompilerParams(vmem_limit_bytes=32 * 2**20),
    )(*gathered, inverse)
    return jnp.swapaxes(p_t, 1, 2), jnp.swapaxes(q_new, 1, 2)


def solution(mesh):
    placed = (P(None, "dp", "tensor"), P(None, "dp", None), P())
    return jax.shard_map(
        local, mesh=mesh, in_specs=placed, out_specs=(P(None, "tensor", None), P()), check_vma=False
    )
```

```python
import functools

import jax
import jax.numpy as jnp
from jax import lax
from jax.experimental import pallas as pl
from jax.experimental.pallas import tpu as pltpu
from jax.sharding import PartitionSpec as P

MESH = pl.DeviceIdType.MESH
F32 = jnp.float32
BF16 = jnp.bfloat16
NN = (((1,), (0,)), ((), ()))
NT = (((1,), (1,)), ((), ()))
TILE = 256
WIDTHS = (2048, 1536, 1536)
STARTS = (0, 2048, 3584)
P_WIDTHS = (768, 512)
P_STARTS = (0, 768)


def hops(offset):
    return sum(min(d, 4 - d) for d in offset)


OFFSETS = [(dz, dy, dx) for dz in range(4) for dy in range(4) for dx in range(4)]
CUBE = sorted([o for o in OFFSETS if hops(o) > 0], key=hops, reverse=True)
PLANE = [o for o in CUBE if o[0] == 0]
AXIS = [o for o in CUBE if o[1] == 0 and o[2] == 0]
FLY = 5


def dot(a, b, dims):
    return lax.dot_general(a, b, dims, preferred_element_type=F32)


def split3(x):
    hi = x.astype(BF16)
    rest = x - hi.astype(F32)
    mid = rest.astype(BF16)
    low = (rest - mid.astype(F32)).astype(BF16)
    return jnp.concatenate([hi, mid, low], axis=0)


def sum3(x):
    return x[0:32] + x[32:64] + x[64:96]


def to_pieces(ref, value):
    quarter = value.shape[1] // 4
    for j in range(16):
        g, h = j // 4, j % 4
        ref[j] = value[8 * g : 8 * g + 8, quarter * h : quarter * h + quarter]


def from_pieces(ref):
    bands = []
    for g in range(4):
        bands.append(jnp.concatenate([ref[4 * g + h] for h in range(4)], axis=1))
    return jnp.concatenate(bands, axis=0)


def invert_factor(grams):
    rows = lax.broadcasted_iota(jnp.int32, (32, 128), 0)
    lanes = lax.broadcasted_iota(jnp.int32, (32, 128), 1)
    eye = jnp.where(rows == lanes % 32, 1.0, 0.0).astype(F32)
    work = jnp.where((lanes // 32) % 2 == 1, eye, grams)
    first = lanes < 64
    for k in range(32):
        row = work[k : k + 1, :]
        pivot = jnp.where(first[0:1], row[:, k : k + 1], row[:, 64 + k : 65 + k])
        scale = lax.rsqrt(pivot)
        scale = scale * (1.5 - 0.5 * pivot * scale * scale)
        column = jnp.where(first, work[:, k : k + 1], work[:, 64 + k : 65 + k])
        row = row * scale
        work = jnp.where(rows > k, work - (column * scale) * row, jnp.where(rows == k, row, work))
    return work


def exchange_kernel(
    a_hbm, c_hbm, q_hbm,
    zag0, zag1, zag2, pf0, pf1, inv_ref,
    a, c, q, q3t, wt, px0, px1, pxr0, pxr1, pa0, pa1, pb0, pb1, gram,
    zx0, zx1, zx2, zxr0, zxr1, zxr2, zs0, zs1, zs2, zrr0, zrr1, zrr2, zl0, zl1, zl2,
    load_sem, core_sem, corer_sem, psend_sem, pa_sem, pb_sem, pfw_sem, gsend_sem, g_sem,
    zsend_sem, zrs_sem, zline_sem, zag_sem, zfw_sem, near_sem,
):
    dp = lax.axis_index("dp")
    z = lax.axis_index("tensor")
    core = lax.rem(dp, 2)
    plane = dp // 2
    y, x = plane // 4, lax.rem(plane, 4)
    mine, other = core, 1 - core
    sibling = {"dp": plane * 2 + other, "tensor": z}

    ys = [lax.rem(y + d, 4) for d in range(4)]
    xs = [lax.rem(x + d, 4) for d in range(4)]
    zs_at = [lax.rem(z + d, 4) for d in range(4)]

    def place(dz, dy, dx):
        return ys[dy] * 4 + xs[dx], zs_at[dz]

    def device(dz, dy, dx):
        to_plane, to_z = place(dz, dy, dx)
        return {"dp": to_plane * 2 + core, "tensor": to_z}

    def back_from(dz, dy, dx):
        return place((4 - dz) % 4, (4 - dy) % 4, (4 - dx) % 4)

    px, pxr, pa, pb, pf = (px0, px1), (pxr0, pxr1), (pa0, pa1), (pb0, pb1), (pf0, pf1)
    zag, zx, zxr = (zag0, zag1, zag2), (zx0, zx1, zx2), (zxr0, zxr1, zxr2)
    zs, zrr, zl = (zs0, zs1, zs2), (zrr0, zrr1, zrr2), (zl0, zl1, zl2)

    first, second = jnp.where(core == 0, x, y), jnp.where(core == 0, y, x)

    def along_first(d):
        row, column = jnp.where(core == 0, y, ys[d]), jnp.where(core == 0, xs[d], x)
        return {"dp": (row * 4 + column) * 2 + core, "tensor": z}

    def along_second(d):
        row, column = jnp.where(core == 0, ys[d], y), jnp.where(core == 0, x, xs[d])
        return {"dp": (row * 4 + column) * 2 + core, "tensor": z}

    def spin(k, du, dv, dw):
        return ((dw, du, dv), (dv, dw, du), (du, dv, dw))[k]

    def seat(k, offset):
        dz, dy, dx = offset
        u, v = ((ys[dy], xs[dx]), (xs[dx], zs_at[dz]), (zs_at[dz], ys[dy]))[k]
        return u * 4 + v

    def line_at(k):
        return (z, y, x)[k]

    def remote(src, dst, send, recv, device):
        return pltpu.make_async_remote_copy(
            src_ref=src, dst_ref=dst, send_sem=send, recv_sem=recv, device_id=device, device_id_type=MESH
        )

    pending = []

    def drain():
        for done in pending:
            done()

    items = []
    for layer in (other, mine):
        items.append((q_hbm.at[layer], q.at[layer]))
    for layer in (other, mine):
        items.append((a_hbm.at[layer], a.at[layer]))
        for t in range(512 // TILE):
            items.append((c_hbm.at[layer, pl.ds(t * TILE, TILE)], c.at[layer, pl.ds(t * TILE, TILE)]))
    loads = [pltpu.make_async_copy(s, d, load_sem.at[i]) for i, (s, d) in enumerate(items)]
    for load in loads[:FLY]:
        load.start()

    barrier = pltpu.get_barrier_semaphore()

    pl.semaphore_signal(barrier, inc=1, device_id=sibling, device_id_type=MESH)
    for offset in PLANE + AXIS:
        pl.semaphore_signal(barrier, inc=1, device_id=device(*offset), device_id_type=MESH)

    def arrive(i):
        loads[i].wait()
        if i + FLY < len(loads):
            loads[i + FLY].start()

    for i, layer in enumerate((other, mine)):
        arrive(i)
        q3t[layer] = split3(q[layer]).T
    for n, layer in enumerate((other, mine)):
        base = 2 + n * (1 + 512 // TILE)
        arrive(base)
        for t in range(512 // TILE):
            arrive(base + 1 + t)
            w = dot(c[layer, t * TILE : (t + 1) * TILE, :], q3t[layer], NN)
            wt[:, t * TILE : (t + 1) * TILE] = sum3(w.T) * (1.0 / 32.0)
        part = sum3(dot(split3(wt[...]), a[layer], NN))
        if n == 0:
            for k in range(2):
                px[k][...] = part[:, P_STARTS[k] : P_STARTS[k] + P_WIDTHS[k]]
            pl.semaphore_wait(barrier, 1 + len(PLANE) + len(AXIS))
            p_copies = []
            for k in range(2):
                cp = remote(px[k], pxr[k], core_sem.at[k], corer_sem.at[k], sibling)
                cp.start()
                p_copies.append(cp)
                pending.append(cp.wait_send)
            for offset in AXIS:
                pl.semaphore_signal(near_sem, inc=1, device_id=device(*offset), device_id_type=MESH)

    def all_of(ref, count, send, recv):
        view = ref.at[pl.ds(0, count)]
        return remote(view, view, send, recv, sibling)

    for k in range(2):
        p_copies[k].wait_recv()
        pa[k][first] = part[:, P_STARTS[k] : P_STARTS[k] + P_WIDTHS[k]] + pxr[k][...]
        slot = pa[k].at[first]
        for d, _, _ in AXIS:
            remote(slot, slot, psend_sem.at[k, 0], pa_sem.at[k], along_first(d)).start()
        pending.append(all_of(pa[k], 3, psend_sem.at[k, 0], pa_sem.at[k]).wait_send)
    for k in range(2):
        all_of(pa[k], 3, psend_sem.at[k, 0], pa_sem.at[k]).wait_recv()
        pb[k][second] = pa[k][0] + pa[k][1] + pa[k][2] + pa[k][3]
        slot = pb[k].at[second]
        for d, _, _ in AXIS:
            remote(slot, slot, psend_sem.at[k, 1], pb_sem.at[k], along_second(d)).start()
        pending.append(all_of(pb[k], 3, psend_sem.at[k, 1], pb_sem.at[k]).wait_send)
    for k in range(2):
        all_of(pb[k], 3, psend_sem.at[k, 1], pb_sem.at[k]).wait_recv()
        pf[k][mine] = pb[k][0] + pb[k][1] + pb[k][2] + pb[k][3]
        slot = pf[k].at[mine]
        cp = remote(slot, slot, psend_sem.at[k, 2], pfw_sem.at[k], sibling)
        cp.start()
        pending.append(cp.wait_send)

    def p_pieces(layer):
        return split3(jnp.concatenate([pf[0][layer], pf[1][layer]], axis=1))

    def y_pieces(p3, layer):
        return split3(sum3(dot(p3, a[layer], NT)) * (1.0 / 32.0))

    def gram_of(p3):
        g3 = sum3(dot(p3, p3, NT))
        return g3[:, 0:32] + g3[:, 32:64] + g3[:, 64:96]

    def z_part(y3, layer, k):
        return sum3(dot(y3, c[layer, :, STARTS[k] : STARTS[k] + WIDTHS[k]], NN))

    p3 = p_pieces(mine)
    y3 = y_pieces(p3, mine)
    z_copies = []
    for k in range(3):
        to_pieces(zx[k], z_part(y3, mine, k))
        cp = remote(zx[k], zxr[k], core_sem.at[2 + k], corer_sem.at[2 + k], sibling)
        cp.start()
        z_copies.append(cp)
        pending.append(cp.wait_send)
    g_mine = gram_of(p3)

    for k in range(2):
        slot = pf[k].at[other]
        remote(slot, slot, psend_sem.at[k, 2], pfw_sem.at[k], sibling).wait_recv()
    p3 = p_pieces(other)
    y3 = y_pieces(p3, other)
    for k in range(3):
        to_pieces(zs[k], z_part(y3, other, k))
        z_copies[k].wait_recv()
        zs[k][...] += zxr[k][...]
        if k == 0:
            pl.semaphore_wait(near_sem, len(AXIS))
        me = seat(k, (0, 0, 0))
        for _, du, dv in PLANE:
            offset = spin(k, du, dv, 0)
            remote(
                zs[k].at[seat(k, offset)], zrr[k].at[me], zsend_sem.at[k, 0], zrs_sem.at[k], device(*offset)
            ).start()
        pending.append(all_of(zs[k], 15, zsend_sem.at[k, 0], zrs_sem.at[k]).wait_send)
        zrr[k][me] = zs[k][me]
    g_other = gram_of(p3)
    zero = jnp.zeros((32, 32), F32)
    g_first = jnp.where(core == 0, g_mine, g_other)
    g_second = jnp.where(core == 0, g_other, g_mine)
    gram[z] = jnp.concatenate([g_first, zero, g_second, zero], axis=1)
    for offset in AXIS:
        remote(gram.at[z], gram.at[z], gsend_sem.at[0], g_sem.at[z], device(*offset)).start()
    pending.append(all_of(gram, 3, gsend_sem.at[0], g_sem.at[0]).wait_send)

    for k in range(3):
        all_of(zrr[k], 15, zsend_sem.at[k, 0], zrs_sem.at[k]).wait_recv()
        w = line_at(k)
        zl[k][w] = jnp.sum(zrr[k][...], axis=0)
        for dw, _, _ in AXIS:
            remote(
                zl[k].at[w], zl[k].at[w], zsend_sem.at[k, 1], zline_sem.at[k], device(*spin(k, 0, 0, dw))
            ).start()
        pending.append(all_of(zl[k], 3, zsend_sem.at[k, 1], zline_sem.at[k]).wait_send)
    for k in range(3):
        all_of(zl[k], 3, zsend_sem.at[k, 1], zline_sem.at[k]).wait_recv()
        me = seat(k, (0, 0, 0))
        zag[k][other, me] = zl[k][0] + zl[k][1] + zl[k][2] + zl[k][3]
        own = zag[k].at[other, me]
        for _, du, dv in PLANE:
            remote(own, own, zsend_sem.at[k, 2], zag_sem.at[k, me // 4], device(*spin(k, du, dv, 0))).start()
        pending.append(all_of(zag[k].at[other], 15, zsend_sem.at[k, 2], zag_sem.at[k, 0]).wait_send)

    for offset in AXIS:
        _, from_z = back_from(*offset)
        remote(gram.at[from_z], gram.at[from_z], gsend_sem.at[0], g_sem.at[from_z], sibling).wait_recv()
    inv_ref[...] = invert_factor(gram[0] + gram[1] + gram[2] + gram[3])

    for k in range(3):
        for d in (0, 1, 3, 2):
            u = lax.rem(seat(k, (0, 0, 0)) // 4 + d, 4)
            block = zag[k].at[other, pl.ds(u * 4, 3 if d == 0 else 4)]
            remote(block, block, zsend_sem.at[k, 3], zag_sem.at[k, u], sibling).wait_recv()
            block = zag[k].at[other, pl.ds(u * 4, 4)]
            remote(block, block, zsend_sem.at[k, 3], zfw_sem.at[k], sibling).start()
        pending.append(remote(zag[k].at[other], zag[k].at[other], zsend_sem.at[k, 3], zfw_sem.at[k], sibling).wait_send)
    for k in range(3):
        remote(zag[k].at[mine], zag[k].at[mine], zsend_sem.at[k, 3], zfw_sem.at[k], sibling).wait_recv()
    drain()


def finish_kernel(zag0, zag1, zag2, pf0, pf1, inv_ref, p_out, q_out, *, root):
    for layer in range(2):
        inverse = inv_ref[:, 64 * layer + 32 : 64 * layer + 64]
        pieces = split3(inverse)
        left = jnp.concatenate([pieces, pieces, pieces], axis=1)
        for pf, start, width in zip((pf0, pf1), P_STARTS, P_WIDTHS):
            p_out[layer, :, start : start + width] = sum3(dot(left, split3(pf[layer]), NN)) * root
        for zag, start, width in zip((zag0, zag1, zag2), STARTS, WIDTHS):
            block = from_pieces(zag.at[layer])
            q_out[layer, :, start : start + width] = sum3(dot(left, split3(block), NN))


def local(acts, cotangent, q_start):
    width = cotangent.shape[2]
    q_t = jnp.swapaxes(q_start, 1, 2)
    hbm = pl.BlockSpec(memory_space=pltpu.HBM)
    vmem = pl.BlockSpec(memory_space=pltpu.VMEM)
    dma = pltpu.SemaphoreType.DMA
    *gathered, inverse = pl.pallas_call(
        exchange_kernel,
        out_shape=(
            *[jax.ShapeDtypeStruct((2, 16, 8, width // 4), F32) for width in WIDTHS],
            *[jax.ShapeDtypeStruct((2, 32, width), F32) for width in P_WIDTHS],
            jax.ShapeDtypeStruct((32, 128), F32),
        ),
        in_specs=[hbm] * 3,
        out_specs=(vmem,) * 6,
        scratch_shapes=[
            pltpu.VMEM((2, 512, 1280), BF16),
            pltpu.VMEM((2, 512, 5120), BF16),
            pltpu.VMEM((2, 32, 5120), F32),
            pltpu.VMEM((2, 5120, 96), BF16),
            pltpu.VMEM((32, 512), F32),
            *[pltpu.VMEM((32, width), F32) for _ in range(2) for width in P_WIDTHS],
            *[pltpu.VMEM((4, 32, width), F32) for _ in range(2) for width in P_WIDTHS],
            pltpu.VMEM((4, 32, 128), F32),
            *[pltpu.VMEM((16, 8, width // 4), F32) for _ in range(4) for width in WIDTHS],
            *[pltpu.VMEM((4, 8, width // 4), F32) for width in WIDTHS],
            dma((16,)), dma((5,)), dma((5,)), dma((2, 3)), dma((2,)), dma((2,)), dma((2,)), dma((1,)), dma((4,)),
            dma((3, 4)), dma((3,)), dma((3,)), dma((3, 4)), dma((3,)), pltpu.SemaphoreType.REGULAR,
        ],
        name="exchange",
        compiler_params=pltpu.CompilerParams(
            collective_id=0, has_side_effects=True, vmem_limit_bytes=52 * 2**20
        ),
    )(acts, cotangent, q_t)
    p_t, q_new = pl.pallas_call(
        functools.partial(finish_kernel, root=float(width) ** 0.5),
        out_shape=(
            jax.ShapeDtypeStruct((2, 32, 1280), F32),
            jax.ShapeDtypeStruct((2, 32, 5120), F32),
        ),
        in_specs=[vmem] * 6,
        out_specs=(vmem, vmem),
        name="finish",
        compiler_params=pltpu.CompilerParams(vmem_limit_bytes=32 * 2**20),
    )(*gathered, inverse)
    return jnp.swapaxes(p_t, 1, 2), jnp.swapaxes(q_new, 1, 2)


def solution(mesh):
    placed = (P(None, "dp", "tensor"), P(None, "dp", None), P())
    return jax.shard_map(
        local, mesh=mesh, in_specs=placed, out_specs=(P(None, "tensor", None), P()), check_vma=False
    )
```

```python
import functools

import jax
import jax.numpy as jnp
from jax import lax
from jax.experimental import pallas as pl
from jax.experimental.pallas import tpu as pltpu
from jax.sharding import PartitionSpec as P

MESH = pl.DeviceIdType.MESH
F32 = jnp.float32
BF16 = jnp.bfloat16
NN = (((1,), (0,)), ((), ()))
NT = (((1,), (1,)), ((), ()))
TILE = 256
FLY = 5
WIDTHS = (1024, 1024, 512)
P_WIDTHS = (384, 256)
STARTS = tuple(sum(WIDTHS[:k]) for k in range(len(WIDTHS)))
P_STARTS = tuple(sum(P_WIDTHS[:k]) for k in range(len(P_WIDTHS)))
Z_CHUNKS, P_CHUNKS = len(WIDTHS), len(P_WIDTHS)
Z_HALF, P_HALF = sum(WIDTHS), sum(P_WIDTHS)


def hops(offset):
    return sum(min(d, 4 - d) for d in offset)


OFFSETS = [(dz, dy, dx) for dz in range(4) for dy in range(4) for dx in range(4)]
CUBE = sorted([o for o in OFFSETS if hops(o) > 0], key=hops, reverse=True)
PLANE = [o for o in CUBE if o[0] == 0]
AXIS = [o for o in CUBE if o[1] == 0 and o[2] == 0]
FLY = 5


def dot(a, b, dims):
    return lax.dot_general(a, b, dims, preferred_element_type=F32)


def split3(x):
    hi = x.astype(BF16)
    rest = x - hi.astype(F32)
    mid = rest.astype(BF16)
    low = (rest - mid.astype(F32)).astype(BF16)
    return jnp.concatenate([hi, mid, low], axis=0)


def sum3(x):
    return x[0:32] + x[32:64] + x[64:96]


def to_pieces(ref, value):
    quarter = value.shape[1] // 4
    for j in range(16):
        g, h = j // 4, j % 4
        ref[j] = value[8 * g : 8 * g + 8, quarter * h : quarter * h + quarter]


def from_pieces(ref):
    bands = []
    for g in range(4):
        bands.append(jnp.concatenate([ref[4 * g + h] for h in range(4)], axis=1))
    return jnp.concatenate(bands, axis=0)


def invert_factor(grams):
    rows = lax.broadcasted_iota(jnp.int32, (32, 128), 0)
    lanes = lax.broadcasted_iota(jnp.int32, (32, 128), 1)
    eye = jnp.where(rows == lanes % 32, 1.0, 0.0).astype(F32)
    work = jnp.where((lanes // 32) % 2 == 1, eye, grams)
    first = lanes < 64
    for k in range(32):
        row = work[k : k + 1, :]
        pivot = jnp.where(first[0:1], row[:, k : k + 1], row[:, 64 + k : 65 + k])
        scale = lax.rsqrt(pivot)
        scale = scale * (1.5 - 0.5 * pivot * scale * scale)
        column = jnp.where(first, work[:, k : k + 1], work[:, 64 + k : 65 + k])
        row = row * scale
        work = jnp.where(rows > k, work - (column * scale) * row, jnp.where(rows == k, row, work))
    return work


def exchange_kernel(a_hbm, c_hbm, q_hbm, *refs):
    left = list(refs)

    def take(count):
        taken = left[:count]
        del left[:count]
        return taken

    zag, pf = [take(Z_CHUNKS) for _ in range(2)], [take(P_CHUNKS) for _ in range(2)]
    (inv_ref,) = take(1)
    a, c, q, q3t, wt, px, pxr, gram = take(8)
    pa, pb = ([take(P_CHUNKS) for _ in range(2)] for _ in range(2))
    zx, zxr, zs, zrr, zl = ([take(Z_CHUNKS) for _ in range(2)] for _ in range(5))
    load_sem, px_sem, pxr_sem, psend_sem, pa_sem, pb_sem, pfw_sem, gsend_sem, g_sem = take(9)
    zx_sem, zxr_sem, zsend_sem, zrs_sem, zline_sem, zag_sem, zfw_sem, near_sem = take(8)
    dp = lax.axis_index("dp")
    z = lax.axis_index("tensor")
    core = lax.rem(dp, 2)
    plane = dp // 2
    y, x = plane // 4, lax.rem(plane, 4)
    mine, other = core, 1 - core
    sibling = {"dp": plane * 2 + other, "tensor": z}

    ys = [lax.rem(y + d, 4) for d in range(4)]
    xs = [lax.rem(x + d, 4) for d in range(4)]
    zs_at = [lax.rem(z + d, 4) for d in range(4)]

    def place(dz, dy, dx):
        return ys[dy] * 4 + xs[dx], zs_at[dz]

    def device(dz, dy, dx):
        to_plane, to_z = place(dz, dy, dx)
        return {"dp": to_plane * 2 + core, "tensor": to_z}

    def back_from(dz, dy, dx):
        return place((4 - dz) % 4, (4 - dy) % 4, (4 - dx) % 4)

    first, second = jnp.where(core == 0, x, y), jnp.where(core == 0, y, x)

    def along_first(d):
        row, column = jnp.where(core == 0, y, ys[d]), jnp.where(core == 0, xs[d], x)
        return {"dp": (row * 4 + column) * 2 + core, "tensor": z}

    def along_second(d):
        row, column = jnp.where(core == 0, ys[d], y), jnp.where(core == 0, x, xs[d])
        return {"dp": (row * 4 + column) * 2 + core, "tensor": z}

    def spin(l, k, du, dv, dw):
        return ((dw, du, dv), (dv, dw, du), (du, dv, dw))[(l + k) % 3]

    def seat(l, k, offset):
        dz, dy, dx = offset
        u, v = ((ys[dy], xs[dx]), (xs[dx], zs_at[dz]), (zs_at[dz], ys[dy]))[(l + k) % 3]
        return u * 4 + v

    def line_at(l, k):
        return (z, y, x)[(l + k) % 3]

    def remote(src, dst, send, recv, device):
        return pltpu.make_async_remote_copy(
            src_ref=src, dst_ref=dst, send_sem=send, recv_sem=recv, device_id=device, device_id_type=MESH
        )

    pending = []

    def drain():
        for done in pending:
            done()

    def all_of(ref, count, send, recv):
        view = ref.at[pl.ds(0, count)]
        return remote(view, view, send, recv, sibling)

    items = []
    for l in range(2):
        items.append((q_hbm.at[l], q.at[l]))
    for l in range(2):
        items.append((a_hbm.at[l], a.at[l]))
        for t in range(512 // TILE):
            items.append((c_hbm.at[l, pl.ds(t * TILE, TILE)], c.at[l, pl.ds(t * TILE, TILE)]))
    loads = [pltpu.make_async_copy(s, d, load_sem.at[i]) for i, (s, d) in enumerate(items)]
    for load in loads[:FLY]:
        load.start()

    barrier = pltpu.get_barrier_semaphore()

    pl.semaphore_signal(barrier, inc=1, device_id=sibling, device_id_type=MESH)
    for offset in PLANE + AXIS:
        pl.semaphore_signal(barrier, inc=1, device_id=device(*offset), device_id_type=MESH)

    def arrive(i):
        loads[i].wait()
        if i + FLY < len(loads):
            loads[i + FLY].start()

    def half_of(h):
        return pl.ds(pl.multiple_of(h * P_HALF, 128), P_HALF)

    def tokens(l, t):
        base = 2 + l * (1 + 512 // TILE)
        if t == 0:
            arrive(base)
        arrive(base + 1 + t)
        w = dot(c[l, t * TILE : (t + 1) * TILE, :], q3t[l], NN)
        wt[:, t * TILE : (t + 1) * TILE] = sum3(w.T) * (1.0 / 32.0)

    def p_part(l, h):
        return sum3(dot(split3(wt[...]), a[l, :, half_of(h)], NN))

    def pair_start(l):
        px[l] = p_part(l, other)
        cp = remote(px.at[l], pxr.at[l], px_sem.at[l], pxr_sem.at[l], sibling)
        cp.start()
        pending.append(cp.wait_send)
        return p_part(l, mine)

    def p_first(l, part):
        remote(px.at[l], pxr.at[l], px_sem.at[l], pxr_sem.at[l], sibling).wait_recv()
        for k in range(P_CHUNKS):
            cols = slice(P_STARTS[k], P_STARTS[k] + P_WIDTHS[k])
            pa[l][k][first] = part[:, cols] + pxr[l, :, cols]
            slot = pa[l][k].at[first]
            for d, _, _ in AXIS:
                remote(slot, slot, psend_sem.at[l, k, 0], pa_sem.at[l, k], along_first(d)).start()
            pending.append(all_of(pa[l][k], 3, psend_sem.at[l, k, 0], pa_sem.at[l, k]).wait_send)

    def p_second(l):
        for k in range(P_CHUNKS):
            src, dst = pa[l][k], pb[l][k]
            all_of(src, 3, psend_sem.at[l, k, 0], pa_sem.at[l, k]).wait_recv()
            dst[second] = src[0] + src[1] + src[2] + src[3]
            slot = dst.at[second]
            for d, _, _ in AXIS:
                remote(slot, slot, psend_sem.at[l, k, 1], pb_sem.at[l, k], along_second(d)).start()
            pending.append(all_of(dst, 3, psend_sem.at[l, k, 1], pb_sem.at[l, k]).wait_send)

    def p_third(l):
        for k in range(P_CHUNKS):
            src = pb[l][k]
            all_of(src, 3, psend_sem.at[l, k, 1], pb_sem.at[l, k]).wait_recv()
            pf[l][k][mine] = src[0] + src[1] + src[2] + src[3]
            slot = pf[l][k].at[mine]
            cp = remote(slot, slot, psend_sem.at[l, k, 2], pfw_sem.at[l, k], sibling)
            cp.start()
            pending.append(cp.wait_send)

    def half_pieces(l, h):
        return split3(jnp.concatenate([pf[l][k][h] for k in range(P_CHUNKS)], axis=1))

    def gram_of(p3):
        g3 = sum3(dot(p3, p3, NT))
        return g3[:, 0:32] + g3[:, 32:64] + g3[:, 64:96]

    def y_pieces(l):
        p_mine = half_pieces(l, mine)
        y = sum3(dot(p_mine, a[l, :, half_of(mine)], NT))
        for k in range(P_CHUNKS):
            slot = pf[l][k].at[other]
            remote(slot, slot, psend_sem.at[l, k, 2], pfw_sem.at[l, k], sibling).wait_recv()
        p_other = half_pieces(l, other)
        y = y + sum3(dot(p_other, a[l, :, half_of(other)], NT))
        return split3(y * (1.0 / 32.0)), p_mine, p_other

    def z_part(l, k, h, y3):
        cols = pl.ds(pl.multiple_of(h * Z_HALF + STARTS[k], 128), WIDTHS[k])
        return sum3(dot(y3, c[l, :, cols], NN))

    def z_scatter(l, y3):
        for k in range(Z_CHUNKS):
            to_pieces(zx[l][k], z_part(l, k, other, y3))
            cp = remote(zx[l][k], zxr[l][k], zx_sem.at[l, k], zxr_sem.at[l, k], sibling)
            cp.start()
            pending.append(cp.wait_send)
        for k in range(Z_CHUNKS):
            to_pieces(zs[l][k], z_part(l, k, mine, y3))
            remote(zx[l][k], zxr[l][k], zx_sem.at[l, k], zxr_sem.at[l, k], sibling).wait_recv()
            zs[l][k][...] += zxr[l][k][...]
            me = seat(l, k, (0, 0, 0))
            for _, du, dv in PLANE:
                offset = spin(l, k, du, dv, 0)
                remote(
                    zs[l][k].at[seat(l, k, offset)], zrr[l][k].at[me],
                    zsend_sem.at[l, k, 0], zrs_sem.at[l, k], device(*offset),
                ).start()
            pending.append(all_of(zs[l][k], 15, zsend_sem.at[l, k, 0], zrs_sem.at[l, k]).wait_send)
            zrr[l][k][me] = zs[l][k][me]

    def z_line(l):
        for k in range(Z_CHUNKS):
            all_of(zrr[l][k], 15, zsend_sem.at[l, k, 0], zrs_sem.at[l, k]).wait_recv()
            w = line_at(l, k)
            zl[l][k][w] = jnp.sum(zrr[l][k][...], axis=0)
            slot = zl[l][k].at[w]
            for dw, _, _ in AXIS:
                remote(
                    slot, slot, zsend_sem.at[l, k, 1], zline_sem.at[l, k], device(*spin(l, k, 0, 0, dw))
                ).start()
            pending.append(all_of(zl[l][k], 3, zsend_sem.at[l, k, 1], zline_sem.at[l, k]).wait_send)

    def z_gather(l):
        for k in range(Z_CHUNKS):
            src = zl[l][k]
            all_of(src, 3, zsend_sem.at[l, k, 1], zline_sem.at[l, k]).wait_recv()
            me = seat(l, k, (0, 0, 0))
            zag[l][k][mine, me] = src[0] + src[1] + src[2] + src[3]
            own = zag[l][k].at[mine, me]
            for _, du, dv in PLANE:
                remote(
                    own, own, zsend_sem.at[l, k, 2], zag_sem.at[l, k, me // 4], device(*spin(l, k, du, dv, 0))
                ).start()
            pending.append(all_of(zag[l][k].at[mine], 15, zsend_sem.at[l, k, 2], zag_sem.at[l, k, 0]).wait_send)

    def z_forward(l):
        for k in range(Z_CHUNKS):
            whole = zag[l][k].at[mine]
            for d in (0, 1, 3, 2):
                u = lax.rem(seat(l, k, (0, 0, 0)) // 4 + d, 4)
                block = zag[l][k].at[mine, pl.ds(u * 4, 3 if d == 0 else 4)]
                remote(block, block, zsend_sem.at[l, k, 3], zag_sem.at[l, k, u], sibling).wait_recv()
                block = zag[l][k].at[mine, pl.ds(u * 4, 4)]
                remote(block, block, zsend_sem.at[l, k, 3], zfw_sem.at[l, k], sibling).start()
            pending.append(remote(whole, whole, zsend_sem.at[l, k, 3], zfw_sem.at[l, k], sibling).wait_send)

    def z_finish(l):
        for k in range(Z_CHUNKS):
            whole = zag[l][k].at[other]
            remote(whole, whole, zsend_sem.at[l, k, 3], zfw_sem.at[l, k], sibling).wait_recv()

    for l in range(2):
        arrive(l)
        q3t[l] = split3(q[l]).T
    for t in range(512 // TILE):
        tokens(0, t)
    pl.semaphore_wait(barrier, 1 + len(PLANE) + len(AXIS))
    for offset in AXIS:
        pl.semaphore_signal(near_sem, inc=1, device_id=device(*offset), device_id_type=MESH)
    part = pair_start(0)
    tokens(1, 0)
    p_first(0, part)
    for t in range(1, 512 // TILE):
        tokens(1, t)
    part = pair_start(1)
    p_first(1, part)
    p_second(0)
    p_second(1)
    pl.semaphore_wait(near_sem, len(AXIS))
    p_third(0)
    y3, p_mine, p_other = y_pieces(0)
    z_scatter(0, y3)
    g_first = gram_of(p_mine) + gram_of(p_other)
    p_third(1)
    y3, p_mine, p_other = y_pieces(1)
    z_scatter(1, y3)
    g_second = gram_of(p_mine) + gram_of(p_other)
    zero = jnp.zeros((32, 32), F32)
    gram[z] = jnp.concatenate([g_first, zero, g_second, zero], axis=1)
    for offset in AXIS:
        remote(gram.at[z], gram.at[z], gsend_sem.at[0], g_sem.at[z], device(*offset)).start()
    pending.append(all_of(gram, 3, gsend_sem.at[0], g_sem.at[0]).wait_send)
    z_line(0)
    z_gather(0)
    z_line(1)
    for offset in AXIS:
        _, from_z = back_from(*offset)
        remote(gram.at[from_z], gram.at[from_z], gsend_sem.at[0], g_sem.at[from_z], sibling).wait_recv()
    inv_ref[...] = invert_factor(gram[0] + gram[1] + gram[2] + gram[3])
    z_gather(1)
    z_forward(0)
    z_forward(1)
    z_finish(0)
    z_finish(1)
    drain()


def finish_kernel(*refs, root):
    zags, pfs = refs[: 2 * Z_CHUNKS], refs[2 * Z_CHUNKS : 2 * Z_CHUNKS + 2 * P_CHUNKS]
    inv_ref, p_out, q_out = refs[2 * Z_CHUNKS + 2 * P_CHUNKS :]
    for l in range(2):
        pieces = split3(inv_ref[:, 64 * l + 32 : 64 * l + 64])
        left = jnp.concatenate([pieces, pieces, pieces], axis=1)
        for h in range(2):
            for k in range(P_CHUNKS):
                start = h * P_HALF + P_STARTS[k]
                block = pfs[l * P_CHUNKS + k][h]
                p_out[l, :, start : start + P_WIDTHS[k]] = sum3(dot(left, split3(block), NN)) * root
            for k in range(Z_CHUNKS):
                start = h * Z_HALF + STARTS[k]
                block = from_pieces(zags[l * Z_CHUNKS + k].at[h])
                q_out[l, :, start : start + WIDTHS[k]] = sum3(dot(left, split3(block), NN))


def local(acts, cotangent, q_start):
    width = cotangent.shape[2]
    q_t = jnp.swapaxes(q_start, 1, 2)
    hbm = pl.BlockSpec(memory_space=pltpu.HBM)
    vmem = pl.BlockSpec(memory_space=pltpu.VMEM)
    dma = pltpu.SemaphoreType.DMA
    count = 2 * Z_CHUNKS + 2 * P_CHUNKS + 1

    def chunks(shape_of, widths, times=1):
        return [pltpu.VMEM(shape_of(width), F32) for _ in range(2 * times) for width in widths]

    *gathered, inverse = pl.pallas_call(
        exchange_kernel,
        out_shape=(
            *[jax.ShapeDtypeStruct((2, 16, 8, w // 4), F32) for _ in range(2) for w in WIDTHS],
            *[jax.ShapeDtypeStruct((2, 32, w), F32) for _ in range(2) for w in P_WIDTHS],
            jax.ShapeDtypeStruct((32, 128), F32),
        ),
        in_specs=[hbm] * 3,
        out_specs=(vmem,) * count,
        scratch_shapes=[
            pltpu.VMEM((2, 512, 1280), BF16),
            pltpu.VMEM((2, 512, 5120), BF16),
            pltpu.VMEM((2, 32, 5120), F32),
            pltpu.VMEM((2, 5120, 96), BF16),
            pltpu.VMEM((32, 512), F32),
            pltpu.VMEM((2, 32, P_HALF), F32),
            pltpu.VMEM((2, 32, P_HALF), F32),
            pltpu.VMEM((4, 32, 128), F32),
            *chunks(lambda w: (4, 32, w), P_WIDTHS, 2),
            *chunks(lambda w: (16, 8, w // 4), WIDTHS, 4),
            *chunks(lambda w: (4, 8, w // 4), WIDTHS),
            dma((16,)), dma((2,)), dma((2,)), dma((2, P_CHUNKS, 3)), dma((2, P_CHUNKS)), dma((2, P_CHUNKS)),
            dma((2, P_CHUNKS)), dma((1,)), dma((4,)),
            dma((2, Z_CHUNKS)), dma((2, Z_CHUNKS)), dma((2, Z_CHUNKS, 4)), dma((2, Z_CHUNKS)), dma((2, Z_CHUNKS)),
            dma((2, Z_CHUNKS, 4)), dma((2, Z_CHUNKS)), pltpu.SemaphoreType.REGULAR,
        ],
        name="exchange",
        compiler_params=pltpu.CompilerParams(
            collective_id=0, has_side_effects=True, vmem_limit_bytes=52 * 2**20
        ),
    )(acts, cotangent, q_t)
    p_t, q_new = pl.pallas_call(
        functools.partial(finish_kernel, root=float(width) ** 0.5),
        out_shape=(
            jax.ShapeDtypeStruct((2, 32, 1280), F32),
            jax.ShapeDtypeStruct((2, 32, 5120), F32),
        ),
        in_specs=[vmem] * count,
        out_specs=(vmem, vmem),
        name="finish",
        compiler_params=pltpu.CompilerParams(vmem_limit_bytes=32 * 2**20),
    )(*gathered, inverse)
    return jnp.swapaxes(p_t, 1, 2), jnp.swapaxes(q_new, 1, 2)


def solution(mesh):
    placed = (P(None, "dp", "tensor"), P(None, "dp", None), P())
    return jax.shard_map(
        local, mesh=mesh, in_specs=placed, out_specs=(P(None, "tensor", None), P()), check_vma=False
    )
```

```python
import functools

import jax
import jax.numpy as jnp
from jax import lax
from jax.experimental import pallas as pl
from jax.experimental.pallas import tpu as pltpu
from jax.sharding import PartitionSpec as P

MESH = pl.DeviceIdType.MESH
F32 = jnp.float32
BF16 = jnp.bfloat16
NN = (((1,), (0,)), ((), ()))
NT = (((1,), (1,)), ((), ()))
TILE = 256
FLY = 5
WIDTHS = (1024, 1024, 512)
P_WIDTHS = (384, 256)
STARTS = tuple(sum(WIDTHS[:k]) for k in range(len(WIDTHS)))
P_STARTS = tuple(sum(P_WIDTHS[:k]) for k in range(len(P_WIDTHS)))
Z_CHUNKS, P_CHUNKS = len(WIDTHS), len(P_WIDTHS)
Z_HALF, P_HALF = sum(WIDTHS), sum(P_WIDTHS)


def hops(offset):
    return sum(min(d, 4 - d) for d in offset)


OFFSETS = [(dz, dy, dx) for dz in range(4) for dy in range(4) for dx in range(4)]
CUBE = sorted([o for o in OFFSETS if hops(o) > 0], key=hops, reverse=True)
PLANE = [o for o in CUBE if o[0] == 0]
AXIS = [o for o in CUBE if o[1] == 0 and o[2] == 0]
FLY = 5


def dot(a, b, dims):
    return lax.dot_general(a, b, dims, preferred_element_type=F32)


def split3(x):
    hi = x.astype(BF16)
    rest = x - hi.astype(F32)
    mid = rest.astype(BF16)
    low = (rest - mid.astype(F32)).astype(BF16)
    return jnp.concatenate([hi, mid, low], axis=0)


def sum3(x):
    return x[0:32] + x[32:64] + x[64:96]


def to_pieces(ref, value):
    quarter = value.shape[1] // 4
    for j in range(16):
        g, h = j // 4, j % 4
        ref[j] = value[8 * g : 8 * g + 8, quarter * h : quarter * h + quarter]


def from_pieces(ref):
    bands = []
    for g in range(4):
        bands.append(jnp.concatenate([ref[4 * g + h] for h in range(4)], axis=1))
    return jnp.concatenate(bands, axis=0)


def eliminate(work, steps, start=False):
    rows = lax.broadcasted_iota(jnp.int32, (32, 128), 0)
    lanes = lax.broadcasted_iota(jnp.int32, (32, 128), 1)
    if start:
        eye = jnp.where(rows == lanes % 32, 1.0, 0.0).astype(F32)
        work = jnp.where((lanes // 32) % 2 == 1, eye, work)
    first = lanes < 64
    for k in steps:
        row = work[k : k + 1, :]
        pivot = jnp.where(first[0:1], row[:, k : k + 1], row[:, 64 + k : 65 + k])
        scale = lax.rsqrt(pivot)
        scale = scale * (1.5 - 0.5 * pivot * scale * scale)
        column = jnp.where(first, work[:, k : k + 1], work[:, 64 + k : 65 + k])
        row = row * scale
        work = jnp.where(rows > k, work - (column * scale) * row, jnp.where(rows == k, row, work))
    return work


def exchange_kernel(a_hbm, c_hbm, q_hbm, *refs):
    left = list(refs)

    def take(count):
        taken = left[:count]
        del left[:count]
        return taken

    zag, pf = [take(Z_CHUNKS) for _ in range(2)], [take(P_CHUNKS) for _ in range(2)]
    (inv_ref,) = take(1)
    a, c, q, q3t, wt, px, pxr, gram = take(8)
    pa, pb = ([take(P_CHUNKS) for _ in range(2)] for _ in range(2))
    zx, zxr, zs, zrr, zl = ([take(Z_CHUNKS) for _ in range(2)] for _ in range(5))
    load_sem, px_sem, pxr_sem, psend_sem, pa_sem, pb_sem, pfw_sem, gsend_sem, g_sem = take(9)
    zx_sem, zxr_sem, zsend_sem, zrs_sem, zline_sem, zag_sem, zfw_sem, near_sem = take(8)
    dp = lax.axis_index("dp")
    z = lax.axis_index("tensor")
    core = lax.rem(dp, 2)
    plane = dp // 2
    y, x = plane // 4, lax.rem(plane, 4)
    mine, other = core, 1 - core
    sibling = {"dp": plane * 2 + other, "tensor": z}

    ys = [lax.rem(y + d, 4) for d in range(4)]
    xs = [lax.rem(x + d, 4) for d in range(4)]
    zs_at = [lax.rem(z + d, 4) for d in range(4)]

    def place(dz, dy, dx):
        return ys[dy] * 4 + xs[dx], zs_at[dz]

    def device(dz, dy, dx):
        to_plane, to_z = place(dz, dy, dx)
        return {"dp": to_plane * 2 + core, "tensor": to_z}

    def back_from(dz, dy, dx):
        return place((4 - dz) % 4, (4 - dy) % 4, (4 - dx) % 4)

    first, second = jnp.where(core == 0, x, y), jnp.where(core == 0, y, x)

    def along_first(d):
        row, column = jnp.where(core == 0, y, ys[d]), jnp.where(core == 0, xs[d], x)
        return {"dp": (row * 4 + column) * 2 + core, "tensor": z}

    def along_second(d):
        row, column = jnp.where(core == 0, ys[d], y), jnp.where(core == 0, x, xs[d])
        return {"dp": (row * 4 + column) * 2 + core, "tensor": z}

    def spin(l, k, du, dv, dw):
        return ((dw, du, dv), (dv, dw, du), (du, dv, dw))[(l + k) % 3]

    def seat(l, k, offset):
        dz, dy, dx = offset
        u, v = ((ys[dy], xs[dx]), (xs[dx], zs_at[dz]), (zs_at[dz], ys[dy]))[(l + k) % 3]
        return u * 4 + v

    def line_at(l, k):
        return (z, y, x)[(l + k) % 3]

    def remote(src, dst, send, recv, device):
        return pltpu.make_async_remote_copy(
            src_ref=src, dst_ref=dst, send_sem=send, recv_sem=recv, device_id=device, device_id_type=MESH
        )

    pending = []

    def drain():
        for done in pending:
            done()

    def all_of(ref, count, send, recv):
        view = ref.at[pl.ds(0, count)]
        return remote(view, view, send, recv, sibling)

    items = []
    for l in range(2):
        items.append((q_hbm.at[l], q.at[l]))
    for l in range(2):
        items.append((a_hbm.at[l], a.at[l]))
        for t in range(512 // TILE):
            items.append((c_hbm.at[l, pl.ds(t * TILE, TILE)], c.at[l, pl.ds(t * TILE, TILE)]))
    loads = [pltpu.make_async_copy(s, d, load_sem.at[i]) for i, (s, d) in enumerate(items)]
    for load in loads[:FLY]:
        load.start()

    barrier = pltpu.get_barrier_semaphore()

    pl.semaphore_signal(barrier, inc=1, device_id=sibling, device_id_type=MESH)
    for offset in PLANE + AXIS:
        pl.semaphore_signal(barrier, inc=1, device_id=device(*offset), device_id_type=MESH)

    def arrive(i):
        loads[i].wait()
        if i + FLY < len(loads):
            loads[i + FLY].start()

    def half_of(h):
        return pl.ds(pl.multiple_of(h * P_HALF, 128), P_HALF)

    def tokens(l, t):
        base = 2 + l * (1 + 512 // TILE)
        if t == 0:
            arrive(base)
        arrive(base + 1 + t)
        w = dot(c[l, t * TILE : (t + 1) * TILE, :], q3t[l], NN)
        wt[:, t * TILE : (t + 1) * TILE] = sum3(w.T) * (1.0 / 32.0)

    def p_part(l, h):
        return sum3(dot(split3(wt[...]), a[l, :, half_of(h)], NN))

    def pair_start(l):
        px[l] = p_part(l, other)
        cp = remote(px.at[l], pxr.at[l], px_sem.at[l], pxr_sem.at[l], sibling)
        cp.start()
        pending.append(cp.wait_send)
        return p_part(l, mine)

    def p_first(l, part):
        remote(px.at[l], pxr.at[l], px_sem.at[l], pxr_sem.at[l], sibling).wait_recv()
        for k in range(P_CHUNKS):
            cols = slice(P_STARTS[k], P_STARTS[k] + P_WIDTHS[k])
            pa[l][k][first] = part[:, cols] + pxr[l, :, cols]
            slot = pa[l][k].at[first]
            for d, _, _ in AXIS:
                remote(slot, slot, psend_sem.at[l, k, 0], pa_sem.at[l, k], along_first(d)).start()
            pending.append(all_of(pa[l][k], 3, psend_sem.at[l, k, 0], pa_sem.at[l, k]).wait_send)

    def p_second(l):
        for k in range(P_CHUNKS):
            src, dst = pa[l][k], pb[l][k]
            all_of(src, 3, psend_sem.at[l, k, 0], pa_sem.at[l, k]).wait_recv()
            dst[second] = src[0] + src[1] + src[2] + src[3]
            slot = dst.at[second]
            for d, _, _ in AXIS:
                remote(slot, slot, psend_sem.at[l, k, 1], pb_sem.at[l, k], along_second(d)).start()
            pending.append(all_of(dst, 3, psend_sem.at[l, k, 1], pb_sem.at[l, k]).wait_send)

    def p_third(l):
        for k in range(P_CHUNKS):
            src = pb[l][k]
            all_of(src, 3, psend_sem.at[l, k, 1], pb_sem.at[l, k]).wait_recv()
            pf[l][k][mine] = src[0] + src[1] + src[2] + src[3]
            slot = pf[l][k].at[mine]
            cp = remote(slot, slot, psend_sem.at[l, k, 2], pfw_sem.at[l, k], sibling)
            cp.start()
            pending.append(cp.wait_send)

    def half_pieces(l, h):
        return split3(jnp.concatenate([pf[l][k][h] for k in range(P_CHUNKS)], axis=1))

    def gram_of(p3):
        g3 = sum3(dot(p3, p3, NT))
        return g3[:, 0:32] + g3[:, 32:64] + g3[:, 64:96]

    def y_pieces(l):
        p_mine = half_pieces(l, mine)
        y = sum3(dot(p_mine, a[l, :, half_of(mine)], NT))
        for k in range(P_CHUNKS):
            slot = pf[l][k].at[other]
            remote(slot, slot, psend_sem.at[l, k, 2], pfw_sem.at[l, k], sibling).wait_recv()
        p_other = half_pieces(l, other)
        y = y + sum3(dot(p_other, a[l, :, half_of(other)], NT))
        return split3(y * (1.0 / 32.0)), p_mine, p_other

    def z_part(l, k, h, y3):
        cols = pl.ds(pl.multiple_of(h * Z_HALF + STARTS[k], 128), WIDTHS[k])
        return sum3(dot(y3, c[l, :, cols], NN))

    def z_scatter(l, y3):
        for k in range(Z_CHUNKS):
            to_pieces(zx[l][k], z_part(l, k, other, y3))
            cp = remote(zx[l][k], zxr[l][k], zx_sem.at[l, k], zxr_sem.at[l, k], sibling)
            cp.start()
            pending.append(cp.wait_send)
        for k in range(Z_CHUNKS):
            to_pieces(zs[l][k], z_part(l, k, mine, y3))
            remote(zx[l][k], zxr[l][k], zx_sem.at[l, k], zxr_sem.at[l, k], sibling).wait_recv()
            zs[l][k][...] += zxr[l][k][...]
            me = seat(l, k, (0, 0, 0))
            for _, du, dv in PLANE:
                offset = spin(l, k, du, dv, 0)
                remote(
                    zs[l][k].at[seat(l, k, offset)], zrr[l][k].at[me],
                    zsend_sem.at[l, k, 0], zrs_sem.at[l, k], device(*offset),
                ).start()
            pending.append(all_of(zs[l][k], 15, zsend_sem.at[l, k, 0], zrs_sem.at[l, k]).wait_send)
            zrr[l][k][me] = zs[l][k][me]

    def z_line(l):
        for k in range(Z_CHUNKS):
            all_of(zrr[l][k], 15, zsend_sem.at[l, k, 0], zrs_sem.at[l, k]).wait_recv()
            w = line_at(l, k)
            zl[l][k][w] = jnp.sum(zrr[l][k][...], axis=0)
            slot = zl[l][k].at[w]
            for dw, _, _ in AXIS:
                remote(
                    slot, slot, zsend_sem.at[l, k, 1], zline_sem.at[l, k], device(*spin(l, k, 0, 0, dw))
                ).start()
            pending.append(all_of(zl[l][k], 3, zsend_sem.at[l, k, 1], zline_sem.at[l, k]).wait_send)

    def z_gather(l):
        for k in range(Z_CHUNKS):
            src = zl[l][k]
            all_of(src, 3, zsend_sem.at[l, k, 1], zline_sem.at[l, k]).wait_recv()
            me = seat(l, k, (0, 0, 0))
            zag[l][k][mine, me] = src[0] + src[1] + src[2] + src[3]
            own = zag[l][k].at[mine, me]
            for _, du, dv in PLANE:
                remote(
                    own, own, zsend_sem.at[l, k, 2], zag_sem.at[l, k, me // 4], device(*spin(l, k, du, dv, 0))
                ).start()
            pending.append(all_of(zag[l][k].at[mine], 15, zsend_sem.at[l, k, 2], zag_sem.at[l, k, 0]).wait_send)

    def z_forward(l):
        for k in range(Z_CHUNKS):
            whole = zag[l][k].at[mine]
            for d in (0, 1, 3, 2):
                u = lax.rem(seat(l, k, (0, 0, 0)) // 4 + d, 4)
                block = zag[l][k].at[mine, pl.ds(u * 4, 3 if d == 0 else 4)]
                remote(block, block, zsend_sem.at[l, k, 3], zag_sem.at[l, k, u], sibling).wait_recv()
                block = zag[l][k].at[mine, pl.ds(u * 4, 4)]
                remote(block, block, zsend_sem.at[l, k, 3], zfw_sem.at[l, k], sibling).start()
            pending.append(remote(whole, whole, zsend_sem.at[l, k, 3], zfw_sem.at[l, k], sibling).wait_send)

    def z_finish(l):
        for k in range(Z_CHUNKS):
            whole = zag[l][k].at[other]
            remote(whole, whole, zsend_sem.at[l, k, 3], zfw_sem.at[l, k], sibling).wait_recv()

    for l in range(2):
        arrive(l)
        q3t[l] = split3(q[l]).T
    for t in range(512 // TILE):
        tokens(0, t)
    pl.semaphore_wait(barrier, 1 + len(PLANE) + len(AXIS))
    for offset in AXIS:
        pl.semaphore_signal(near_sem, inc=1, device_id=device(*offset), device_id_type=MESH)
    part = pair_start(0)
    tokens(1, 0)
    p_first(0, part)
    for t in range(1, 512 // TILE):
        tokens(1, t)
    part = pair_start(1)
    p_first(1, part)
    p_second(0)
    p_second(1)
    pl.semaphore_wait(near_sem, len(AXIS))
    p_third(0)
    y3, p_mine, p_other = y_pieces(0)
    z_scatter(0, y3)
    g_first = gram_of(p_mine) + gram_of(p_other)
    p_third(1)
    y3, p_mine, p_other = y_pieces(1)
    z_scatter(1, y3)
    g_second = gram_of(p_mine) + gram_of(p_other)
    zero = jnp.zeros((32, 32), F32)
    gram[z] = jnp.concatenate([g_first, zero, g_second, zero], axis=1)
    for offset in AXIS:
        remote(gram.at[z], gram.at[z], gsend_sem.at[0], g_sem.at[z], device(*offset)).start()
    pending.append(all_of(gram, 3, gsend_sem.at[0], g_sem.at[0]).wait_send)
    z_line(0)
    z_line(1)
    z_gather(0)
    z_gather(1)
    for offset in AXIS:
        _, from_z = back_from(*offset)
        remote(gram.at[from_z], gram.at[from_z], gsend_sem.at[0], g_sem.at[from_z], sibling).wait_recv()
    inv_ref[...] = eliminate(gram[0] + gram[1] + gram[2] + gram[3], range(32), True)
    z_forward(0)
    z_forward(1)
    z_finish(0)
    z_finish(1)
    drain()


def finish_kernel(*refs, root):
    zags, pfs = refs[: 2 * Z_CHUNKS], refs[2 * Z_CHUNKS : 2 * Z_CHUNKS + 2 * P_CHUNKS]
    inv_ref, p_out, q_out = refs[2 * Z_CHUNKS + 2 * P_CHUNKS :]
    for l in range(2):
        pieces = split3(inv_ref[:, 64 * l + 32 : 64 * l + 64])
        left = jnp.concatenate([pieces, pieces, pieces], axis=1)
        for h in range(2):
            for k in range(P_CHUNKS):
                start = h * P_HALF + P_STARTS[k]
                block = pfs[l * P_CHUNKS + k][h]
                p_out[l, :, start : start + P_WIDTHS[k]] = sum3(dot(left, split3(block), NN)) * root
            for k in range(Z_CHUNKS):
                start = h * Z_HALF + STARTS[k]
                block = from_pieces(zags[l * Z_CHUNKS + k].at[h])
                q_out[l, :, start : start + WIDTHS[k]] = sum3(dot(left, split3(block), NN))


def local(acts, cotangent, q_start):
    width = cotangent.shape[2]
    q_t = jnp.swapaxes(q_start, 1, 2)
    hbm = pl.BlockSpec(memory_space=pltpu.HBM)
    vmem = pl.BlockSpec(memory_space=pltpu.VMEM)
    dma = pltpu.SemaphoreType.DMA
    count = 2 * Z_CHUNKS + 2 * P_CHUNKS + 1

    def chunks(shape_of, widths, times=1):
        return [pltpu.VMEM(shape_of(width), F32) for _ in range(2 * times) for width in widths]

    *gathered, inverse = pl.pallas_call(
        exchange_kernel,
        out_shape=(
            *[jax.ShapeDtypeStruct((2, 16, 8, w // 4), F32) for _ in range(2) for w in WIDTHS],
            *[jax.ShapeDtypeStruct((2, 32, w), F32) for _ in range(2) for w in P_WIDTHS],
            jax.ShapeDtypeStruct((32, 128), F32),
        ),
        in_specs=[hbm] * 3,
        out_specs=(vmem,) * count,
        scratch_shapes=[
            pltpu.VMEM((2, 512, 1280), BF16),
            pltpu.VMEM((2, 512, 5120), BF16),
            pltpu.VMEM((2, 32, 5120), F32),
            pltpu.VMEM((2, 5120, 96), BF16),
            pltpu.VMEM((32, 512), F32),
            pltpu.VMEM((2, 32, P_HALF), F32),
            pltpu.VMEM((2, 32, P_HALF), F32),
            pltpu.VMEM((4, 32, 128), F32),
            *chunks(lambda w: (4, 32, w), P_WIDTHS, 2),
            *chunks(lambda w: (16, 8, w // 4), WIDTHS, 4),
            *chunks(lambda w: (4, 8, w // 4), WIDTHS),
            dma((16,)), dma((2,)), dma((2,)), dma((2, P_CHUNKS, 3)), dma((2, P_CHUNKS)), dma((2, P_CHUNKS)),
            dma((2, P_CHUNKS)), dma((1,)), dma((4,)),
            dma((2, Z_CHUNKS)), dma((2, Z_CHUNKS)), dma((2, Z_CHUNKS, 4)), dma((2, Z_CHUNKS)), dma((2, Z_CHUNKS)),
            dma((2, Z_CHUNKS, 4)), dma((2, Z_CHUNKS)), pltpu.SemaphoreType.REGULAR,
        ],
        name="exchange",
        compiler_params=pltpu.CompilerParams(
            collective_id=0, has_side_effects=True, vmem_limit_bytes=52 * 2**20
        ),
    )(acts, cotangent, q_t)
    p_t, q_new = pl.pallas_call(
        functools.partial(finish_kernel, root=float(width) ** 0.5),
        out_shape=(
            jax.ShapeDtypeStruct((2, 32, 1280), F32),
            jax.ShapeDtypeStruct((2, 32, 5120), F32),
        ),
        in_specs=[vmem] * count,
        out_specs=(vmem, vmem),
        name="finish",
        compiler_params=pltpu.CompilerParams(vmem_limit_bytes=32 * 2**20),
    )(*gathered, inverse)
    return jnp.swapaxes(p_t, 1, 2), jnp.swapaxes(q_new, 1, 2)


def solution(mesh):
    placed = (P(None, "dp", "tensor"), P(None, "dp", None), P())
    return jax.shard_map(
        local, mesh=mesh, in_specs=placed, out_specs=(P(None, "tensor", None), P()), check_vma=False
    )
```

```python
import functools

import jax
import jax.numpy as jnp
from jax import lax
from jax.experimental import pallas as pl
from jax.experimental.pallas import tpu as pltpu
from jax.sharding import PartitionSpec as P

MESH = pl.DeviceIdType.MESH
F32 = jnp.float32
BF16 = jnp.bfloat16
NN = (((1,), (0,)), ((), ()))
NT = (((1,), (1,)), ((), ()))
TILE = 256
FLY = 5
WIDTHS = (1024, 1024, 512)
P_WIDTHS = (384, 256)
STARTS = tuple(sum(WIDTHS[:k]) for k in range(len(WIDTHS)))
P_STARTS = tuple(sum(P_WIDTHS[:k]) for k in range(len(P_WIDTHS)))
Z_CHUNKS, P_CHUNKS = len(WIDTHS), len(P_WIDTHS)
Z_HALF, P_HALF = sum(WIDTHS), sum(P_WIDTHS)


def hops(offset):
    return sum(min(d, 4 - d) for d in offset)


OFFSETS = [(dz, dy, dx) for dz in range(4) for dy in range(4) for dx in range(4)]
CUBE = sorted([o for o in OFFSETS if hops(o) > 0], key=hops, reverse=True)
PLANE = [o for o in CUBE if o[0] == 0]
AXIS = [o for o in CUBE if o[1] == 0 and o[2] == 0]
FLY = 5


def dot(a, b, dims):
    return lax.dot_general(a, b, dims, preferred_element_type=F32)


def split3(x):
    hi = x.astype(BF16)
    rest = x - hi.astype(F32)
    mid = rest.astype(BF16)
    low = (rest - mid.astype(F32)).astype(BF16)
    return jnp.concatenate([hi, mid, low], axis=0)


def sum3(x):
    return x[0:32] + x[32:64] + x[64:96]


def to_pieces(ref, value):
    quarter = value.shape[1] // 4
    for j in range(16):
        g, h = j // 4, j % 4
        ref[j] = value[8 * g : 8 * g + 8, quarter * h : quarter * h + quarter]


def from_pieces(ref):
    bands = []
    for g in range(4):
        bands.append(jnp.concatenate([ref[4 * g + h] for h in range(4)], axis=1))
    return jnp.concatenate(bands, axis=0)


def eliminate(work, steps, start=False):
    rows = lax.broadcasted_iota(jnp.int32, (32, 128), 0)
    lanes = lax.broadcasted_iota(jnp.int32, (32, 128), 1)
    if start:
        eye = jnp.where(rows == lanes % 32, 1.0, 0.0).astype(F32)
        work = jnp.where((lanes // 32) % 2 == 1, eye, work)
    first = lanes < 64
    for k in steps:
        row = work[k : k + 1, :]
        pivot = jnp.where(first[0:1], row[:, k : k + 1], row[:, 64 + k : 65 + k])
        scale = lax.rsqrt(pivot)
        scale = scale * (1.5 - 0.5 * pivot * scale * scale)
        column = jnp.where(first, work[:, k : k + 1], work[:, 64 + k : 65 + k])
        row = row * scale
        work = jnp.where(rows > k, work - (column * scale) * row, jnp.where(rows == k, row, work))
    return work


def factor(inv_ref, l):
    pieces = split3(inv_ref[:, 64 * l + 32 : 64 * l + 64])
    return jnp.concatenate([pieces, pieces, pieces], axis=1)


def exchange_kernel(a_hbm, c_hbm, q_hbm, *refs, root):
    left = list(refs)

    def take(count):
        taken = left[:count]
        del left[:count]
        return taken

    q_done, p_done = take(2)
    late = take(Z_CHUNKS)
    (inv_ref,) = take(1)
    zag, pf = [take(Z_CHUNKS), late], [take(P_CHUNKS) for _ in range(2)]
    a, c, q, q3t, wt, px, pxr, gram = take(8)
    pa, pb = ([take(P_CHUNKS) for _ in range(2)] for _ in range(2))
    zx, zxr, zs, zrr, zl = ([take(Z_CHUNKS) for _ in range(2)] for _ in range(5))
    load_sem, px_sem, pxr_sem, psend_sem, pa_sem, pb_sem, pfw_sem, gsend_sem, g_sem = take(9)
    zx_sem, zxr_sem, zsend_sem, zrs_sem, zline_sem, zag_sem, zfw_sem, near_sem = take(8)
    dp = lax.axis_index("dp")
    z = lax.axis_index("tensor")
    core = lax.rem(dp, 2)
    plane = dp // 2
    y, x = plane // 4, lax.rem(plane, 4)
    mine, other = core, 1 - core
    sibling = {"dp": plane * 2 + other, "tensor": z}

    ys = [lax.rem(y + d, 4) for d in range(4)]
    xs = [lax.rem(x + d, 4) for d in range(4)]
    zs_at = [lax.rem(z + d, 4) for d in range(4)]

    def place(dz, dy, dx):
        return ys[dy] * 4 + xs[dx], zs_at[dz]

    def device(dz, dy, dx):
        to_plane, to_z = place(dz, dy, dx)
        return {"dp": to_plane * 2 + core, "tensor": to_z}

    def back_from(dz, dy, dx):
        return place((4 - dz) % 4, (4 - dy) % 4, (4 - dx) % 4)

    first, second = jnp.where(core == 0, x, y), jnp.where(core == 0, y, x)

    def along_first(d):
        row, column = jnp.where(core == 0, y, ys[d]), jnp.where(core == 0, xs[d], x)
        return {"dp": (row * 4 + column) * 2 + core, "tensor": z}

    def along_second(d):
        row, column = jnp.where(core == 0, ys[d], y), jnp.where(core == 0, x, xs[d])
        return {"dp": (row * 4 + column) * 2 + core, "tensor": z}

    def spin(l, k, du, dv, dw):
        return ((dw, du, dv), (dv, dw, du), (du, dv, dw))[(l + k) % 3]

    def seat(l, k, offset):
        dz, dy, dx = offset
        u, v = ((ys[dy], xs[dx]), (xs[dx], zs_at[dz]), (zs_at[dz], ys[dy]))[(l + k) % 3]
        return u * 4 + v

    def line_at(l, k):
        return (z, y, x)[(l + k) % 3]

    def remote(src, dst, send, recv, device):
        return pltpu.make_async_remote_copy(
            src_ref=src, dst_ref=dst, send_sem=send, recv_sem=recv, device_id=device, device_id_type=MESH
        )

    pending = []

    def drain():
        for done in pending:
            done()

    def all_of(ref, count, send, recv):
        view = ref.at[pl.ds(0, count)]
        return remote(view, view, send, recv, sibling)

    items = []
    for l in range(2):
        items.append((q_hbm.at[l], q.at[l]))
    for l in range(2):
        items.append((a_hbm.at[l], a.at[l]))
        for t in range(512 // TILE):
            items.append((c_hbm.at[l, pl.ds(t * TILE, TILE)], c.at[l, pl.ds(t * TILE, TILE)]))
    loads = [pltpu.make_async_copy(s, d, load_sem.at[i]) for i, (s, d) in enumerate(items)]
    for load in loads[:FLY]:
        load.start()

    barrier = pltpu.get_barrier_semaphore()

    pl.semaphore_signal(barrier, inc=1, device_id=sibling, device_id_type=MESH)
    for offset in PLANE + AXIS:
        pl.semaphore_signal(barrier, inc=1, device_id=device(*offset), device_id_type=MESH)

    def arrive(i):
        loads[i].wait()
        if i + FLY < len(loads):
            loads[i + FLY].start()

    def half_of(h):
        return pl.ds(pl.multiple_of(h * P_HALF, 128), P_HALF)

    def tokens(l, t):
        base = 2 + l * (1 + 512 // TILE)
        if t == 0:
            arrive(base)
        arrive(base + 1 + t)
        w = dot(c[l, t * TILE : (t + 1) * TILE, :], q3t[l], NN)
        wt[:, t * TILE : (t + 1) * TILE] = sum3(w.T) * (1.0 / 32.0)

    def p_part(l, h):
        return sum3(dot(split3(wt[...]), a[l, :, half_of(h)], NN))

    def pair_start(l):
        px[l] = p_part(l, other)
        cp = remote(px.at[l], pxr.at[l], px_sem.at[l], pxr_sem.at[l], sibling)
        cp.start()
        pending.append(cp.wait_send)
        return p_part(l, mine)

    def p_first(l, part):
        remote(px.at[l], pxr.at[l], px_sem.at[l], pxr_sem.at[l], sibling).wait_recv()
        for k in range(P_CHUNKS):
            cols = slice(P_STARTS[k], P_STARTS[k] + P_WIDTHS[k])
            pa[l][k][first] = part[:, cols] + pxr[l, :, cols]
            slot = pa[l][k].at[first]
            for d, _, _ in AXIS:
                remote(slot, slot, psend_sem.at[l, k, 0], pa_sem.at[l, k], along_first(d)).start()
            pending.append(all_of(pa[l][k], 3, psend_sem.at[l, k, 0], pa_sem.at[l, k]).wait_send)

    def p_second(l):
        for k in range(P_CHUNKS):
            src, dst = pa[l][k], pb[l][k]
            all_of(src, 3, psend_sem.at[l, k, 0], pa_sem.at[l, k]).wait_recv()
            dst[second] = src[0] + src[1] + src[2] + src[3]
            slot = dst.at[second]
            for d, _, _ in AXIS:
                remote(slot, slot, psend_sem.at[l, k, 1], pb_sem.at[l, k], along_second(d)).start()
            pending.append(all_of(dst, 3, psend_sem.at[l, k, 1], pb_sem.at[l, k]).wait_send)

    def p_third(l):
        for k in range(P_CHUNKS):
            src = pb[l][k]
            all_of(src, 3, psend_sem.at[l, k, 1], pb_sem.at[l, k]).wait_recv()
            pf[l][k][mine] = src[0] + src[1] + src[2] + src[3]
            slot = pf[l][k].at[mine]
            cp = remote(slot, slot, psend_sem.at[l, k, 2], pfw_sem.at[l, k], sibling)
            cp.start()
            pending.append(cp.wait_send)

    def half_pieces(l, h):
        return split3(jnp.concatenate([pf[l][k][h] for k in range(P_CHUNKS)], axis=1))

    def gram_of(p3):
        g3 = sum3(dot(p3, p3, NT))
        return g3[:, 0:32] + g3[:, 32:64] + g3[:, 64:96]

    def y_pieces(l):
        p_mine = half_pieces(l, mine)
        y = sum3(dot(p_mine, a[l, :, half_of(mine)], NT))
        for k in range(P_CHUNKS):
            slot = pf[l][k].at[other]
            remote(slot, slot, psend_sem.at[l, k, 2], pfw_sem.at[l, k], sibling).wait_recv()
        p_other = half_pieces(l, other)
        y = y + sum3(dot(p_other, a[l, :, half_of(other)], NT))
        return split3(y * (1.0 / 32.0)), p_mine, p_other

    def z_part(l, k, h, y3):
        cols = pl.ds(pl.multiple_of(h * Z_HALF + STARTS[k], 128), WIDTHS[k])
        return sum3(dot(y3, c[l, :, cols], NN))

    def z_scatter(l, y3):
        for k in range(Z_CHUNKS):
            to_pieces(zx[l][k], z_part(l, k, other, y3))
            cp = remote(zx[l][k], zxr[l][k], zx_sem.at[l, k], zxr_sem.at[l, k], sibling)
            cp.start()
            pending.append(cp.wait_send)
        for k in range(Z_CHUNKS):
            to_pieces(zs[l][k], z_part(l, k, mine, y3))
            remote(zx[l][k], zxr[l][k], zx_sem.at[l, k], zxr_sem.at[l, k], sibling).wait_recv()
            zs[l][k][...] += zxr[l][k][...]
            me = seat(l, k, (0, 0, 0))
            for _, du, dv in PLANE:
                offset = spin(l, k, du, dv, 0)
                remote(
                    zs[l][k].at[seat(l, k, offset)], zrr[l][k].at[me],
                    zsend_sem.at[l, k, 0], zrs_sem.at[l, k], device(*offset),
                ).start()
            pending.append(all_of(zs[l][k], 15, zsend_sem.at[l, k, 0], zrs_sem.at[l, k]).wait_send)
            zrr[l][k][me] = zs[l][k][me]

    def z_line(l):
        for k in range(Z_CHUNKS):
            all_of(zrr[l][k], 15, zsend_sem.at[l, k, 0], zrs_sem.at[l, k]).wait_recv()
            w = line_at(l, k)
            zl[l][k][w] = jnp.sum(zrr[l][k][...], axis=0)
            slot = zl[l][k].at[w]
            for dw, _, _ in AXIS:
                remote(
                    slot, slot, zsend_sem.at[l, k, 1], zline_sem.at[l, k], device(*spin(l, k, 0, 0, dw))
                ).start()
            pending.append(all_of(zl[l][k], 3, zsend_sem.at[l, k, 1], zline_sem.at[l, k]).wait_send)

    def z_gather(l):
        for k in range(Z_CHUNKS):
            src = zl[l][k]
            all_of(src, 3, zsend_sem.at[l, k, 1], zline_sem.at[l, k]).wait_recv()
            me = seat(l, k, (0, 0, 0))
            zag[l][k][mine, me] = src[0] + src[1] + src[2] + src[3]
            own = zag[l][k].at[mine, me]
            for _, du, dv in PLANE:
                remote(
                    own, own, zsend_sem.at[l, k, 2], zag_sem.at[l, k, me // 4], device(*spin(l, k, du, dv, 0))
                ).start()
            pending.append(all_of(zag[l][k].at[mine], 15, zsend_sem.at[l, k, 2], zag_sem.at[l, k, 0]).wait_send)

    def z_forward(l):
        for k in range(Z_CHUNKS):
            whole = zag[l][k].at[mine]
            for d in (0, 1, 3, 2):
                u = lax.rem(seat(l, k, (0, 0, 0)) // 4 + d, 4)
                block = zag[l][k].at[mine, pl.ds(u * 4, 3 if d == 0 else 4)]
                remote(block, block, zsend_sem.at[l, k, 3], zag_sem.at[l, k, u], sibling).wait_recv()
                block = zag[l][k].at[mine, pl.ds(u * 4, 4)]
                remote(block, block, zsend_sem.at[l, k, 3], zfw_sem.at[l, k], sibling).start()
            pending.append(remote(whole, whole, zsend_sem.at[l, k, 3], zfw_sem.at[l, k], sibling).wait_send)

    def z_finish(l):
        for k in range(Z_CHUNKS):
            whole = zag[l][k].at[other]
            remote(whole, whole, zsend_sem.at[l, k, 3], zfw_sem.at[l, k], sibling).wait_recv()

    for l in range(2):
        arrive(l)
        q3t[l] = split3(q[l]).T
    for t in range(512 // TILE):
        tokens(0, t)
    pl.semaphore_wait(barrier, 1 + len(PLANE) + len(AXIS))
    for offset in AXIS:
        pl.semaphore_signal(near_sem, inc=1, device_id=device(*offset), device_id_type=MESH)
    part = pair_start(0)
    tokens(1, 0)
    p_first(0, part)
    for t in range(1, 512 // TILE):
        tokens(1, t)
    part = pair_start(1)
    p_first(1, part)
    p_second(0)
    p_second(1)
    pl.semaphore_wait(near_sem, len(AXIS))
    p_third(0)
    y3, p_mine, p_other = y_pieces(0)
    z_scatter(0, y3)
    g_first = gram_of(p_mine) + gram_of(p_other)
    p_third(1)
    y3, p_mine, p_other = y_pieces(1)
    z_scatter(1, y3)
    g_second = gram_of(p_mine) + gram_of(p_other)
    zero = jnp.zeros((32, 32), F32)
    gram[z] = jnp.concatenate([g_first, zero, g_second, zero], axis=1)
    for offset in AXIS:
        remote(gram.at[z], gram.at[z], gsend_sem.at[0], g_sem.at[z], device(*offset)).start()
    pending.append(all_of(gram, 3, gsend_sem.at[0], g_sem.at[0]).wait_send)
    z_line(0)
    z_line(1)
    z_gather(0)
    z_gather(1)
    for offset in AXIS:
        _, from_z = back_from(*offset)
        remote(gram.at[from_z], gram.at[from_z], gsend_sem.at[0], g_sem.at[from_z], sibling).wait_recv()
    inv_ref[...] = eliminate(gram[0] + gram[1] + gram[2] + gram[3], range(32), True)
    inverse = [factor(inv_ref, l) for l in range(2)]

    def q_half(l, h):
        for k in range(Z_CHUNKS):
            cols = pl.ds(pl.multiple_of(h * Z_HALF + STARTS[k], 128), WIDTHS[k])
            q_done[l, :, cols] = sum3(dot(inverse[l], split3(from_pieces(zag[l][k].at[h])), NN))

    for l in range(2):
        for h in range(2):
            for k in range(P_CHUNKS):
                start = h * P_HALF + P_STARTS[k]
                p_done[l, :, start : start + P_WIDTHS[k]] = sum3(dot(inverse[l], split3(pf[l][k][h]), NN)) * root
    z_forward(0)
    q_half(0, mine)
    z_finish(0)
    q_half(0, other)
    z_forward(1)
    q_half(1, mine)
    z_finish(1)
    drain()


def finish_kernel(q_done, p_done, *refs):
    late, (inv_ref, p_out, q_out, last, sem) = refs[:Z_CHUNKS], refs[Z_CHUNKS:]
    mine = lax.rem(lax.axis_index("dp"), 2)
    other = 1 - mine
    own = pl.ds(pl.multiple_of(mine * Z_HALF, 128), Z_HALF)
    rest = pl.ds(pl.multiple_of(other * Z_HALF, 128), Z_HALF)
    copies = [
        pltpu.make_async_copy(q_done.at[0], q_out.at[0], sem.at[0]),
        pltpu.make_async_copy(q_done.at[1, :, own], q_out.at[1, :, own], sem.at[1]),
        pltpu.make_async_copy(p_done, p_out, sem.at[2]),
    ]
    for cp in copies:
        cp.start()
    inverse = factor(inv_ref, 1)
    for k in range(Z_CHUNKS):
        block = from_pieces(late[k].at[other])
        last[:, STARTS[k] : STARTS[k] + WIDTHS[k]] = sum3(dot(inverse, split3(block), NN))
    copies.append(pltpu.make_async_copy(last, q_out.at[1, :, rest], sem.at[3]))
    copies[3].start()
    for cp in copies:
        cp.wait()


def local(acts, cotangent, q_start):
    width = cotangent.shape[2]
    q_t = jnp.swapaxes(q_start, 1, 2)
    hbm = pl.BlockSpec(memory_space=pltpu.HBM)
    vmem = pl.BlockSpec(memory_space=pltpu.VMEM)
    dma = pltpu.SemaphoreType.DMA
    count = Z_CHUNKS + 3

    def chunks(shape_of, widths, times=1):
        return [pltpu.VMEM(shape_of(width), F32) for _ in range(2 * times) for width in widths]

    finished = pl.pallas_call(
        functools.partial(exchange_kernel, root=float(width) ** 0.5),
        out_shape=(
            jax.ShapeDtypeStruct((2, 32, 2 * Z_HALF), F32),
            jax.ShapeDtypeStruct((2, 32, 2 * P_HALF), F32),
            *[jax.ShapeDtypeStruct((2, 16, 8, w // 4), F32) for w in WIDTHS],
            jax.ShapeDtypeStruct((32, 128), F32),
        ),
        in_specs=[hbm] * 3,
        out_specs=(vmem,) * count,
        scratch_shapes=[
            *[pltpu.VMEM((2, 16, 8, w // 4), F32) for w in WIDTHS],
            *chunks(lambda w: (2, 32, w), P_WIDTHS),
            pltpu.VMEM((2, 512, 1280), BF16),
            pltpu.VMEM((2, 512, 5120), BF16),
            pltpu.VMEM((2, 32, 5120), F32),
            pltpu.VMEM((2, 5120, 96), BF16),
            pltpu.VMEM((32, 512), F32),
            pltpu.VMEM((2, 32, P_HALF), F32),
            pltpu.VMEM((2, 32, P_HALF), F32),
            pltpu.VMEM((4, 32, 128), F32),
            *chunks(lambda w: (4, 32, w), P_WIDTHS, 2),
            *chunks(lambda w: (16, 8, w // 4), WIDTHS, 4),
            *chunks(lambda w: (4, 8, w // 4), WIDTHS),
            dma((16,)), dma((2,)), dma((2,)), dma((2, P_CHUNKS, 3)), dma((2, P_CHUNKS)), dma((2, P_CHUNKS)),
            dma((2, P_CHUNKS)), dma((1,)), dma((4,)),
            dma((2, Z_CHUNKS)), dma((2, Z_CHUNKS)), dma((2, Z_CHUNKS, 4)), dma((2, Z_CHUNKS)), dma((2, Z_CHUNKS)),
            dma((2, Z_CHUNKS, 4)), dma((2, Z_CHUNKS)), pltpu.SemaphoreType.REGULAR,
        ],
        name="exchange",
        compiler_params=pltpu.CompilerParams(
            collective_id=0, has_side_effects=True, vmem_limit_bytes=51 * 2**20
        ),
    )(acts, cotangent, q_t)
    p_t, q_new = pl.pallas_call(
        finish_kernel,
        out_shape=(
            jax.ShapeDtypeStruct((2, 32, 2 * P_HALF), F32),
            jax.ShapeDtypeStruct((2, 32, 2 * Z_HALF), F32),
        ),
        in_specs=[vmem] * count,
        out_specs=(hbm, hbm),
        scratch_shapes=[pltpu.VMEM((32, Z_HALF), F32), dma((4,))],
        name="finish",
        compiler_params=pltpu.CompilerParams(vmem_limit_bytes=32 * 2**20),
    )(*finished)
    return jnp.swapaxes(p_t, 1, 2), jnp.swapaxes(q_new, 1, 2)


def solution(mesh):
    placed = (P(None, "dp", "tensor"), P(None, "dp", None), P())
    return jax.shard_map(
        local, mesh=mesh, in_specs=placed, out_specs=(P(None, "tensor", None), P()), check_vma=False
    )
```

```python
import functools

import jax
import jax.numpy as jnp
from jax import lax
from jax.experimental import pallas as pl
from jax.experimental.pallas import tpu as pltpu
from jax.sharding import PartitionSpec as P

MESH = pl.DeviceIdType.MESH
F32 = jnp.float32
BF16 = jnp.bfloat16
NN = (((1,), (0,)), ((), ()))
NT = (((1,), (1,)), ((), ()))
TILE = 256
FLY = 5
WIDTHS = (1024, 1024, 512)
P_WIDTHS = (384, 256)
STARTS = tuple(sum(WIDTHS[:k]) for k in range(len(WIDTHS)))
P_STARTS = tuple(sum(P_WIDTHS[:k]) for k in range(len(P_WIDTHS)))
Z_CHUNKS, P_CHUNKS = len(WIDTHS), len(P_WIDTHS)
TURN = 1
Z_HALF, P_HALF = sum(WIDTHS), sum(P_WIDTHS)


def hops(offset):
    return sum(min(d, 4 - d) for d in offset)


OFFSETS = [(dz, dy, dx) for dz in range(4) for dy in range(4) for dx in range(4)]
CUBE = sorted([o for o in OFFSETS if hops(o) > 0], key=hops, reverse=True)
PLANE = [o for o in CUBE if o[0] == 0]
AXIS = [o for o in CUBE if o[1] == 0 and o[2] == 0]


def dot(a, b, dims):
    return lax.dot_general(a, b, dims, preferred_element_type=F32)


def split3(x):
    hi = x.astype(BF16)
    rest = x - hi.astype(F32)
    mid = rest.astype(BF16)
    low = (rest - mid.astype(F32)).astype(BF16)
    return jnp.concatenate([hi, mid, low], axis=0)


def sum3(x):
    return x[0:32] + x[32:64] + x[64:96]


def to_pieces(ref, value):
    quarter = value.shape[1] // 4
    for j in range(16):
        g, h = j // 4, j % 4
        ref[j] = value[8 * g : 8 * g + 8, quarter * h : quarter * h + quarter]


def from_pieces(ref):
    bands = []
    for g in range(4):
        bands.append(jnp.concatenate([ref[4 * g + h] for h in range(4)], axis=1))
    return jnp.concatenate(bands, axis=0)


def eliminate(work, steps, start=False):
    rows = lax.broadcasted_iota(jnp.int32, (32, 128), 0)
    lanes = lax.broadcasted_iota(jnp.int32, (32, 128), 1)
    if start:
        eye = jnp.where(rows == lanes % 32, 1.0, 0.0).astype(F32)
        work = jnp.where((lanes // 32) % 2 == 1, eye, work)
    first = lanes < 64
    for k in steps:
        row = work[k : k + 1, :]
        pivot = jnp.where(first[0:1], row[:, k : k + 1], row[:, 64 + k : 65 + k])
        scale = lax.rsqrt(pivot)
        scale = scale * (1.5 - 0.5 * pivot * scale * scale)
        column = jnp.where(first, work[:, k : k + 1], work[:, 64 + k : 65 + k])
        row = row * scale
        work = jnp.where(rows > k, work - (column * scale) * row, jnp.where(rows == k, row, work))
    return work


def factor(inv_ref, l):
    pieces = split3(inv_ref[:, 64 * l + 32 : 64 * l + 64])
    return jnp.concatenate([pieces, pieces, pieces], axis=1)


def exchange_kernel(a_hbm, c_hbm, q_hbm, *refs, root):
    left = list(refs)

    def take(count):
        taken = left[:count]
        del left[:count]
        return taken

    q_done, p_done = take(2)
    late = take(Z_CHUNKS)
    (inv_ref,) = take(1)
    zag, pf = [take(Z_CHUNKS), late], [take(P_CHUNKS) for _ in range(2)]
    a, c, q, q3t, wt, px, pxr, gram = take(8)
    pa, pb = ([take(P_CHUNKS) for _ in range(2)] for _ in range(2))
    zx, zxr, zs, zrr, zl = ([take(Z_CHUNKS) for _ in range(2)] for _ in range(5))
    load_sem, px_sem, pxr_sem, psend_sem, pa_sem, pb_sem, pfw_sem, gsend_sem, g_sem = take(9)
    zx_sem, zxr_sem, zsend_sem, zrs_sem, zline_sem, zag_sem, zfw_sem, near_sem = take(8)
    dp = lax.axis_index("dp")
    z = lax.axis_index("tensor")
    core = lax.rem(dp, 2)
    plane = dp // 2
    y, x = plane // 4, lax.rem(plane, 4)
    mine, other = core, 1 - core
    sibling = {"dp": plane * 2 + other, "tensor": z}

    ys = [lax.rem(y + d, 4) for d in range(4)]
    xs = [lax.rem(x + d, 4) for d in range(4)]
    zs_at = [lax.rem(z + d, 4) for d in range(4)]

    def place(dz, dy, dx):
        return ys[dy] * 4 + xs[dx], zs_at[dz]

    def device(dz, dy, dx):
        to_plane, to_z = place(dz, dy, dx)
        return {"dp": to_plane * 2 + core, "tensor": to_z}

    def back_from(dz, dy, dx):
        return place((4 - dz) % 4, (4 - dy) % 4, (4 - dx) % 4)

    first, second = jnp.where(core == 0, x, y), jnp.where(core == 0, y, x)

    def along_first(d):
        row, column = jnp.where(core == 0, y, ys[d]), jnp.where(core == 0, xs[d], x)
        return {"dp": (row * 4 + column) * 2 + core, "tensor": z}

    def along_second(d):
        row, column = jnp.where(core == 0, ys[d], y), jnp.where(core == 0, x, xs[d])
        return {"dp": (row * 4 + column) * 2 + core, "tensor": z}

    def pick(zero, one):
        return jnp.where(core == 0, zero, one)

    def turns(l, k):
        return (l + k) % 3, (l + k + TURN) % 3

    def spun(turn, du, dv, dw):
        dz, dy, dx = ((dw, du, dv), (dv, dw, du), (du, dv, dw))[turn]
        return ys[dy], xs[dx], zs_at[dz]

    def spin(l, k, du, dv, dw):
        to_y, to_x, to_z = (pick(p, q) for p, q in zip(*(spun(t, du, dv, dw) for t in turns(l, k))))
        return {"dp": (to_y * 4 + to_x) * 2 + core, "tensor": to_z}

    def seat(l, k, du, dv):
        seats = []
        for t in turns(l, k):
            to_y, to_x, to_z = spun(t, du, dv, 0)
            u, v = ((to_y, to_x), (to_x, to_z), (to_z, to_y))[t]
            seats.append(u * 4 + v)
        return pick(*seats)

    def line_at(l, k):
        return pick(*((z, y, x)[t] for t in turns(l, k)))

    def remote(src, dst, send, recv, device):
        return pltpu.make_async_remote_copy(
            src_ref=src, dst_ref=dst, send_sem=send, recv_sem=recv, device_id=device, device_id_type=MESH
        )

    pending = []

    def drain():
        while pending:
            pending.pop(0)()

    def all_of(ref, count, send, recv):
        view = ref.at[pl.ds(0, count)]
        return remote(view, view, send, recv, sibling)

    items = []
    for l in range(2):
        items.append((q_hbm.at[l], q.at[l]))
    for l in range(2):
        items.append((a_hbm.at[l], a.at[l]))
        for t in range(512 // TILE):
            items.append((c_hbm.at[l, pl.ds(t * TILE, TILE)], c.at[l, pl.ds(t * TILE, TILE)]))
    loads = [pltpu.make_async_copy(s, d, load_sem.at[i]) for i, (s, d) in enumerate(items)]
    for load in loads[:FLY]:
        load.start()

    barrier = pltpu.get_barrier_semaphore()

    pl.semaphore_signal(barrier, inc=1, device_id=sibling, device_id_type=MESH)
    for offset in PLANE + AXIS:
        pl.semaphore_signal(barrier, inc=1, device_id=device(*offset), device_id_type=MESH)

    def arrive(i):
        loads[i].wait()
        if i + FLY < len(loads):
            loads[i + FLY].start()

    def half_of(h):
        return pl.ds(pl.multiple_of(h * P_HALF, 128), P_HALF)

    def tokens(l, t):
        base = 2 + l * (1 + 512 // TILE)
        if t == 0:
            arrive(base)
        arrive(base + 1 + t)
        w = dot(c[l, t * TILE : (t + 1) * TILE, :], q3t[l], NN)
        wt[:, t * TILE : (t + 1) * TILE] = sum3(w.T) * (1.0 / 32.0)

    def p_part(l, h):
        return sum3(dot(split3(wt[...]), a[l, :, half_of(h)], NN))

    def pair_start(l):
        px[l] = p_part(l, other)
        cp = remote(px.at[l], pxr.at[l], px_sem.at[l], pxr_sem.at[l], sibling)
        cp.start()
        pending.append(cp.wait_send)
        return p_part(l, mine)

    def p_first(l, part):
        remote(px.at[l], pxr.at[l], px_sem.at[l], pxr_sem.at[l], sibling).wait_recv()
        for k in range(P_CHUNKS):
            cols = slice(P_STARTS[k], P_STARTS[k] + P_WIDTHS[k])
            pa[l][k][first] = part[:, cols] + pxr[l, :, cols]
            slot = pa[l][k].at[first]
            for d, _, _ in AXIS:
                remote(slot, slot, psend_sem.at[l, k, 0], pa_sem.at[l, k], along_first(d)).start()
            pending.append(all_of(pa[l][k], 3, psend_sem.at[l, k, 0], pa_sem.at[l, k]).wait_send)

    def p_second(l):
        for k in range(P_CHUNKS):
            src, dst = pa[l][k], pb[l][k]
            all_of(src, 3, psend_sem.at[l, k, 0], pa_sem.at[l, k]).wait_recv()
            dst[second] = src[0] + src[1] + src[2] + src[3]
            slot = dst.at[second]
            for d, _, _ in AXIS:
                remote(slot, slot, psend_sem.at[l, k, 1], pb_sem.at[l, k], along_second(d)).start()
            pending.append(all_of(dst, 3, psend_sem.at[l, k, 1], pb_sem.at[l, k]).wait_send)

    def p_third(l):
        for k in range(P_CHUNKS):
            src = pb[l][k]
            all_of(src, 3, psend_sem.at[l, k, 1], pb_sem.at[l, k]).wait_recv()
            pf[l][k][mine] = src[0] + src[1] + src[2] + src[3]
            slot = pf[l][k].at[mine]
            cp = remote(slot, slot, psend_sem.at[l, k, 2], pfw_sem.at[l, k], sibling)
            cp.start()
            pending.append(cp.wait_send)

    def half_pieces(l, h):
        return split3(jnp.concatenate([pf[l][k][h] for k in range(P_CHUNKS)], axis=1))

    def gram_of(p3):
        g3 = sum3(dot(p3, p3, NT))
        return g3[:, 0:32] + g3[:, 32:64] + g3[:, 64:96]

    def y_pieces(l):
        p_mine = half_pieces(l, mine)
        y = sum3(dot(p_mine, a[l, :, half_of(mine)], NT))
        for k in range(P_CHUNKS):
            slot = pf[l][k].at[other]
            remote(slot, slot, psend_sem.at[l, k, 2], pfw_sem.at[l, k], sibling).wait_recv()
        p_other = half_pieces(l, other)
        y = y + sum3(dot(p_other, a[l, :, half_of(other)], NT))
        return split3(y * (1.0 / 32.0)), p_mine, p_other

    def z_part(l, k, h, y3):
        cols = pl.ds(pl.multiple_of(h * Z_HALF + STARTS[k], 128), WIDTHS[k])
        return sum3(dot(y3, c[l, :, cols], NN))

    def z_pair(l, y3):
        for k in range(Z_CHUNKS):
            to_pieces(zx[l][k], z_part(l, k, other, y3))
            cp = remote(zx[l][k], zxr[l][k], zx_sem.at[l, k], zxr_sem.at[l, k], sibling)
            cp.start()
            pending.append(cp.wait_send)
        for k in range(Z_CHUNKS):
            to_pieces(zs[l][k], z_part(l, k, mine, y3))

    def z_scatter(l):
        for k in range(Z_CHUNKS):
            remote(zx[l][k], zxr[l][k], zx_sem.at[l, k], zxr_sem.at[l, k], sibling).wait_recv()
            zs[l][k][...] += zxr[l][k][...]
            me = seat(l, k, 0, 0)
            for _, du, dv in PLANE:
                remote(
                    zs[l][k].at[seat(l, k, du, dv)], zrr[l][k].at[me],
                    zsend_sem.at[l, k, 0], zrs_sem.at[l, k], spin(l, k, du, dv, 0),
                ).start()
            pending.append(all_of(zs[l][k], 15, zsend_sem.at[l, k, 0], zrs_sem.at[l, k]).wait_send)
            zrr[l][k][me] = zs[l][k][me]

    def z_line(l):
        for k in range(Z_CHUNKS):
            all_of(zrr[l][k], 15, zsend_sem.at[l, k, 0], zrs_sem.at[l, k]).wait_recv()
            w = line_at(l, k)
            zl[l][k][w] = jnp.sum(zrr[l][k][...], axis=0)
            slot = zl[l][k].at[w]
            for dw, _, _ in AXIS:
                remote(
                    slot, slot, zsend_sem.at[l, k, 1], zline_sem.at[l, k], spin(l, k, 0, 0, dw)
                ).start()
            pending.append(all_of(zl[l][k], 3, zsend_sem.at[l, k, 1], zline_sem.at[l, k]).wait_send)

    def z_gather(l):
        for k in range(Z_CHUNKS):
            src = zl[l][k]
            all_of(src, 3, zsend_sem.at[l, k, 1], zline_sem.at[l, k]).wait_recv()
            me = seat(l, k, 0, 0)
            zag[l][k][mine, me] = src[0] + src[1] + src[2] + src[3]
            own = zag[l][k].at[mine, me]
            for _, du, dv in PLANE:
                remote(
                    own, own, zsend_sem.at[l, k, 2], zag_sem.at[l, k, me // 4], spin(l, k, du, dv, 0)
                ).start()
            pending.append(all_of(zag[l][k].at[mine], 15, zsend_sem.at[l, k, 2], zag_sem.at[l, k, 0]).wait_send)

    def z_forward(l):
        for k in range(Z_CHUNKS):
            whole = zag[l][k].at[mine]
            for d in (0, 1, 3, 2):
                u = lax.rem(seat(l, k, 0, 0) // 4 + d, 4)
                block = zag[l][k].at[mine, pl.ds(u * 4, 3 if d == 0 else 4)]
                remote(block, block, zsend_sem.at[l, k, 3], zag_sem.at[l, k, u], sibling).wait_recv()
                block = zag[l][k].at[mine, pl.ds(u * 4, 4)]
                remote(block, block, zsend_sem.at[l, k, 3], zfw_sem.at[l, k], sibling).start()
            pending.append(remote(whole, whole, zsend_sem.at[l, k, 3], zfw_sem.at[l, k], sibling).wait_send)

    def z_finish(l):
        for k in range(Z_CHUNKS):
            whole = zag[l][k].at[other]
            remote(whole, whole, zsend_sem.at[l, k, 3], zfw_sem.at[l, k], sibling).wait_recv()

    for l in range(2):
        arrive(l)
        q3t[l] = split3(q[l]).T
    for t in range(512 // TILE):
        tokens(0, t)
    pl.semaphore_wait(barrier, 1 + len(PLANE) + len(AXIS))
    for offset in AXIS:
        pl.semaphore_signal(near_sem, inc=1, device_id=device(*offset), device_id_type=MESH)
    part = pair_start(0)
    tokens(1, 0)
    p_first(0, part)
    for t in range(1, 512 // TILE):
        tokens(1, t)
    part = pair_start(1)
    p_first(1, part)
    p_second(0)
    p_second(1)
    pl.semaphore_wait(near_sem, len(AXIS))
    p_third(0)
    y3, *p_early = y_pieces(0)
    z_pair(0, y3)
    p_third(1)
    z_scatter(0)
    y3, *p_late = y_pieces(1)
    z_pair(1, y3)
    z_scatter(1)
    g_first = gram_of(p_early[0]) + gram_of(p_early[1])
    g_second = gram_of(p_late[0]) + gram_of(p_late[1])
    zero = jnp.zeros((32, 32), F32)
    gram[z] = jnp.concatenate([g_first, zero, g_second, zero], axis=1)
    for offset in AXIS:
        remote(gram.at[z], gram.at[z], gsend_sem.at[0], g_sem.at[z], device(*offset)).start()
    pending.append(all_of(gram, 3, gsend_sem.at[0], g_sem.at[0]).wait_send)
    z_line(0)
    z_line(1)
    sent = list(pending)
    pending.clear()
    z_gather(0)
    z_gather(1)
    for offset in AXIS:
        _, from_z = back_from(*offset)
        remote(gram.at[from_z], gram.at[from_z], gsend_sem.at[0], g_sem.at[from_z], sibling).wait_recv()
    inv_ref[...] = eliminate(gram[0] + gram[1] + gram[2] + gram[3], range(32), True)
    inverse = [factor(inv_ref, l) for l in range(2)]

    def q_half(l, h):
        for k in range(Z_CHUNKS):
            cols = pl.ds(pl.multiple_of(h * Z_HALF + STARTS[k], 128), WIDTHS[k])
            q_done[l, :, cols] = sum3(dot(inverse[l], split3(from_pieces(zag[l][k].at[h])), NN))

    for l in range(2):
        for h in range(2):
            for k in range(P_CHUNKS):
                start = h * P_HALF + P_STARTS[k]
                p_done[l, :, start : start + P_WIDTHS[k]] = sum3(dot(inverse[l], split3(pf[l][k][h]), NN)) * root
    for done in sent:
        done()
    z_forward(0)
    q_half(0, mine)
    z_finish(0)
    q_half(0, other)
    z_forward(1)
    q_half(1, mine)
    z_finish(1)
    drain()


def finish_kernel(q_done, p_done, *refs):
    late, (inv_ref, p_out, q_out, last, sem) = refs[:Z_CHUNKS], refs[Z_CHUNKS:]
    mine = lax.rem(lax.axis_index("dp"), 2)
    other = 1 - mine
    own = pl.ds(pl.multiple_of(mine * Z_HALF, 128), Z_HALF)
    rest = pl.ds(pl.multiple_of(other * Z_HALF, 128), Z_HALF)
    copies = [
        pltpu.make_async_copy(q_done.at[0], q_out.at[0], sem.at[0]),
        pltpu.make_async_copy(q_done.at[1, :, own], q_out.at[1, :, own], sem.at[1]),
        pltpu.make_async_copy(p_done, p_out, sem.at[2]),
    ]
    for cp in copies:
        cp.start()
    inverse = factor(inv_ref, 1)
    for k in range(Z_CHUNKS):
        block = from_pieces(late[k].at[other])
        last[:, STARTS[k] : STARTS[k] + WIDTHS[k]] = sum3(dot(inverse, split3(block), NN))
    copies.append(pltpu.make_async_copy(last, q_out.at[1, :, rest], sem.at[3]))
    copies[3].start()
    for cp in copies:
        cp.wait()


def local(acts, cotangent, q_start):
    width = cotangent.shape[2]
    q_t = jnp.swapaxes(q_start, 1, 2)
    hbm = pl.BlockSpec(memory_space=pltpu.HBM)
    vmem = pl.BlockSpec(memory_space=pltpu.VMEM)
    dma = pltpu.SemaphoreType.DMA
    count = Z_CHUNKS + 3

    def chunks(shape_of, widths, times=1):
        return [pltpu.VMEM(shape_of(width), F32) for _ in range(2 * times) for width in widths]

    finished = pl.pallas_call(
        functools.partial(exchange_kernel, root=float(width) ** 0.5),
        out_shape=(
            jax.ShapeDtypeStruct((2, 32, 2 * Z_HALF), F32),
            jax.ShapeDtypeStruct((2, 32, 2 * P_HALF), F32),
            *[jax.ShapeDtypeStruct((2, 16, 8, w // 4), F32) for w in WIDTHS],
            jax.ShapeDtypeStruct((32, 128), F32),
        ),
        in_specs=[hbm] * 3,
        out_specs=(vmem,) * count,
        scratch_shapes=[
            *[pltpu.VMEM((2, 16, 8, w // 4), F32) for w in WIDTHS],
            *chunks(lambda w: (2, 32, w), P_WIDTHS),
            pltpu.VMEM((2, 512, 1280), BF16),
            pltpu.VMEM((2, 512, 5120), BF16),
            pltpu.VMEM((2, 32, 5120), F32),
            pltpu.VMEM((2, 5120, 96), BF16),
            pltpu.VMEM((32, 512), F32),
            pltpu.VMEM((2, 32, P_HALF), F32),
            pltpu.VMEM((2, 32, P_HALF), F32),
            pltpu.VMEM((4, 32, 128), F32),
            *chunks(lambda w: (4, 32, w), P_WIDTHS, 2),
            *chunks(lambda w: (16, 8, w // 4), WIDTHS, 4),
            *chunks(lambda w: (4, 8, w // 4), WIDTHS),
            dma((16,)), dma((2,)), dma((2,)), dma((2, P_CHUNKS, 3)), dma((2, P_CHUNKS)), dma((2, P_CHUNKS)),
            dma((2, P_CHUNKS)), dma((1,)), dma((4,)),
            dma((2, Z_CHUNKS)), dma((2, Z_CHUNKS)), dma((2, Z_CHUNKS, 4)), dma((2, Z_CHUNKS)), dma((2, Z_CHUNKS)),
            dma((2, Z_CHUNKS, 4)), dma((2, Z_CHUNKS)), pltpu.SemaphoreType.REGULAR,
        ],
        name="exchange",
        compiler_params=pltpu.CompilerParams(
            collective_id=0, has_side_effects=True, vmem_limit_bytes=51 * 2**20
        ),
    )(acts, cotangent, q_t)
    p_t, q_new = pl.pallas_call(
        finish_kernel,
        out_shape=(
            jax.ShapeDtypeStruct((2, 32, 2 * P_HALF), F32),
            jax.ShapeDtypeStruct((2, 32, 2 * Z_HALF), F32),
        ),
        in_specs=[vmem] * count,
        out_specs=(hbm, hbm),
        scratch_shapes=[pltpu.VMEM((32, Z_HALF), F32), dma((4,))],
        name="finish",
        compiler_params=pltpu.CompilerParams(vmem_limit_bytes=32 * 2**20),
    )(*finished)
    return jnp.swapaxes(p_t, 1, 2), jnp.swapaxes(q_new, 1, 2)


def solution(mesh):
    placed = (P(None, "dp", "tensor"), P(None, "dp", None), P())
    return jax.shard_map(
        local, mesh=mesh, in_specs=placed, out_specs=(P(None, "tensor", None), P()), check_vma=False
    )
```

```python
import functools

import jax
import jax.numpy as jnp
from jax import lax
from jax.experimental import pallas as pl
from jax.experimental.pallas import tpu as pltpu
from jax.sharding import PartitionSpec as P

MESH = pl.DeviceIdType.MESH
F32 = jnp.float32
BF16 = jnp.bfloat16
NN = (((1,), (0,)), ((), ()))
NT = (((1,), (1,)), ((), ()))
TILE = 256
FLY = 5
WIDTHS = (1024, 1024, 512)
P_WIDTHS = (384, 256)
STARTS = tuple(sum(WIDTHS[:k]) for k in range(len(WIDTHS)))
P_STARTS = tuple(sum(P_WIDTHS[:k]) for k in range(len(P_WIDTHS)))
Z_CHUNKS, P_CHUNKS = len(WIDTHS), len(P_WIDTHS)
TURN = 1
Z_HALF, P_HALF = sum(WIDTHS), sum(P_WIDTHS)


def hops(offset):
    return sum(min(d, 4 - d) for d in offset)


OFFSETS = [(dz, dy, dx) for dz in range(4) for dy in range(4) for dx in range(4)]
CUBE = sorted([o for o in OFFSETS if hops(o) > 0], key=hops, reverse=True)
PLANE = [o for o in CUBE if o[0] == 0]
AXIS = [o for o in CUBE if o[1] == 0 and o[2] == 0]


def dot(a, b, dims):
    return lax.dot_general(a, b, dims, preferred_element_type=F32)


def split3(x):
    hi = x.astype(BF16)
    rest = x - hi.astype(F32)
    mid = rest.astype(BF16)
    low = (rest - mid.astype(F32)).astype(BF16)
    return jnp.concatenate([hi, mid, low], axis=0)


def sum3(x):
    return x[0:32] + x[32:64] + x[64:96]


def to_pieces(ref, value):
    quarter = value.shape[1] // 4
    for j in range(16):
        g, h = j // 4, j % 4
        ref[j] = value[8 * g : 8 * g + 8, quarter * h : quarter * h + quarter]


def from_pieces(ref):
    bands = []
    for g in range(4):
        bands.append(jnp.concatenate([ref[4 * g + h] for h in range(4)], axis=1))
    return jnp.concatenate(bands, axis=0)


def eliminate(work, steps, start=False):
    rows = lax.broadcasted_iota(jnp.int32, (32, 128), 0)
    lanes = lax.broadcasted_iota(jnp.int32, (32, 128), 1)
    if start:
        eye = jnp.where(rows == lanes % 32, 1.0, 0.0).astype(F32)
        work = jnp.where((lanes // 32) % 2 == 1, eye, work)
    first = lanes < 64
    for k in steps:
        row = work[k : k + 1, :]
        pivot = jnp.where(first[0:1], row[:, k : k + 1], row[:, 64 + k : 65 + k])
        scale = lax.rsqrt(pivot)
        scale = scale * (1.5 - 0.5 * pivot * scale * scale)
        column = jnp.where(first, work[:, k : k + 1], work[:, 64 + k : 65 + k])
        row = row * scale
        work = jnp.where(rows > k, work - (column * scale) * row, jnp.where(rows == k, row, work))
    return work


def factor(inv_ref, l):
    pieces = split3(inv_ref[:, 64 * l + 32 : 64 * l + 64])
    return jnp.concatenate([pieces, pieces, pieces], axis=1)


def exchange_kernel(a_hbm, c_hbm, q_hbm, *refs, root):
    left = list(refs)

    def take(count):
        taken = left[:count]
        del left[:count]
        return taken

    q_done, p_done = take(2)
    late = take(Z_CHUNKS)
    (inv_ref,) = take(1)
    zag, pf = [take(Z_CHUNKS), late], [take(P_CHUNKS) for _ in range(2)]
    a, c, q, q3t, wt, px, pxr, gram = take(8)
    pa, pb = ([take(P_CHUNKS) for _ in range(2)] for _ in range(2))
    zx, zxr, zs, zrr, zl = ([take(Z_CHUNKS) for _ in range(2)] for _ in range(5))
    load_sem, px_sem, pxr_sem, psend_sem, pa_sem, pb_sem, pfw_sem, gsend_sem, g_sem = take(9)
    zx_sem, zxr_sem, zsend_sem, zrs_sem, zline_sem, zag_sem, zfw_sem, near_sem = take(8)
    dp = lax.axis_index("dp")
    z = lax.axis_index("tensor")
    core = lax.rem(dp, 2)
    plane = dp // 2
    y, x = plane // 4, lax.rem(plane, 4)
    mine, other = core, 1 - core
    sibling = {"dp": plane * 2 + other, "tensor": z}

    ys = [lax.rem(y + d, 4) for d in range(4)]
    xs = [lax.rem(x + d, 4) for d in range(4)]
    zs_at = [lax.rem(z + d, 4) for d in range(4)]

    def place(dz, dy, dx):
        return ys[dy] * 4 + xs[dx], zs_at[dz]

    def device(dz, dy, dx):
        to_plane, to_z = place(dz, dy, dx)
        return {"dp": to_plane * 2 + core, "tensor": to_z}

    def back_from(dz, dy, dx):
        return place((4 - dz) % 4, (4 - dy) % 4, (4 - dx) % 4)

    first, second = jnp.where(core == 0, x, y), jnp.where(core == 0, y, x)

    def along_first(d):
        row, column = jnp.where(core == 0, y, ys[d]), jnp.where(core == 0, xs[d], x)
        return {"dp": (row * 4 + column) * 2 + core, "tensor": z}

    def along_second(d):
        row, column = jnp.where(core == 0, ys[d], y), jnp.where(core == 0, x, xs[d])
        return {"dp": (row * 4 + column) * 2 + core, "tensor": z}

    def pick(zero, one):
        return jnp.where(core == 0, zero, one)

    def turns(l, k):
        return (l + k) % 3, (l + k + TURN) % 3

    def spun(turn, du, dv, dw):
        dz, dy, dx = ((dw, du, dv), (dv, dw, du), (du, dv, dw))[turn]
        return ys[dy], xs[dx], zs_at[dz]

    def spin(l, k, du, dv, dw):
        to_y, to_x, to_z = (pick(p, q) for p, q in zip(*(spun(t, du, dv, dw) for t in turns(l, k))))
        return {"dp": (to_y * 4 + to_x) * 2 + core, "tensor": to_z}

    def seat(l, k, du, dv):
        seats = []
        for t in turns(l, k):
            to_y, to_x, to_z = spun(t, du, dv, 0)
            u, v = ((to_y, to_x), (to_x, to_z), (to_z, to_y))[t]
            seats.append(u * 4 + v)
        return pick(*seats)

    def line_at(l, k):
        return pick(*((z, y, x)[t] for t in turns(l, k)))

    def remote(src, dst, send, recv, device):
        return pltpu.make_async_remote_copy(
            src_ref=src, dst_ref=dst, send_sem=send, recv_sem=recv, device_id=device, device_id_type=MESH
        )

    pending = []

    def drain():
        while pending:
            pending.pop(0)()

    def all_of(ref, count, send, recv):
        view = ref.at[pl.ds(0, count)]
        return remote(view, view, send, recv, sibling)

    items = []
    for l in range(2):
        items.append((q_hbm.at[l], q.at[l]))
    for l in range(2):
        items.append((a_hbm.at[l], a.at[l]))
        for t in range(512 // TILE):
            items.append((c_hbm.at[l, pl.ds(t * TILE, TILE)], c.at[l, pl.ds(t * TILE, TILE)]))
    loads = [pltpu.make_async_copy(s, d, load_sem.at[i]) for i, (s, d) in enumerate(items)]
    for load in loads[:FLY]:
        load.start()

    barrier = pltpu.get_barrier_semaphore()

    pl.semaphore_signal(barrier, inc=1, device_id=sibling, device_id_type=MESH)
    for offset in PLANE + AXIS:
        pl.semaphore_signal(barrier, inc=1, device_id=device(*offset), device_id_type=MESH)

    def arrive(i):
        loads[i].wait()
        if i + FLY < len(loads):
            loads[i + FLY].start()

    def half_of(h):
        return pl.ds(pl.multiple_of(h * P_HALF, 128), P_HALF)

    def tokens(l, t):
        base = 2 + l * (1 + 512 // TILE)
        if t == 0:
            arrive(base)
        arrive(base + 1 + t)
        w = dot(c[l, t * TILE : (t + 1) * TILE, :], q3t[l], NN)
        wt[:, t * TILE : (t + 1) * TILE] = sum3(w.T) * (1.0 / 32.0)

    def p_part(l, h):
        return sum3(dot(split3(wt[...]), a[l, :, half_of(h)], NN))

    def pair_start(l):
        px[l] = p_part(l, other)
        cp = remote(px.at[l], pxr.at[l], px_sem.at[l], pxr_sem.at[l], sibling)
        cp.start()
        pending.append(cp.wait_send)
        return p_part(l, mine)

    def p_first(l, part):
        remote(px.at[l], pxr.at[l], px_sem.at[l], pxr_sem.at[l], sibling).wait_recv()
        for k in range(P_CHUNKS):
            cols = slice(P_STARTS[k], P_STARTS[k] + P_WIDTHS[k])
            pa[l][k][first] = part[:, cols] + pxr[l, :, cols]
            slot = pa[l][k].at[first]
            for d, _, _ in AXIS:
                remote(slot, slot, psend_sem.at[l, k, 0], pa_sem.at[l, k], along_first(d)).start()
            pending.append(all_of(pa[l][k], 3, psend_sem.at[l, k, 0], pa_sem.at[l, k]).wait_send)

    def p_second(l):
        for k in range(P_CHUNKS):
            src, dst = pa[l][k], pb[l][k]
            all_of(src, 3, psend_sem.at[l, k, 0], pa_sem.at[l, k]).wait_recv()
            dst[second] = src[0] + src[1] + src[2] + src[3]
            slot = dst.at[second]
            for d, _, _ in AXIS:
                remote(slot, slot, psend_sem.at[l, k, 1], pb_sem.at[l, k], along_second(d)).start()
            pending.append(all_of(dst, 3, psend_sem.at[l, k, 1], pb_sem.at[l, k]).wait_send)

    def p_third(l):
        for k in range(P_CHUNKS):
            src = pb[l][k]
            all_of(src, 3, psend_sem.at[l, k, 1], pb_sem.at[l, k]).wait_recv()
            pf[l][k][mine] = src[0] + src[1] + src[2] + src[3]
            slot = pf[l][k].at[mine]
            cp = remote(slot, slot, psend_sem.at[l, k, 2], pfw_sem.at[l, k], sibling)
            cp.start()
            pending.append(cp.wait_send)

    def half_pieces(l, h):
        return split3(jnp.concatenate([pf[l][k][h] for k in range(P_CHUNKS)], axis=1))

    def gram_of(p3):
        g3 = sum3(dot(p3, p3, NT))
        return g3[:, 0:32] + g3[:, 32:64] + g3[:, 64:96]

    def y_pieces(l):
        p_mine = half_pieces(l, mine)
        y = sum3(dot(p_mine, a[l, :, half_of(mine)], NT))
        for k in range(P_CHUNKS):
            slot = pf[l][k].at[other]
            remote(slot, slot, psend_sem.at[l, k, 2], pfw_sem.at[l, k], sibling).wait_recv()
        p_other = half_pieces(l, other)
        y = y + sum3(dot(p_other, a[l, :, half_of(other)], NT))
        return split3(y * (1.0 / 32.0)), p_mine, p_other

    def z_part(l, k, h, y3):
        cols = pl.ds(pl.multiple_of(h * Z_HALF + STARTS[k], 128), WIDTHS[k])
        return sum3(dot(y3, c[l, :, cols], NN))

    def z_pair(l, y3):
        for k in range(Z_CHUNKS):
            to_pieces(zx[l][k], z_part(l, k, other, y3))
            cp = remote(zx[l][k], zxr[l][k], zx_sem.at[l, k], zxr_sem.at[l, k], sibling)
            cp.start()
            pending.append(cp.wait_send)
        for k in range(Z_CHUNKS):
            to_pieces(zs[l][k], z_part(l, k, mine, y3))

    def z_scatter(l):
        for k in range(Z_CHUNKS):
            remote(zx[l][k], zxr[l][k], zx_sem.at[l, k], zxr_sem.at[l, k], sibling).wait_recv()
            zs[l][k][...] += zxr[l][k][...]
            me = seat(l, k, 0, 0)
            for _, du, dv in PLANE:
                remote(
                    zs[l][k].at[seat(l, k, du, dv)], zrr[l][k].at[me],
                    zsend_sem.at[l, k, 0], zrs_sem.at[l, k], spin(l, k, du, dv, 0),
                ).start()
            pending.append(all_of(zs[l][k], 15, zsend_sem.at[l, k, 0], zrs_sem.at[l, k]).wait_send)
            zrr[l][k][me] = zs[l][k][me]

    def z_line(l):
        for k in range(Z_CHUNKS):
            all_of(zrr[l][k], 15, zsend_sem.at[l, k, 0], zrs_sem.at[l, k]).wait_recv()
            w = line_at(l, k)
            zl[l][k][w] = jnp.sum(zrr[l][k][...], axis=0)
            slot = zl[l][k].at[w]
            for dw, _, _ in AXIS:
                remote(
                    slot, slot, zsend_sem.at[l, k, 1], zline_sem.at[l, k], spin(l, k, 0, 0, dw)
                ).start()
            pending.append(all_of(zl[l][k], 3, zsend_sem.at[l, k, 1], zline_sem.at[l, k]).wait_send)

    def z_gather(l):
        for k in range(Z_CHUNKS):
            src = zl[l][k]
            all_of(src, 3, zsend_sem.at[l, k, 1], zline_sem.at[l, k]).wait_recv()
            me = seat(l, k, 0, 0)
            zag[l][k][mine, me] = src[0] + src[1] + src[2] + src[3]
            own = zag[l][k].at[mine, me]
            for _, du, dv in PLANE:
                remote(
                    own, own, zsend_sem.at[l, k, 2], zag_sem.at[l, k, me // 4], spin(l, k, du, dv, 0)
                ).start()
            pending.append(all_of(zag[l][k].at[mine], 15, zsend_sem.at[l, k, 2], zag_sem.at[l, k, 0]).wait_send)

    def z_forward(l):
        for k in range(Z_CHUNKS):
            whole = zag[l][k].at[mine]
            for d in (0, 1, 3, 2):
                u = lax.rem(seat(l, k, 0, 0) // 4 + d, 4)
                block = zag[l][k].at[mine, pl.ds(u * 4, 3 if d == 0 else 4)]
                remote(block, block, zsend_sem.at[l, k, 3], zag_sem.at[l, k, u], sibling).wait_recv()
                block = zag[l][k].at[mine, pl.ds(u * 4, 4)]
                remote(block, block, zsend_sem.at[l, k, 3], zfw_sem.at[l, k], sibling).start()
            pending.append(remote(whole, whole, zsend_sem.at[l, k, 3], zfw_sem.at[l, k], sibling).wait_send)

    def z_finish(l):
        for k in range(Z_CHUNKS):
            whole = zag[l][k].at[other]
            remote(whole, whole, zsend_sem.at[l, k, 3], zfw_sem.at[l, k], sibling).wait_recv()

    for l in range(2):
        arrive(l)
        q3t[l] = split3(q[l]).T
    for t in range(512 // TILE):
        tokens(0, t)
    pl.semaphore_wait(barrier, 1 + len(PLANE) + len(AXIS))
    for offset in AXIS:
        pl.semaphore_signal(near_sem, inc=1, device_id=device(*offset), device_id_type=MESH)
    part = pair_start(0)
    tokens(1, 0)
    p_first(0, part)
    for t in range(1, 512 // TILE):
        tokens(1, t)
    part = pair_start(1)
    p_first(1, part)
    p_second(0)
    p_second(1)
    pl.semaphore_wait(near_sem, len(AXIS))
    p_third(0)
    y3, *p_early = y_pieces(0)
    z_pair(0, y3)
    p_third(1)
    z_scatter(0)
    y3, *p_late = y_pieces(1)
    z_pair(1, y3)
    z_scatter(1)
    g_first = gram_of(p_early[0]) + gram_of(p_early[1])
    g_second = gram_of(p_late[0]) + gram_of(p_late[1])
    zero = jnp.zeros((32, 32), F32)
    gram[z] = jnp.concatenate([g_first, zero, g_second, zero], axis=1)
    for offset in AXIS:
        remote(gram.at[z], gram.at[z], gsend_sem.at[0], g_sem.at[z], device(*offset)).start()
    pending.append(all_of(gram, 3, gsend_sem.at[0], g_sem.at[0]).wait_send)
    z_line(0)
    for offset in AXIS:
        _, from_z = back_from(*offset)
        remote(gram.at[from_z], gram.at[from_z], gsend_sem.at[0], g_sem.at[from_z], sibling).wait_recv()
    work = eliminate(gram[0] + gram[1] + gram[2] + gram[3], range(0), True)
    z_line(1)
    sent = list(pending)
    pending.clear()
    z_gather(0)
    work = eliminate(work, range(0, 14))
    z_gather(1)
    inv_ref[...] = eliminate(work, range(14, 32))
    inverse = [factor(inv_ref, l) for l in range(2)]

    def q_half(l, h):
        for k in range(Z_CHUNKS):
            cols = pl.ds(pl.multiple_of(h * Z_HALF + STARTS[k], 128), WIDTHS[k])
            q_done[l, :, cols] = sum3(dot(inverse[l], split3(from_pieces(zag[l][k].at[h])), NN))

    for l in range(2):
        for h in range(2):
            for k in range(P_CHUNKS):
                start = h * P_HALF + P_STARTS[k]
                p_done[l, :, start : start + P_WIDTHS[k]] = sum3(dot(inverse[l], split3(pf[l][k][h]), NN)) * root
    for done in sent:
        done()
    z_forward(0)
    q_half(0, mine)
    z_finish(0)
    q_half(0, other)
    z_forward(1)
    q_half(1, mine)
    z_finish(1)
    drain()


def finish_kernel(q_done, p_done, *refs):
    late, (inv_ref, p_out, q_out, last, sem) = refs[:Z_CHUNKS], refs[Z_CHUNKS:]
    mine = lax.rem(lax.axis_index("dp"), 2)
    other = 1 - mine
    own = pl.ds(pl.multiple_of(mine * Z_HALF, 128), Z_HALF)
    rest = pl.ds(pl.multiple_of(other * Z_HALF, 128), Z_HALF)
    copies = [
        pltpu.make_async_copy(q_done.at[0], q_out.at[0], sem.at[0]),
        pltpu.make_async_copy(q_done.at[1, :, own], q_out.at[1, :, own], sem.at[1]),
        pltpu.make_async_copy(p_done, p_out, sem.at[2]),
    ]
    for cp in copies:
        cp.start()
    inverse = factor(inv_ref, 1)
    for k in range(Z_CHUNKS):
        block = from_pieces(late[k].at[other])
        last[:, STARTS[k] : STARTS[k] + WIDTHS[k]] = sum3(dot(inverse, split3(block), NN))
    copies.append(pltpu.make_async_copy(last, q_out.at[1, :, rest], sem.at[3]))
    copies[3].start()
    for cp in copies:
        cp.wait()


def local(acts, cotangent, q_start):
    width = cotangent.shape[2]
    q_t = jnp.swapaxes(q_start, 1, 2)
    hbm = pl.BlockSpec(memory_space=pltpu.HBM)
    vmem = pl.BlockSpec(memory_space=pltpu.VMEM)
    dma = pltpu.SemaphoreType.DMA
    count = Z_CHUNKS + 3

    def chunks(shape_of, widths, times=1):
        return [pltpu.VMEM(shape_of(width), F32) for _ in range(2 * times) for width in widths]

    finished = pl.pallas_call(
        functools.partial(exchange_kernel, root=float(width) ** 0.5),
        out_shape=(
            jax.ShapeDtypeStruct((2, 32, 2 * Z_HALF), F32),
            jax.ShapeDtypeStruct((2, 32, 2 * P_HALF), F32),
            *[jax.ShapeDtypeStruct((2, 16, 8, w // 4), F32) for w in WIDTHS],
            jax.ShapeDtypeStruct((32, 128), F32),
        ),
        in_specs=[hbm] * 3,
        out_specs=(vmem,) * count,
        scratch_shapes=[
            *[pltpu.VMEM((2, 16, 8, w // 4), F32) for w in WIDTHS],
            *chunks(lambda w: (2, 32, w), P_WIDTHS),
            pltpu.VMEM((2, 512, 1280), BF16),
            pltpu.VMEM((2, 512, 5120), BF16),
            pltpu.VMEM((2, 32, 5120), F32),
            pltpu.VMEM((2, 5120, 96), BF16),
            pltpu.VMEM((32, 512), F32),
            pltpu.VMEM((2, 32, P_HALF), F32),
            pltpu.VMEM((2, 32, P_HALF), F32),
            pltpu.VMEM((4, 32, 128), F32),
            *chunks(lambda w: (4, 32, w), P_WIDTHS, 2),
            *chunks(lambda w: (16, 8, w // 4), WIDTHS, 4),
            *chunks(lambda w: (4, 8, w // 4), WIDTHS),
            dma((16,)), dma((2,)), dma((2,)), dma((2, P_CHUNKS, 3)), dma((2, P_CHUNKS)), dma((2, P_CHUNKS)),
            dma((2, P_CHUNKS)), dma((1,)), dma((4,)),
            dma((2, Z_CHUNKS)), dma((2, Z_CHUNKS)), dma((2, Z_CHUNKS, 4)), dma((2, Z_CHUNKS)), dma((2, Z_CHUNKS)),
            dma((2, Z_CHUNKS, 4)), dma((2, Z_CHUNKS)), pltpu.SemaphoreType.REGULAR,
        ],
        name="exchange",
        compiler_params=pltpu.CompilerParams(
            collective_id=0, has_side_effects=True, vmem_limit_bytes=51 * 2**20
        ),
    )(acts, cotangent, q_t)
    p_t, q_new = pl.pallas_call(
        finish_kernel,
        out_shape=(
            jax.ShapeDtypeStruct((2, 32, 2 * P_HALF), F32),
            jax.ShapeDtypeStruct((2, 32, 2 * Z_HALF), F32),
        ),
        in_specs=[vmem] * count,
        out_specs=(hbm, hbm),
        scratch_shapes=[pltpu.VMEM((32, Z_HALF), F32), dma((4,))],
        name="finish",
        compiler_params=pltpu.CompilerParams(vmem_limit_bytes=32 * 2**20),
    )(*finished)
    return jnp.swapaxes(p_t, 1, 2), jnp.swapaxes(q_new, 1, 2)


def solution(mesh):
    placed = (P(None, "dp", "tensor"), P(None, "dp", None), P())
    return jax.shard_map(
        local, mesh=mesh, in_specs=placed, out_specs=(P(None, "tensor", None), P()), check_vma=False
    )
```

```python
import functools

import jax
import jax.numpy as jnp
from jax import lax
from jax.experimental import pallas as pl
from jax.experimental.pallas import tpu as pltpu
from jax.sharding import PartitionSpec as P

MESH = pl.DeviceIdType.MESH
F32 = jnp.float32
BF16 = jnp.bfloat16
NN = (((1,), (0,)), ((), ()))
NT = (((1,), (1,)), ((), ()))
TILE = 256
FLY = 5
WIDTHS = (1024, 1024, 512)
P_WIDTHS = (384, 256)
STARTS = tuple(sum(WIDTHS[:k]) for k in range(len(WIDTHS)))
P_STARTS = tuple(sum(P_WIDTHS[:k]) for k in range(len(P_WIDTHS)))
Z_CHUNKS, P_CHUNKS = len(WIDTHS), len(P_WIDTHS)
TURN = 1
Z_HALF, P_HALF = sum(WIDTHS), sum(P_WIDTHS)


def hops(offset):
    return sum(min(d, 4 - d) for d in offset)


OFFSETS = [(dz, dy, dx) for dz in range(4) for dy in range(4) for dx in range(4)]
CUBE = sorted([o for o in OFFSETS if hops(o) > 0], key=hops, reverse=True)
PLANE = [o for o in CUBE if o[0] == 0]
AXIS = [o for o in CUBE if o[1] == 0 and o[2] == 0]


def dot(a, b, dims):
    return lax.dot_general(a, b, dims, preferred_element_type=F32)


def split3(x):
    hi = x.astype(BF16)
    rest = x - hi.astype(F32)
    mid = rest.astype(BF16)
    low = (rest - mid.astype(F32)).astype(BF16)
    return jnp.concatenate([hi, mid, low], axis=0)


def sum2(x):
    return x[0:32] + x[32:64]


def sum3(x):
    return x[0:32] + x[32:64] + x[64:96]


def to_pieces(ref, value):
    quarter = value.shape[1] // 4
    for j in range(16):
        g, h = j // 4, j % 4
        ref[j] = value[8 * g : 8 * g + 8, quarter * h : quarter * h + quarter]


def from_pieces(ref):
    bands = []
    for g in range(4):
        bands.append(jnp.concatenate([ref[4 * g + h] for h in range(4)], axis=1))
    return jnp.concatenate(bands, axis=0)


def eliminate(work, steps, start=False):
    rows = lax.broadcasted_iota(jnp.int32, (32, 128), 0)
    lanes = lax.broadcasted_iota(jnp.int32, (32, 128), 1)
    if start:
        eye = jnp.where(rows == lanes % 32, 1.0, 0.0).astype(F32)
        work = jnp.where((lanes // 32) % 2 == 1, eye, work)
    first = lanes < 64
    for k in steps:
        row = work[k : k + 1, :]
        pivot = jnp.where(first[0:1], row[:, k : k + 1], row[:, 64 + k : 65 + k])
        scale = lax.rsqrt(pivot)
        scale = scale * (1.5 - 0.5 * pivot * scale * scale)
        column = jnp.where(first, work[:, k : k + 1], work[:, 64 + k : 65 + k])
        row = row * scale
        work = jnp.where(rows > k, work - (column * scale) * row, jnp.where(rows == k, row, work))
    return work


def factor(inv_ref, l):
    pieces = split3(inv_ref[:, 64 * l + 32 : 64 * l + 64])
    return jnp.concatenate([pieces, pieces, pieces], axis=1)


def exchange_kernel(a_hbm, c_hbm, q_hbm, *refs, root):
    left = list(refs)

    def take(count):
        taken = left[:count]
        del left[:count]
        return taken

    q_done, p_done = take(2)
    late = take(Z_CHUNKS)
    (inv_ref,) = take(1)
    zag, pf = [take(Z_CHUNKS), late], [take(P_CHUNKS) for _ in range(2)]
    a, c, q, q3t, wt, px, pxr, gram = take(8)
    pa, pb = ([take(P_CHUNKS) for _ in range(2)] for _ in range(2))
    zx, zxr, zs, zrr, zl = ([take(Z_CHUNKS) for _ in range(2)] for _ in range(5))
    load_sem, px_sem, pxr_sem, psend_sem, pa_sem, pb_sem, pfw_sem, gsend_sem, g_sem = take(9)
    zx_sem, zxr_sem, zsend_sem, zrs_sem, zline_sem, zag_sem, zfw_sem, near_sem = take(8)
    dp = lax.axis_index("dp")
    z = lax.axis_index("tensor")
    core = lax.rem(dp, 2)
    plane = dp // 2
    y, x = plane // 4, lax.rem(plane, 4)
    mine, other = core, 1 - core
    sibling = {"dp": plane * 2 + other, "tensor": z}

    ys = [lax.rem(y + d, 4) for d in range(4)]
    xs = [lax.rem(x + d, 4) for d in range(4)]
    zs_at = [lax.rem(z + d, 4) for d in range(4)]

    def place(dz, dy, dx):
        return ys[dy] * 4 + xs[dx], zs_at[dz]

    def device(dz, dy, dx):
        to_plane, to_z = place(dz, dy, dx)
        return {"dp": to_plane * 2 + core, "tensor": to_z}

    def back_from(dz, dy, dx):
        return place((4 - dz) % 4, (4 - dy) % 4, (4 - dx) % 4)

    first, second = jnp.where(core == 0, x, y), jnp.where(core == 0, y, x)

    def along_first(d):
        row, column = jnp.where(core == 0, y, ys[d]), jnp.where(core == 0, xs[d], x)
        return {"dp": (row * 4 + column) * 2 + core, "tensor": z}

    def along_second(d):
        row, column = jnp.where(core == 0, ys[d], y), jnp.where(core == 0, x, xs[d])
        return {"dp": (row * 4 + column) * 2 + core, "tensor": z}

    def pick(zero, one):
        return jnp.where(core == 0, zero, one)

    def turns(l, k):
        return (l + k) % 3, (l + k + TURN) % 3

    def spun(turn, du, dv, dw):
        dz, dy, dx = ((dw, du, dv), (dv, dw, du), (du, dv, dw))[turn]
        return ys[dy], xs[dx], zs_at[dz]

    def spin(l, k, du, dv, dw):
        to_y, to_x, to_z = (pick(p, q) for p, q in zip(*(spun(t, du, dv, dw) for t in turns(l, k))))
        return {"dp": (to_y * 4 + to_x) * 2 + core, "tensor": to_z}

    def seat(l, k, du, dv):
        seats = []
        for t in turns(l, k):
            to_y, to_x, to_z = spun(t, du, dv, 0)
            u, v = ((to_y, to_x), (to_x, to_z), (to_z, to_y))[t]
            seats.append(u * 4 + v)
        return pick(*seats)

    def line_at(l, k):
        return pick(*((z, y, x)[t] for t in turns(l, k)))

    def remote(src, dst, send, recv, device):
        return pltpu.make_async_remote_copy(
            src_ref=src, dst_ref=dst, send_sem=send, recv_sem=recv, device_id=device, device_id_type=MESH
        )

    pending = []

    def drain():
        while pending:
            pending.pop(0)()

    def all_of(ref, count, send, recv):
        view = ref.at[pl.ds(0, count)]
        return remote(view, view, send, recv, sibling)

    items = []
    for l in range(2):
        items.append((q_hbm.at[l], q.at[l]))
    for l in range(2):
        items.append((a_hbm.at[l], a.at[l]))
        for t in range(512 // TILE):
            items.append((c_hbm.at[l, pl.ds(t * TILE, TILE)], c.at[l, pl.ds(t * TILE, TILE)]))
    loads = [pltpu.make_async_copy(s, d, load_sem.at[i]) for i, (s, d) in enumerate(items)]
    for load in loads[:FLY]:
        load.start()

    barrier = pltpu.get_barrier_semaphore()

    pl.semaphore_signal(barrier, inc=1, device_id=sibling, device_id_type=MESH)
    for offset in PLANE + AXIS:
        pl.semaphore_signal(barrier, inc=1, device_id=device(*offset), device_id_type=MESH)

    def arrive(i):
        loads[i].wait()
        if i + FLY < len(loads):
            loads[i + FLY].start()

    def half_of(h):
        return pl.ds(pl.multiple_of(h * P_HALF, 128), P_HALF)

    def tokens(l, t):
        base = 2 + l * (1 + 512 // TILE)
        if t == 0:
            arrive(base)
        arrive(base + 1 + t)
        w = dot(c[l, t * TILE : (t + 1) * TILE, :], q3t[l], NN)
        wt[:, t * TILE : (t + 1) * TILE] = sum3(w.T) * (1.0 / 32.0)

    def p_part(l, h):
        return sum3(dot(split3(wt[...]), a[l, :, half_of(h)], NN))

    def pair_start(l):
        px[l] = p_part(l, other)
        cp = remote(px.at[l], pxr.at[l], px_sem.at[l], pxr_sem.at[l], sibling)
        cp.start()
        pending.append(cp.wait_send)
        return p_part(l, mine)

    def p_first(l, part):
        remote(px.at[l], pxr.at[l], px_sem.at[l], pxr_sem.at[l], sibling).wait_recv()
        for k in range(P_CHUNKS):
            cols = slice(P_STARTS[k], P_STARTS[k] + P_WIDTHS[k])
            pa[l][k][first] = part[:, cols] + pxr[l, :, cols]
            slot = pa[l][k].at[first]
            for d, _, _ in AXIS:
                remote(slot, slot, psend_sem.at[l, k, 0], pa_sem.at[l, k], along_first(d)).start()
            pending.append(all_of(pa[l][k], 3, psend_sem.at[l, k, 0], pa_sem.at[l, k]).wait_send)

    def p_second(l):
        for k in range(P_CHUNKS):
            src, dst = pa[l][k], pb[l][k]
            all_of(src, 3, psend_sem.at[l, k, 0], pa_sem.at[l, k]).wait_recv()
            dst[second] = src[0] + src[1] + src[2] + src[3]
            slot = dst.at[second]
            for d, _, _ in AXIS:
                remote(slot, slot, psend_sem.at[l, k, 1], pb_sem.at[l, k], along_second(d)).start()
            pending.append(all_of(dst, 3, psend_sem.at[l, k, 1], pb_sem.at[l, k]).wait_send)

    def p_third(l):
        for k in range(P_CHUNKS):
            src = pb[l][k]
            all_of(src, 3, psend_sem.at[l, k, 1], pb_sem.at[l, k]).wait_recv()
            pf[l][k][mine] = src[0] + src[1] + src[2] + src[3]
            slot = pf[l][k].at[mine]
            cp = remote(slot, slot, psend_sem.at[l, k, 2], pfw_sem.at[l, k], sibling)
            cp.start()
            pending.append(cp.wait_send)

    def half_pieces(l, h):
        return split3(jnp.concatenate([pf[l][k][h] for k in range(P_CHUNKS)], axis=1))

    def gram_of(p3):
        g3 = sum3(dot(p3, p3, NT))
        return g3[:, 0:32] + g3[:, 32:64] + g3[:, 64:96]

    def y_pieces(l):
        p_mine = half_pieces(l, mine)
        y = sum2(dot(p_mine[0:64], a[l, :, half_of(mine)], NT))
        for k in range(P_CHUNKS):
            slot = pf[l][k].at[other]
            remote(slot, slot, psend_sem.at[l, k, 2], pfw_sem.at[l, k], sibling).wait_recv()
        p_other = half_pieces(l, other)
        y = y + sum2(dot(p_other[0:64], a[l, :, half_of(other)], NT))
        return split3(y * (1.0 / 32.0))[0:64], p_mine, p_other

    def z_part(l, k, h, y3):
        cols = pl.ds(pl.multiple_of(h * Z_HALF + STARTS[k], 128), WIDTHS[k])
        return sum2(dot(y3, c[l, :, cols], NN))

    def z_pair(l, y3):
        for k in range(Z_CHUNKS):
            to_pieces(zx[l][k], z_part(l, k, other, y3))
            cp = remote(zx[l][k], zxr[l][k], zx_sem.at[l, k], zxr_sem.at[l, k], sibling)
            cp.start()
            pending.append(cp.wait_send)
        for k in range(Z_CHUNKS):
            to_pieces(zs[l][k], z_part(l, k, mine, y3))

    def z_scatter(l):
        for k in range(Z_CHUNKS):
            remote(zx[l][k], zxr[l][k], zx_sem.at[l, k], zxr_sem.at[l, k], sibling).wait_recv()
            zs[l][k][...] += zxr[l][k][...]
            me = seat(l, k, 0, 0)
            for _, du, dv in PLANE:
                remote(
                    zs[l][k].at[seat(l, k, du, dv)], zrr[l][k].at[me],
                    zsend_sem.at[l, k, 0], zrs_sem.at[l, k], spin(l, k, du, dv, 0),
                ).start()
            pending.append(all_of(zs[l][k], 15, zsend_sem.at[l, k, 0], zrs_sem.at[l, k]).wait_send)
            zrr[l][k][me] = zs[l][k][me]

    def z_line(l):
        for k in range(Z_CHUNKS):
            all_of(zrr[l][k], 15, zsend_sem.at[l, k, 0], zrs_sem.at[l, k]).wait_recv()
            w = line_at(l, k)
            zl[l][k][w] = jnp.sum(zrr[l][k][...], axis=0)
            slot = zl[l][k].at[w]
            for dw, _, _ in AXIS:
                remote(
                    slot, slot, zsend_sem.at[l, k, 1], zline_sem.at[l, k], spin(l, k, 0, 0, dw)
                ).start()
            pending.append(all_of(zl[l][k], 3, zsend_sem.at[l, k, 1], zline_sem.at[l, k]).wait_send)

    def z_gather(l):
        for k in range(Z_CHUNKS):
            src = zl[l][k]
            all_of(src, 3, zsend_sem.at[l, k, 1], zline_sem.at[l, k]).wait_recv()
            me = seat(l, k, 0, 0)
            zag[l][k][mine, me] = src[0] + src[1] + src[2] + src[3]
            own = zag[l][k].at[mine, me]
            for _, du, dv in PLANE:
                remote(
                    own, own, zsend_sem.at[l, k, 2], zag_sem.at[l, k, me // 4], spin(l, k, du, dv, 0)
                ).start()
            pending.append(all_of(zag[l][k].at[mine], 15, zsend_sem.at[l, k, 2], zag_sem.at[l, k, 0]).wait_send)

    def z_forward(l):
        for k in range(Z_CHUNKS):
            whole = zag[l][k].at[mine]
            for d in (0, 1, 3, 2):
                u = lax.rem(seat(l, k, 0, 0) // 4 + d, 4)
                block = zag[l][k].at[mine, pl.ds(u * 4, 3 if d == 0 else 4)]
                remote(block, block, zsend_sem.at[l, k, 3], zag_sem.at[l, k, u], sibling).wait_recv()
                block = zag[l][k].at[mine, pl.ds(u * 4, 4)]
                remote(block, block, zsend_sem.at[l, k, 3], zfw_sem.at[l, k], sibling).start()
            pending.append(remote(whole, whole, zsend_sem.at[l, k, 3], zfw_sem.at[l, k], sibling).wait_send)

    def z_finish(l):
        for k in range(Z_CHUNKS):
            whole = zag[l][k].at[other]
            remote(whole, whole, zsend_sem.at[l, k, 3], zfw_sem.at[l, k], sibling).wait_recv()

    for l in range(2):
        arrive(l)
        q3t[l] = split3(q[l]).T
    for t in range(512 // TILE):
        tokens(0, t)
    pl.semaphore_wait(barrier, 1 + len(PLANE) + len(AXIS))
    for offset in AXIS:
        pl.semaphore_signal(near_sem, inc=1, device_id=device(*offset), device_id_type=MESH)
    part = pair_start(0)
    tokens(1, 0)
    p_first(0, part)
    for t in range(1, 512 // TILE):
        tokens(1, t)
    part = pair_start(1)
    p_first(1, part)
    p_second(0)
    p_second(1)
    pl.semaphore_wait(near_sem, len(AXIS))
    p_third(0)
    y3, *p_early = y_pieces(0)
    z_pair(0, y3)
    p_third(1)
    z_scatter(0)
    y3, *p_late = y_pieces(1)
    z_pair(1, y3)
    z_scatter(1)
    g_first = gram_of(p_early[0]) + gram_of(p_early[1])
    g_second = gram_of(p_late[0]) + gram_of(p_late[1])
    zero = jnp.zeros((32, 32), F32)
    gram[z] = jnp.concatenate([g_first, zero, g_second, zero], axis=1)
    for offset in AXIS:
        remote(gram.at[z], gram.at[z], gsend_sem.at[0], g_sem.at[z], device(*offset)).start()
    pending.append(all_of(gram, 3, gsend_sem.at[0], g_sem.at[0]).wait_send)
    z_line(0)
    for offset in AXIS:
        _, from_z = back_from(*offset)
        remote(gram.at[from_z], gram.at[from_z], gsend_sem.at[0], g_sem.at[from_z], sibling).wait_recv()
    work = eliminate(gram[0] + gram[1] + gram[2] + gram[3], range(0), True)
    z_line(1)
    sent = list(pending)
    pending.clear()
    z_gather(0)
    work = eliminate(work, range(0, 14))
    z_gather(1)
    inv_ref[...] = eliminate(work, range(14, 32))
    inverse = [factor(inv_ref, l) for l in range(2)]

    def q_half(l, h):
        for k in range(Z_CHUNKS):
            cols = pl.ds(pl.multiple_of(h * Z_HALF + STARTS[k], 128), WIDTHS[k])
            q_done[l, :, cols] = sum3(dot(inverse[l], split3(from_pieces(zag[l][k].at[h])), NN))

    for l in range(2):
        for h in range(2):
            for k in range(P_CHUNKS):
                start = h * P_HALF + P_STARTS[k]
                p_done[l, :, start : start + P_WIDTHS[k]] = sum3(dot(inverse[l], split3(pf[l][k][h]), NN)) * root
    for done in sent:
        done()
    z_forward(0)
    q_half(0, mine)
    z_finish(0)
    q_half(0, other)
    z_forward(1)
    q_half(1, mine)
    z_finish(1)
    drain()


def finish_kernel(q_done, p_done, *refs):
    late, (inv_ref, p_out, q_out, last, sem) = refs[:Z_CHUNKS], refs[Z_CHUNKS:]
    mine = lax.rem(lax.axis_index("dp"), 2)
    other = 1 - mine
    own = pl.ds(pl.multiple_of(mine * Z_HALF, 128), Z_HALF)
    rest = pl.ds(pl.multiple_of(other * Z_HALF, 128), Z_HALF)
    copies = [
        pltpu.make_async_copy(q_done.at[0], q_out.at[0], sem.at[0]),
        pltpu.make_async_copy(q_done.at[1, :, own], q_out.at[1, :, own], sem.at[1]),
        pltpu.make_async_copy(p_done, p_out, sem.at[2]),
    ]
    for cp in copies:
        cp.start()
    inverse = factor(inv_ref, 1)
    for k in range(Z_CHUNKS):
        block = from_pieces(late[k].at[other])
        last[:, STARTS[k] : STARTS[k] + WIDTHS[k]] = sum3(dot(inverse, split3(block), NN))
    copies.append(pltpu.make_async_copy(last, q_out.at[1, :, rest], sem.at[3]))
    copies[3].start()
    for cp in copies:
        cp.wait()


def local(acts, cotangent, q_start):
    width = cotangent.shape[2]
    q_t = jnp.swapaxes(q_start, 1, 2)
    hbm = pl.BlockSpec(memory_space=pltpu.HBM)
    vmem = pl.BlockSpec(memory_space=pltpu.VMEM)
    dma = pltpu.SemaphoreType.DMA
    count = Z_CHUNKS + 3

    def chunks(shape_of, widths, times=1):
        return [pltpu.VMEM(shape_of(width), F32) for _ in range(2 * times) for width in widths]

    finished = pl.pallas_call(
        functools.partial(exchange_kernel, root=float(width) ** 0.5),
        out_shape=(
            jax.ShapeDtypeStruct((2, 32, 2 * Z_HALF), F32),
            jax.ShapeDtypeStruct((2, 32, 2 * P_HALF), F32),
            *[jax.ShapeDtypeStruct((2, 16, 8, w // 4), F32) for w in WIDTHS],
            jax.ShapeDtypeStruct((32, 128), F32),
        ),
        in_specs=[hbm] * 3,
        out_specs=(vmem,) * count,
        scratch_shapes=[
            *[pltpu.VMEM((2, 16, 8, w // 4), F32) for w in WIDTHS],
            *chunks(lambda w: (2, 32, w), P_WIDTHS),
            pltpu.VMEM((2, 512, 1280), BF16),
            pltpu.VMEM((2, 512, 5120), BF16),
            pltpu.VMEM((2, 32, 5120), F32),
            pltpu.VMEM((2, 5120, 96), BF16),
            pltpu.VMEM((32, 512), F32),
            pltpu.VMEM((2, 32, P_HALF), F32),
            pltpu.VMEM((2, 32, P_HALF), F32),
            pltpu.VMEM((4, 32, 128), F32),
            *chunks(lambda w: (4, 32, w), P_WIDTHS, 2),
            *chunks(lambda w: (16, 8, w // 4), WIDTHS, 4),
            *chunks(lambda w: (4, 8, w // 4), WIDTHS),
            dma((16,)), dma((2,)), dma((2,)), dma((2, P_CHUNKS, 3)), dma((2, P_CHUNKS)), dma((2, P_CHUNKS)),
            dma((2, P_CHUNKS)), dma((1,)), dma((4,)),
            dma((2, Z_CHUNKS)), dma((2, Z_CHUNKS)), dma((2, Z_CHUNKS, 4)), dma((2, Z_CHUNKS)), dma((2, Z_CHUNKS)),
            dma((2, Z_CHUNKS, 4)), dma((2, Z_CHUNKS)), pltpu.SemaphoreType.REGULAR,
        ],
        name="exchange",
        compiler_params=pltpu.CompilerParams(
            collective_id=0, has_side_effects=True, vmem_limit_bytes=51 * 2**20
        ),
    )(acts, cotangent, q_t)
    p_t, q_new = pl.pallas_call(
        finish_kernel,
        out_shape=(
            jax.ShapeDtypeStruct((2, 32, 2 * P_HALF), F32),
            jax.ShapeDtypeStruct((2, 32, 2 * Z_HALF), F32),
        ),
        in_specs=[vmem] * count,
        out_specs=(hbm, hbm),
        scratch_shapes=[pltpu.VMEM((32, Z_HALF), F32), dma((4,))],
        name="finish",
        compiler_params=pltpu.CompilerParams(vmem_limit_bytes=32 * 2**20),
    )(*finished)
    return jnp.swapaxes(p_t, 1, 2), jnp.swapaxes(q_new, 1, 2)


def solution(mesh):
    placed = (P(None, "dp", "tensor"), P(None, "dp", None), P())
    return jax.shard_map(
        local, mesh=mesh, in_specs=placed, out_specs=(P(None, "tensor", None), P()), check_vma=False
    )
```

```python
import functools

import jax
import jax.numpy as jnp
from jax import lax
from jax.experimental import pallas as pl
from jax.experimental.pallas import tpu as pltpu
from jax.sharding import PartitionSpec as P

MESH = pl.DeviceIdType.MESH
F32 = jnp.float32
BF16 = jnp.bfloat16
NN = (((1,), (0,)), ((), ()))
NT = (((1,), (1,)), ((), ()))
TILE = 256
FLY = 5
WIDTHS = (1024, 1024, 512)
P_WIDTHS = (384, 256)
STARTS = tuple(sum(WIDTHS[:k]) for k in range(len(WIDTHS)))
P_STARTS = tuple(sum(P_WIDTHS[:k]) for k in range(len(P_WIDTHS)))
Z_CHUNKS, P_CHUNKS = len(WIDTHS), len(P_WIDTHS)
TURN = 1
Z_HALF, P_HALF = sum(WIDTHS), sum(P_WIDTHS)


def hops(offset):
    return sum(min(d, 4 - d) for d in offset)


OFFSETS = [(dz, dy, dx) for dz in range(4) for dy in range(4) for dx in range(4)]
CUBE = sorted([o for o in OFFSETS if hops(o) > 0], key=hops, reverse=True)
PLANE = [o for o in CUBE if o[0] == 0]
AXIS = [o for o in CUBE if o[1] == 0 and o[2] == 0]


def dot(a, b, dims):
    return lax.dot_general(a, b, dims, preferred_element_type=F32)


def split3(x):
    hi = x.astype(BF16)
    rest = x - hi.astype(F32)
    mid = rest.astype(BF16)
    low = (rest - mid.astype(F32)).astype(BF16)
    return jnp.concatenate([hi, mid, low], axis=0)


def sum3(x):
    return x[0:32] + x[32:64] + x[64:96]


def to_pieces(ref, value):
    quarter = value.shape[1] // 4
    for j in range(16):
        g, h = j // 4, j % 4
        ref[j] = value[8 * g : 8 * g + 8, quarter * h : quarter * h + quarter]


def from_pieces(ref):
    bands = []
    for g in range(4):
        bands.append(jnp.concatenate([ref[4 * g + h] for h in range(4)], axis=1))
    return jnp.concatenate(bands, axis=0)


def eliminate(work, steps, start=False):
    rows = lax.broadcasted_iota(jnp.int32, (32, 128), 0)
    lanes = lax.broadcasted_iota(jnp.int32, (32, 128), 1)
    if start:
        eye = jnp.where(rows == lanes % 32, 1.0, 0.0).astype(F32)
        work = jnp.where((lanes // 32) % 2 == 1, eye, work)
    first = lanes < 64
    for k in steps:
        row = work[k : k + 1, :]
        pivot = jnp.where(first[0:1], row[:, k : k + 1], row[:, 64 + k : 65 + k])
        scale = lax.rsqrt(pivot)
        scale = scale * (1.5 - 0.5 * pivot * scale * scale)
        column = jnp.where(first, work[:, k : k + 1], work[:, 64 + k : 65 + k])
        row = row * scale
        work = jnp.where(rows > k, work - (column * scale) * row, jnp.where(rows == k, row, work))
    return work


def factor(inv_ref, l):
    pieces = split3(inv_ref[:, 64 * l + 32 : 64 * l + 64])
    return jnp.concatenate([pieces, pieces, pieces], axis=1)


def exchange_kernel(a_hbm, c_hbm, q_hbm, *refs, root):
    left = list(refs)

    def take(count):
        taken = left[:count]
        del left[:count]
        return taken

    q_done, p_done = take(2)
    late = take(Z_CHUNKS)
    (inv_ref,) = take(1)
    zag, pf = [take(Z_CHUNKS), late], [take(P_CHUNKS) for _ in range(2)]
    a, c, q, q3t, wt, px, pxr, gram = take(8)
    pa, pb = ([take(P_CHUNKS) for _ in range(2)] for _ in range(2))
    zx, zxr, zs, zrr, zl = ([take(Z_CHUNKS) for _ in range(2)] for _ in range(5))
    load_sem, px_sem, pxr_sem, psend_sem, pa_sem, pb_sem, pfw_sem, gsend_sem, g_sem = take(9)
    zx_sem, zxr_sem, zsend_sem, zrs_sem, zline_sem, zag_sem, zfw_sem, near_sem = take(8)
    dp = lax.axis_index("dp")
    z = lax.axis_index("tensor")
    core = lax.rem(dp, 2)
    plane = dp // 2
    y, x = plane // 4, lax.rem(plane, 4)
    mine, other = core, 1 - core
    sibling = {"dp": plane * 2 + other, "tensor": z}

    ys = [lax.rem(y + d, 4) for d in range(4)]
    xs = [lax.rem(x + d, 4) for d in range(4)]
    zs_at = [lax.rem(z + d, 4) for d in range(4)]

    def place(dz, dy, dx):
        return ys[dy] * 4 + xs[dx], zs_at[dz]

    def device(dz, dy, dx):
        to_plane, to_z = place(dz, dy, dx)
        return {"dp": to_plane * 2 + core, "tensor": to_z}

    def back_from(dz, dy, dx):
        return place((4 - dz) % 4, (4 - dy) % 4, (4 - dx) % 4)

    first, second = jnp.where(core == 0, x, y), jnp.where(core == 0, y, x)

    def along_first(d):
        row, column = jnp.where(core == 0, y, ys[d]), jnp.where(core == 0, xs[d], x)
        return {"dp": (row * 4 + column) * 2 + core, "tensor": z}

    def along_second(d):
        row, column = jnp.where(core == 0, ys[d], y), jnp.where(core == 0, x, xs[d])
        return {"dp": (row * 4 + column) * 2 + core, "tensor": z}

    def pick(zero, one):
        return jnp.where(core == 0, zero, one)

    def turns(l, k):
        return (l + k) % 3, (l + k + TURN) % 3

    def spun(turn, du, dv, dw):
        dz, dy, dx = ((dw, du, dv), (dv, dw, du), (du, dv, dw))[turn]
        return ys[dy], xs[dx], zs_at[dz]

    def spin(l, k, du, dv, dw):
        to_y, to_x, to_z = (pick(p, q) for p, q in zip(*(spun(t, du, dv, dw) for t in turns(l, k))))
        return {"dp": (to_y * 4 + to_x) * 2 + core, "tensor": to_z}

    def seat(l, k, du, dv):
        seats = []
        for t in turns(l, k):
            to_y, to_x, to_z = spun(t, du, dv, 0)
            u, v = ((to_y, to_x), (to_x, to_z), (to_z, to_y))[t]
            seats.append(u * 4 + v)
        return pick(*seats)

    def line_at(l, k):
        return pick(*((z, y, x)[t] for t in turns(l, k)))

    def remote(src, dst, send, recv, device):
        return pltpu.make_async_remote_copy(
            src_ref=src, dst_ref=dst, send_sem=send, recv_sem=recv, device_id=device, device_id_type=MESH
        )

    pending = []

    def drain():
        while pending:
            pending.pop(0)()

    def all_of(ref, count, send, recv):
        view = ref.at[pl.ds(0, count)]
        return remote(view, view, send, recv, sibling)

    items = []
    for l in range(2):
        items.append((q_hbm.at[l], q.at[l]))
    for l in range(2):
        items.append((a_hbm.at[l], a.at[l]))
        for t in range(512 // TILE):
            items.append((c_hbm.at[l, pl.ds(t * TILE, TILE)], c.at[l, pl.ds(t * TILE, TILE)]))
    loads = [pltpu.make_async_copy(s, d, load_sem.at[i]) for i, (s, d) in enumerate(items)]
    for load in loads[:FLY]:
        load.start()

    barrier = pltpu.get_barrier_semaphore()

    pl.semaphore_signal(barrier, inc=1, device_id=sibling, device_id_type=MESH)
    for offset in PLANE + AXIS:
        pl.semaphore_signal(barrier, inc=1, device_id=device(*offset), device_id_type=MESH)

    def arrive(i):
        loads[i].wait()
        if i + FLY < len(loads):
            loads[i + FLY].start()

    def half_of(h):
        return pl.ds(pl.multiple_of(h * P_HALF, 128), P_HALF)

    def tokens(l, t):
        base = 2 + l * (1 + 512 // TILE)
        if t == 0:
            arrive(base)
        arrive(base + 1 + t)
        w = dot(c[l, t * TILE : (t + 1) * TILE, :], q3t[l], NN)
        wt[:, t * TILE : (t + 1) * TILE] = sum3(w.T) * (1.0 / 32.0)

    def p_part(l, h):
        return sum3(dot(split3(wt[...]), a[l, :, half_of(h)], NN))

    def pair_start(l):
        px[l] = p_part(l, other)
        cp = remote(px.at[l], pxr.at[l], px_sem.at[l], pxr_sem.at[l], sibling)
        cp.start()
        pending.append(cp.wait_send)
        return p_part(l, mine)

    def p_first(l, part):
        remote(px.at[l], pxr.at[l], px_sem.at[l], pxr_sem.at[l], sibling).wait_recv()
        for k in range(P_CHUNKS):
            cols = slice(P_STARTS[k], P_STARTS[k] + P_WIDTHS[k])
            pa[l][k][first] = part[:, cols] + pxr[l, :, cols]
            slot = pa[l][k].at[first]
            for d, _, _ in AXIS:
                remote(slot, slot, psend_sem.at[l, k, 0], pa_sem.at[l, k], along_first(d)).start()
            pending.append(all_of(pa[l][k], 3, psend_sem.at[l, k, 0], pa_sem.at[l, k]).wait_send)

    def p_second(l):
        for k in range(P_CHUNKS):
            src, dst = pa[l][k], pb[l][k]
            all_of(src, 3, psend_sem.at[l, k, 0], pa_sem.at[l, k]).wait_recv()
            dst[second] = src[0] + src[1] + src[2] + src[3]
            slot = dst.at[second]
            for d, _, _ in AXIS:
                remote(slot, slot, psend_sem.at[l, k, 1], pb_sem.at[l, k], along_second(d)).start()
            pending.append(all_of(dst, 3, psend_sem.at[l, k, 1], pb_sem.at[l, k]).wait_send)

    def p_third(l):
        for k in range(P_CHUNKS):
            src = pb[l][k]
            all_of(src, 3, psend_sem.at[l, k, 1], pb_sem.at[l, k]).wait_recv()
            pf[l][k][mine] = src[0] + src[1] + src[2] + src[3]
            slot = pf[l][k].at[mine]
            cp = remote(slot, slot, psend_sem.at[l, k, 2], pfw_sem.at[l, k], sibling)
            cp.start()
            pending.append(cp.wait_send)

    def half_pieces(l, h):
        return split3(jnp.concatenate([pf[l][k][h] for k in range(P_CHUNKS)], axis=1))

    def gram_of(p3):
        g3 = sum3(dot(p3, p3, NT))
        return g3[:, 0:32] + g3[:, 32:64] + g3[:, 64:96]

    def y_pieces(l):
        p_mine = half_pieces(l, mine)
        y = sum3(dot(p_mine, a[l, :, half_of(mine)], NT))
        for k in range(P_CHUNKS):
            slot = pf[l][k].at[other]
            remote(slot, slot, psend_sem.at[l, k, 2], pfw_sem.at[l, k], sibling).wait_recv()
        p_other = half_pieces(l, other)
        y = y + sum3(dot(p_other, a[l, :, half_of(other)], NT))
        return split3(y * (1.0 / 32.0)), p_mine, p_other

    def z_part(l, k, h, y3):
        cols = pl.ds(pl.multiple_of(h * Z_HALF + STARTS[k], 128), WIDTHS[k])
        return sum3(dot(y3, c[l, :, cols], NN))

    def z_pair(l, y3):
        for k in range(Z_CHUNKS):
            to_pieces(zx[l][k], z_part(l, k, other, y3))
            cp = remote(zx[l][k], zxr[l][k], zx_sem.at[l, k], zxr_sem.at[l, k], sibling)
            cp.start()
            pending.append(cp.wait_send)
        for k in range(Z_CHUNKS):
            to_pieces(zs[l][k], z_part(l, k, mine, y3))

    def z_scatter(l):
        for k in range(Z_CHUNKS):
            remote(zx[l][k], zxr[l][k], zx_sem.at[l, k], zxr_sem.at[l, k], sibling).wait_recv()
            zs[l][k][...] += zxr[l][k][...]
            me = seat(l, k, 0, 0)
            for _, du, dv in PLANE:
                remote(
                    zs[l][k].at[seat(l, k, du, dv)], zrr[l][k].at[me],
                    zsend_sem.at[l, k, 0], zrs_sem.at[l, k], spin(l, k, du, dv, 0),
                ).start()
            pending.append(all_of(zs[l][k], 15, zsend_sem.at[l, k, 0], zrs_sem.at[l, k]).wait_send)
            zrr[l][k][me] = zs[l][k][me]

    def z_line(l):
        for k in range(Z_CHUNKS):
            all_of(zrr[l][k], 15, zsend_sem.at[l, k, 0], zrs_sem.at[l, k]).wait_recv()
            w = line_at(l, k)
            zl[l][k][w] = jnp.sum(zrr[l][k][...], axis=0)
            slot = zl[l][k].at[w]
            for dw, _, _ in AXIS:
                remote(
                    slot, slot, zsend_sem.at[l, k, 1], zline_sem.at[l, k], spin(l, k, 0, 0, dw)
                ).start()
            pending.append(all_of(zl[l][k], 3, zsend_sem.at[l, k, 1], zline_sem.at[l, k]).wait_send)

    def z_gather(l):
        for k in range(Z_CHUNKS):
            src = zl[l][k]
            all_of(src, 3, zsend_sem.at[l, k, 1], zline_sem.at[l, k]).wait_recv()
            me = seat(l, k, 0, 0)
            zag[l][k][mine, me] = src[0] + src[1] + src[2] + src[3]
            own = zag[l][k].at[mine, me]
            for _, du, dv in PLANE:
                remote(
                    own, own, zsend_sem.at[l, k, 2], zag_sem.at[l, k, me // 4], spin(l, k, du, dv, 0)
                ).start()
            pending.append(all_of(zag[l][k].at[mine], 15, zsend_sem.at[l, k, 2], zag_sem.at[l, k, 0]).wait_send)

    def z_forward(l):
        for k in range(Z_CHUNKS):
            whole = zag[l][k].at[mine]
            for d in (0, 1, 3, 2):
                u = lax.rem(seat(l, k, 0, 0) // 4 + d, 4)
                block = zag[l][k].at[mine, pl.ds(u * 4, 3 if d == 0 else 4)]
                remote(block, block, zsend_sem.at[l, k, 3], zag_sem.at[l, k, u], sibling).wait_recv()
                block = zag[l][k].at[mine, pl.ds(u * 4, 4)]
                remote(block, block, zsend_sem.at[l, k, 3], zfw_sem.at[l, k], sibling).start()
            pending.append(remote(whole, whole, zsend_sem.at[l, k, 3], zfw_sem.at[l, k], sibling).wait_send)

    def z_finish(l):
        for k in range(Z_CHUNKS):
            whole = zag[l][k].at[other]
            remote(whole, whole, zsend_sem.at[l, k, 3], zfw_sem.at[l, k], sibling).wait_recv()

    for l in range(2):
        arrive(l)
        q3t[l] = split3(q[l]).T
    for t in range(512 // TILE):
        tokens(0, t)
    pl.semaphore_wait(barrier, 1 + len(PLANE) + len(AXIS))
    for offset in AXIS:
        pl.semaphore_signal(near_sem, inc=1, device_id=device(*offset), device_id_type=MESH)
    part = pair_start(0)
    tokens(1, 0)
    p_first(0, part)
    for t in range(1, 512 // TILE):
        tokens(1, t)
    part = pair_start(1)
    p_first(1, part)
    p_second(0)
    p_second(1)
    pl.semaphore_wait(near_sem, len(AXIS))
    p_third(0)
    y3, *p_early = y_pieces(0)
    z_pair(0, y3)
    p_third(1)
    z_scatter(0)
    y3, *p_late = y_pieces(1)
    z_pair(1, y3)
    z_scatter(1)
    g_first = gram_of(p_early[0]) + gram_of(p_early[1])
    g_second = gram_of(p_late[0]) + gram_of(p_late[1])
    zero = jnp.zeros((32, 32), F32)
    gram[z] = jnp.concatenate([g_first, zero, g_second, zero], axis=1)
    for offset in AXIS:
        remote(gram.at[z], gram.at[z], gsend_sem.at[0], g_sem.at[z], device(*offset)).start()
    pending.append(all_of(gram, 3, gsend_sem.at[0], g_sem.at[0]).wait_send)
    z_line(0)
    for offset in AXIS:
        _, from_z = back_from(*offset)
        remote(gram.at[from_z], gram.at[from_z], gsend_sem.at[0], g_sem.at[from_z], sibling).wait_recv()
    work = eliminate(gram[0] + gram[1] + gram[2] + gram[3], range(0), True)
    z_line(1)
    sent = list(pending)
    pending.clear()
    z_gather(0)
    work = eliminate(work, range(0, 18))
    z_gather(1)
    inv_ref[...] = eliminate(work, range(18, 32))
    inverse = [factor(inv_ref, l) for l in range(2)]

    def q_half(l, h):
        for k in range(Z_CHUNKS):
            cols = pl.ds(pl.multiple_of(h * Z_HALF + STARTS[k], 128), WIDTHS[k])
            q_done[l, :, cols] = sum3(dot(inverse[l], split3(from_pieces(zag[l][k].at[h])), NN))

    for l in range(2):
        for h in range(2):
            for k in range(P_CHUNKS):
                start = h * P_HALF + P_STARTS[k]
                p_done[l, :, start : start + P_WIDTHS[k]] = sum3(dot(inverse[l], split3(pf[l][k][h]), NN)) * root
    for done in sent:
        done()
    z_forward(0)
    q_half(0, mine)
    z_finish(0)
    q_half(0, other)
    z_forward(1)
    q_half(1, mine)
    z_finish(1)
    drain()


def finish_kernel(q_done, p_done, *refs):
    late, (inv_ref, p_out, q_out, last, sem) = refs[:Z_CHUNKS], refs[Z_CHUNKS:]
    mine = lax.rem(lax.axis_index("dp"), 2)
    other = 1 - mine
    own = pl.ds(pl.multiple_of(mine * Z_HALF, 128), Z_HALF)
    rest = pl.ds(pl.multiple_of(other * Z_HALF, 128), Z_HALF)
    copies = [
        pltpu.make_async_copy(q_done.at[0], q_out.at[0], sem.at[0]),
        pltpu.make_async_copy(q_done.at[1, :, own], q_out.at[1, :, own], sem.at[1]),
        pltpu.make_async_copy(p_done, p_out, sem.at[2]),
    ]
    for cp in copies:
        cp.start()
    inverse = factor(inv_ref, 1)
    for k in range(Z_CHUNKS):
        block = from_pieces(late[k].at[other])
        last[:, STARTS[k] : STARTS[k] + WIDTHS[k]] = sum3(dot(inverse, split3(block), NN))
    copies.append(pltpu.make_async_copy(last, q_out.at[1, :, rest], sem.at[3]))
    copies[3].start()
    for cp in copies:
        cp.wait()


def local(acts, cotangent, q_start):
    width = cotangent.shape[2]
    q_t = jnp.swapaxes(q_start, 1, 2)
    hbm = pl.BlockSpec(memory_space=pltpu.HBM)
    vmem = pl.BlockSpec(memory_space=pltpu.VMEM)
    dma = pltpu.SemaphoreType.DMA
    count = Z_CHUNKS + 3

    def chunks(shape_of, widths, times=1):
        return [pltpu.VMEM(shape_of(width), F32) for _ in range(2 * times) for width in widths]

    finished = pl.pallas_call(
        functools.partial(exchange_kernel, root=float(width) ** 0.5),
        out_shape=(
            jax.ShapeDtypeStruct((2, 32, 2 * Z_HALF), F32),
            jax.ShapeDtypeStruct((2, 32, 2 * P_HALF), F32),
            *[jax.ShapeDtypeStruct((2, 16, 8, w // 4), F32) for w in WIDTHS],
            jax.ShapeDtypeStruct((32, 128), F32),
        ),
        in_specs=[hbm] * 3,
        out_specs=(vmem,) * count,
        scratch_shapes=[
            *[pltpu.VMEM((2, 16, 8, w // 4), F32) for w in WIDTHS],
            *chunks(lambda w: (2, 32, w), P_WIDTHS),
            pltpu.VMEM((2, 512, 1280), BF16),
            pltpu.VMEM((2, 512, 5120), BF16),
            pltpu.VMEM((2, 32, 5120), F32),
            pltpu.VMEM((2, 5120, 96), BF16),
            pltpu.VMEM((32, 512), F32),
            pltpu.VMEM((2, 32, P_HALF), F32),
            pltpu.VMEM((2, 32, P_HALF), F32),
            pltpu.VMEM((4, 32, 128), F32),
            *chunks(lambda w: (4, 32, w), P_WIDTHS, 2),
            *chunks(lambda w: (16, 8, w // 4), WIDTHS, 4),
            *chunks(lambda w: (4, 8, w // 4), WIDTHS),
            dma((16,)), dma((2,)), dma((2,)), dma((2, P_CHUNKS, 3)), dma((2, P_CHUNKS)), dma((2, P_CHUNKS)),
            dma((2, P_CHUNKS)), dma((1,)), dma((4,)),
            dma((2, Z_CHUNKS)), dma((2, Z_CHUNKS)), dma((2, Z_CHUNKS, 4)), dma((2, Z_CHUNKS)), dma((2, Z_CHUNKS)),
            dma((2, Z_CHUNKS, 4)), dma((2, Z_CHUNKS)), pltpu.SemaphoreType.REGULAR,
        ],
        name="exchange",
        compiler_params=pltpu.CompilerParams(
            collective_id=0, has_side_effects=True, vmem_limit_bytes=51 * 2**20
        ),
    )(acts, cotangent, q_t)
    p_t, q_new = pl.pallas_call(
        finish_kernel,
        out_shape=(
            jax.ShapeDtypeStruct((2, 32, 2 * P_HALF), F32),
            jax.ShapeDtypeStruct((2, 32, 2 * Z_HALF), F32),
        ),
        in_specs=[vmem] * count,
        out_specs=(hbm, hbm),
        scratch_shapes=[pltpu.VMEM((32, Z_HALF), F32), dma((4,))],
        name="finish",
        compiler_params=pltpu.CompilerParams(vmem_limit_bytes=32 * 2**20),
    )(*finished)
    return jnp.swapaxes(p_t, 1, 2), jnp.swapaxes(q_new, 1, 2)


def solution(mesh):
    placed = (P(None, "dp", "tensor"), P(None, "dp", None), P())
    return jax.shard_map(
        local, mesh=mesh, in_specs=placed, out_specs=(P(None, "tensor", None), P()), check_vma=False
    )
```
